32 devices in a mesh: section: 2 (over x), ctx: 4 (over z), exp: 4 (over y, core).
Axes of the slice: x: 2, y: 2, z: 4, core: 2. Of those that a mesh axis runs over, the one named last changes fastest.
Arguments:
- queries: bfloat16 [2, 256, 2048], P('section', 'ctx', 'exp'), may hold values from -0.8984375 to 0.8984375
- keys_in: bfloat16 [2, 256, 2048], P('section', 'ctx', 'exp'), may hold values from -0.8984375 to 0.8984375
- values: bfloat16 [2, 256, 2048], P('section', 'ctx', 'exp'), may hold values from -6 to 6
- decay_rate: float32 [2, 16, 256], P('section', 'exp', 'ctx'), may hold values from 0 to 1
- out_weight: bfloat16 [2, 2048, 6144], P('section', 'exp'), may hold values from -0.125 to 0.125
- residual: bfloat16 [2, 256, 6144], P('section', ('ctx', 'exp')), may hold values from -6 to 6
- norm_gain: float32 [2, 6144], P('section'), may hold values from 0.5 to 1.5
- router: bfloat16 [2, 6144, 16], P('section'), may hold values from -0.078125 to 0.078125
- expert_ids: int32 [2, 256, 2], P('section', ('ctx', 'exp')), may hold values from 0 to 15, all different within a row; in each aligned block of 16 rows (0 to 15, 16 to 31, ..., all dimensions but the last counted through in order) at most 4 rows name the same one
Outputs:
- expert_rows: bfloat16 [2, 4, 16, 4, 4, 6144], P('section', 'ctx', 'exp')
- expert_gates: bfloat16 [2, 4, 16, 4, 4], P('section', 'ctx', 'exp')
The draws below stay inside these ranges and needn't reach their ends.
Inputs may be any that keep to these rules, and one draw needn't show every extreme that they name: `expert_ids`: in each device's 16 rows, every row names two different experts, no expert is named more than 4 times, and in some devices' rows an expert is named exactly 4 times.
All inputs are finite; a program needn't handle non-finite values.
Results may differ from the reference program's by a relative error of at most 0.02.
Values may be sent and summed in bfloat16 or wider, within the bound.
No kernel may reach another device: no remote copies, remote signals or barrier semaphores. Data moves between devices by JAX's collectives and lax.ppermute only.
A program may use at most 64 MiB of HBM per device.

```python
import math
import jax
import jax.numpy as jnp
import numpy as np
from jax import lax

D = 6144
HEAD_DIM = 128
HEAD_DEV = 4
EXPERTS = 16
TOK_SHARE = 16
L_DEV = 64
SEQUENCE_LENGTH = 256
HEADS = 16
CAP = 4
N_SECTION = 2
N_CTX = 4
N_EXP = 4


def draw_decay_rate(key, part):
    key_rows = jax.random.split(key, 6)
    slow_share = 0.5
    head_shape = (N_SECTION, HEADS, 1)
    complete_shape = (N_SECTION, HEADS, SEQUENCE_LENGTH)
    slow = jax.random.uniform(key_rows[0], head_shape) < slow_share
    fast_rate = jnp.exp(jax.random.uniform(key_rows[1], head_shape, minval=jnp.log(1.0 / 50.0), maxval=jnp.log(1.0 / 30.0)))
    slow_rate = jnp.exp(jax.random.uniform(key_rows[2], head_shape, minval=jnp.log(0.1 / SEQUENCE_LENGTH), maxval=jnp.log(0.8 / SEQUENCE_LENGTH)))
    baseline_decay = jnp.where(slow, slow_rate, fast_rate)
    coarse_estimate = jax.random.uniform(key_rows[3], complete_shape, minval=0.5, maxval=1.5)
    spike_position = jax.random.uniform(key_rows[4], complete_shape) < 2.0 / SEQUENCE_LENGTH
    spike_penalty = jax.random.uniform(key_rows[5], complete_shape, minval=0.2, maxval=0.45)
    return (baseline_decay * coarse_estimate + jnp.where(spike_position, -jnp.log(1.0 - spike_penalty), 0.0)).astype(jnp.float32)


def block_levels(stream_key, extent, cuts, low, high):
    gain = 1.0
    for position, shards_of in cuts:
        steps = jax.random.uniform(jax.random.fold_in(jax.random.fold_in(stream_key, 6), position), (shards_of,), jnp.float32, low / len(cuts), high / len(cuts))
        gain = gain * jnp.repeat(jnp.exp(steps), extent[position] // shards_of).reshape((-1,) + (1,) * (len(extent) - 1 - position))
    return gain


def shared_out(own_key, own, number, rows, count, top, bound, slope):
    sequence = jax.random.permutation(own_key, count)
    packed, ordinary = shares(count, rows * top, bound, slope, True), shares(count, rows * top, bound, slope, False)
    places = jnp.arange(count)

    def named(tallies, turn):
        used = int((tallies > 0).sum())
        fixed = max(1, used // 4)
        shifted = fixed + (places - fixed + turn * (used - fixed)) % max(1, count - fixed)
        return jnp.zeros((count,), jnp.int32).at[sequence[jnp.where(places < fixed, places, shifted)]].set(jnp.asarray(tallies, jnp.int32))

    tallies = jnp.where(number % 4 == 0, named(packed, number // 4), named(ordinary, number - number // 4 - 1))
    mixed = jax.random.permutation(jax.random.fold_in(own, 3), count)
    giver, taker = mixed[0:count // 2 * 2:2], mixed[1:count // 2 * 2:2]
    room = jnp.minimum(tallies[giver] - 1, bound - tallies[taker]) // 2
    room = jnp.where((giver == sequence[0]) | (taker == sequence[0]) | (tallies[taker] == 0), 0, jnp.maximum(room, 0))
    shifted = jax.random.randint(jax.random.fold_in(own, 4), (count // 2,), 0, 1 << 20) % (room + 1)
    tallies = tallies.at[giver].add(-shifted).at[taker].add(shifted)
    items = jnp.searchsorted(jnp.cumsum(tallies), jnp.arange(rows * top), side="right").astype(jnp.int32)
    listing = items.reshape(top, rows).T
    listing = listing[jax.random.permutation(jax.random.fold_in(own, 1), rows)]
    turn = jax.random.randint(jax.random.fold_in(own, 2), (rows, 1), 0, top)
    return jnp.take_along_axis(listing, (jnp.arange(top)[None, :] + turn) % top, axis=1)


def shares(count, total, reach, skew, full):
    loads = [(1 << 20) // math.isqrt(standing ** skew) + 1 for standing in range(1, count + 1)]
    largest = reach if full else min(reach, max(-(-total // count), total * loads[0] // sum(loads)))
    least = 1 if total - largest >= count - 1 else 0
    counts, surplus = [largest] + [least] * (count - 1), total - largest - least * (count - 1)
    while surplus > 0:
        free = [i for i in range(1, count) if counts[i] < largest] or [i for i in range(1, count) if counts[i] < reach]
        mass, left = sum([loads[i] for i in free]), surplus
        for i in free:
            extra = min(reach - counts[i], max(1, left * loads[i] // mass), surplus)
            counts[i] = counts[i] + extra
            surplus = surplus - extra
    return np.array(counts)


def scatter_about(stream_key, dims, deviation, most, cuts=(), kind=jnp.bfloat16):
    values = deviation * jax.random.normal(stream_key, dims, jnp.float32)
    if cuts:
        values = values * block_levels(stream_key, dims, cuts, -0.22, 0.18)
    return jnp.clip(values, -most, most).astype(kind)


def setup_inputs(seed: int = 0) -> dict:
    key_list = jax.random.split(jax.random.key(seed), 10)
    queries = scatter_about(key_list[0], (N_SECTION, SEQUENCE_LENGTH, HEADS * HEAD_DIM), 0.15, 0.8984375, ((0, 2), (1, 4), (2, 4)))
    keys_in = scatter_about(key_list[1], (N_SECTION, SEQUENCE_LENGTH, HEADS * HEAD_DIM), 0.15, 0.8984375, ((0, 2), (1, 4), (2, 4)))
    values = scatter_about(key_list[2], (N_SECTION, SEQUENCE_LENGTH, HEADS * HEAD_DIM), 1.0, 6.0, ((0, 2), (1, 4), (2, 4)))
    decay_rate = draw_decay_rate(jax.random.fold_in(key_list[9], 71), 0)
    out_weight = scatter_about(key_list[4], (N_SECTION, HEADS * HEAD_DIM, D), (HEADS * HEAD_DIM) ** -0.5, 0.125, ((0, 2), (1, 4)))
    residual = scatter_about(key_list[5], (N_SECTION, SEQUENCE_LENGTH, D), 1.0, 6.0, ((0, 2), (1, 16)))
    norm_gain = jnp.clip(1.0 + 0.1 * jax.random.normal(key_list[6], (N_SECTION, D), jnp.float32), 0.5, 1.5)
    router = scatter_about(key_list[7], (N_SECTION, D, EXPERTS), D ** -0.5, 0.078125, ((0, 2),))
    expert_ids_keys = jax.random.split(jax.random.fold_in(key_list[8], 1), N_SECTION * SEQUENCE_LENGTH // TOK_SHARE)
    expert_ids_turns = jax.random.permutation(jax.random.fold_in(key_list[8], 3), N_SECTION * SEQUENCE_LENGTH // TOK_SHARE)
    expert_ids = jax.vmap(lambda own, number: shared_out(jax.random.fold_in(key_list[8], 2), own, number, TOK_SHARE, EXPERTS, 2, CAP, 2))(expert_ids_keys, expert_ids_turns).reshape((N_SECTION, SEQUENCE_LENGTH, 2))
    return {"queries": queries, "keys_in": keys_in, "values": values, "decay_rate": decay_rate, "out_weight": out_weight, "residual": residual, "norm_gain": norm_gain, "router": router, "expert_ids": expert_ids}


precise = lax.Precision.HIGHEST
epsilon = 1e-05

def block_attention(queries, keys_in, values, decay_rate):
    shaped_q = queries.reshape(N_CTX, L_DEV, HEADS, HEAD_DIM).astype(jnp.float32)
    shaped_k = keys_in.reshape(N_CTX, L_DEV, HEADS, HEAD_DIM).astype(jnp.float32)
    shaped_v = values.reshape(N_CTX, L_DEV, HEADS, HEAD_DIM).astype(jnp.float32)
    cum_log = jnp.cumsum(-decay_rate.reshape(HEADS, N_CTX, L_DEV), axis=-1)
    attention_logits = jnp.einsum('nlhd,nmhd->hnlm', shaped_q, shaped_k)
    log_gap = cum_log[:, :, :, None] - cum_log[:, :, None, :]
    causal = jnp.arange(L_DEV, dtype=jnp.int32)[:, None] >= jnp.arange(L_DEV, dtype=jnp.int32)[None, :]
    weight_matrix = jnp.where(causal, attention_logits * jnp.exp(jnp.minimum(log_gap, 0.0)), 0.0).astype(jnp.bfloat16)
    inner_part = jnp.einsum('hnlm,nmhd->nlhd', weight_matrix.astype(jnp.float32), shaped_v)
    tail_decay = jnp.exp(cum_log[:, :, -1:] - cum_log)
    keyed_rows = shaped_k * jnp.transpose(tail_decay, (1, 2, 0))[:, :, :, None]
    local_state = jnp.einsum('nlha,nlhb->nhab', keyed_rows, shaped_v, precision=precise)
    total_log = jnp.transpose(cum_log[:, :, -1])

    def advance(carried, piece):
        block_log, block_state = piece
        return (jnp.exp(block_log)[:, None, None] * carried + block_state, carried)
    start_state = jnp.zeros((HEADS, HEAD_DIM, HEAD_DIM), jnp.float32)
    unused, incoming = lax.scan(advance, start_state, (total_log, local_state))
    outside = jnp.exp(jnp.transpose(cum_log, (1, 2, 0)))[:, :, :, None] * jnp.einsum('nlhd,nhde->nlhe', shaped_q, incoming, precision=precise)
    return (inner_part + outside).astype(jnp.bfloat16).reshape(SEQUENCE_LENGTH, HEADS * HEAD_DIM)

def project_heads(attended, out_weight):
    grouped = attended.reshape(SEQUENCE_LENGTH, N_EXP, HEAD_DEV * HEAD_DIM)
    grouped_w = out_weight.reshape(N_EXP, HEAD_DEV * HEAD_DIM, D)

    def add_group(running, index):
        term = jnp.dot(grouped[:, index], grouped_w[index], preferred_element_type=jnp.float32)
        rounded = lax.optimization_barrier(term.astype(jnp.bfloat16))
        return (running + rounded.astype(jnp.float32), None)
    summed, unused = lax.scan(add_group, jnp.zeros((SEQUENCE_LENGTH, D), jnp.float32), jnp.arange(N_EXP, dtype=jnp.int32))
    return summed

def section_layer(piece):
    queries, keys_in, values, decay_rate, out_weight, residual = piece
    attended = block_attention(queries, keys_in, values, decay_rate)
    summed = project_heads(attended, out_weight)
    return (residual.astype(jnp.float32) + summed).astype(jnp.bfloat16)

def dispatch_section(piece):
    normed_s, ids_s, gates_s = piece
    blocks = N_CTX * N_EXP
    doubled = jnp.repeat(normed_s.reshape(blocks, TOK_SHARE, D), 2, axis=1)
    flat_ids = ids_s.reshape(blocks, 2 * TOK_SHARE)
    onehot = (flat_ids[:, :, None] == jnp.arange(EXPERTS, dtype=jnp.int32)[None, None, :]).astype(jnp.int32)
    slot_rank = lax.optimization_barrier(jnp.sum((jnp.cumsum(onehot, axis=1) - onehot) * onehot, axis=-1)).astype(jnp.int32)
    target = (flat_ids * CAP + slot_rank).astype(jnp.int32)
    placement = (target[:, None, :] == jnp.arange(EXPERTS * CAP, dtype=jnp.int32)[None, :, None]).astype(jnp.float32)
    rows = jnp.einsum('bsa,bad->bsd', placement, doubled.astype(jnp.float32)).astype(jnp.bfloat16)
    gate_rows = jnp.einsum('bsa,ba->bs', placement, gates_s.reshape(blocks, 2 * TOK_SHARE).astype(jnp.float32)).astype(jnp.bfloat16)
    rows = jnp.transpose(rows.reshape(N_CTX, N_EXP, EXPERTS, CAP, D), (0, 2, 1, 3, 4))
    gate_rows = jnp.transpose(gate_rows.reshape(N_CTX, N_EXP, EXPERTS, CAP), (0, 2, 1, 3))
    return (rows, gate_rows)

def reference(queries, keys_in, values, decay_rate, out_weight, residual, norm_gain, router, expert_ids):
    hidden = lax.map(section_layer, (queries, keys_in, values, decay_rate, out_weight, residual))
    received = jnp.roll(hidden, 1, axis=0)
    wide = received.astype(jnp.float32)
    mean_sq = lax.optimization_barrier(jnp.mean(wide * wide, axis=-1, keepdims=True))
    normed = (wide * lax.rsqrt(mean_sq + epsilon) * norm_gain[:, None, :]).astype(jnp.bfloat16)
    logits = jnp.einsum('std,sde->ste', normed.astype(jnp.float32), router.astype(jnp.float32))
    expert_table = jnp.arange(EXPERTS, dtype=jnp.int32)
    picked = lax.optimization_barrier(jnp.sum(jnp.where(expert_ids[:, :, :, None] == expert_table, logits[:, :, None, :], 0.0), axis=-1))
    first_gate = jax.nn.sigmoid(picked[:, :, 0] - picked[:, :, 1])
    gate_pair = jnp.stack([first_gate, 1.0 - first_gate], axis=-1).astype(jnp.bfloat16)
    expert_rows, expert_gates = lax.map(dispatch_section, (normed, expert_ids, gate_pair))
    return (expert_rows, expert_gates)
```

```python
import functools

import jax
import jax.numpy as jnp
from jax import lax
from jax.experimental import pallas as pl
from jax.experimental.pallas import tpu as pltpu
from jax.sharding import PartitionSpec as P

HEADS_LOCAL = 4
CAP = 4
EPSILON = 1e-05
LANES = 128
ROWS = 16
MIB = 1 << 20

VMEM = pl.BlockSpec(memory_space=pltpu.VMEM)
ANY = pl.BlockSpec(memory_space=pl.ANY)
bf16 = jnp.bfloat16
f32 = jnp.float32


def iota(shape, dim):
    return lax.broadcasted_iota(jnp.int32, shape, dim)


def mm(a, b, dims):
    return lax.dot_general(a, b, (dims, ((), ())), preferred_element_type=f32)


NN = ((1,), (0,))
NT = ((1,), (1,))
TN = ((0,), (0,))


def to_column(row):
    n = row.shape[1]
    square = jnp.broadcast_to(row, (n, n))
    return jnp.sum(jnp.where(iota((n, n), 0) == iota((n, n), 1), square, jnp.zeros_like(square)), axis=1, keepdims=True)


def cumulative(row):
    n = row.shape[1]
    at, of = iota((n, n), 0), iota((n, n), 1)
    column = -jnp.sum(jnp.where(of <= at, jnp.broadcast_to(row, (n, n)), 0.0), axis=1, keepdims=True)
    along = jnp.sum(jnp.where(at == of, jnp.broadcast_to(column, (n, n)), 0.0), axis=0, keepdims=True)
    return column, along


def pad_rows(heads):
    return -(-3 * heads // ROWS) * ROWS


def put_log(ref, base, heads, h, value):
    for part in range(3):
        piece = value.astype(bf16)
        ref[base + part * heads + h : base + part * heads + h + 1, :] = piece
        value = value - piece.astype(f32)


def get_log(block, heads, h):
    return block[h : h + 1] + block[heads + h : heads + h + 1] + block[2 * heads + h : 2 * heads + h + 1]


def state_kernel(k_ref, v_ref, decay_ref, msg_ref):
    heads = decay_ref.shape[0]
    dh = k_ref.shape[1] // heads
    base = heads * dh
    msg_ref[base:, :] = jnp.zeros((msg_ref.shape[0] - base, dh), bf16)
    for h in range(heads):
        row = decay_ref[h : h + 1, :]
        column, along = cumulative(row)
        last = along[:, -1:]
        tail = jnp.exp(last - column)
        keyed = (k_ref[:, h * dh : (h + 1) * dh].astype(f32) * tail).astype(bf16)
        msg_ref[h * dh : (h + 1) * dh, :] = mm(keyed, v_ref[:, h * dh : (h + 1) * dh], TN).astype(bf16)
        put_log(msg_ref, base, heads, h, jnp.broadcast_to(last, (1, dh)))


def join_kernel(heads, bit, own_ref, got_ref, msg_ref):
    dh = own_ref.shape[1]
    base = heads * dh
    upper = (lax.axis_index("ctx") >> bit) & 1
    is_upper = jnp.full((1, dh), upper, jnp.int32) == 1
    msg_ref[base:, :] = jnp.zeros((msg_ref.shape[0] - base, dh), bf16)
    own_block = own_ref[base:, :].astype(f32)
    got_block = got_ref[base:, :].astype(f32)
    for h in range(heads):
        own_log, got_log = get_log(own_block, heads, h), get_log(got_block, heads, h)
        own = own_ref[h * dh : (h + 1) * dh, :].astype(f32)
        got = got_ref[h * dh : (h + 1) * dh, :].astype(f32)
        scale_own = jnp.where(is_upper, 1.0, jnp.exp(got_log))
        scale_got = jnp.where(is_upper, jnp.exp(own_log), 1.0)
        msg_ref[h * dh : (h + 1) * dh, :] = (scale_own * own + scale_got * got).astype(bf16)
        put_log(msg_ref, base, heads, h, own_log + got_log)


def inside_kernel(q_ref, k_ref, v_ref, decay_ref, ids_ref, weight_ref, inside_ref, slots_ref, weight_out, sem):
    copy = pltpu.make_async_copy(weight_ref, weight_out, sem)
    copy.start()
    heads = decay_ref.shape[0]
    length = q_ref.shape[0]
    dh = q_ref.shape[1] // heads
    causal = iota((length, length), 0) >= iota((length, length), 1)
    for h in range(heads):
        cols = slice(h * dh, (h + 1) * dh)
        column, along = cumulative(decay_ref[h : h + 1, :])
        scores = mm(q_ref[:, cols], k_ref[:, cols], NT)
        weights = jnp.where(causal, scores * jnp.exp(jnp.minimum(column - along, 0.0)), 0.0).astype(bf16)
        inside_ref[:, cols] = mm(weights, v_ref[:, cols], NN)
    n = ids_ref.shape[1]
    earlier = iota((n, n), 1) < iota((n, n), 0)
    rows = [ids_ref[c : c + 1, :] for c in range(2)]
    places = []
    for c in range(2):
        mine = to_column(rows[c])
        rank = jnp.zeros((n, 1), jnp.int32)
        for other in range(2):
            rank += jnp.sum(jnp.where(earlier & (mine == rows[other]), 1, 0), axis=1, keepdims=True)
        places.append(mine * CAP + rank)
    lane = iota((n, LANES), 1)
    slots_ref[...] = jnp.where(lane == 0, places[0], jnp.where(lane == 1, places[1], 0))
    copy.wait()


def project_kernel(bits, order, q_ref, decay_ref, inside_ref, weight_ref, *rest):
    got_refs, (keep_ref, send_ref, attended) = rest[:bits], rest[bits:]
    heads = decay_ref.shape[0]
    dh = q_ref.shape[1] // heads
    base = heads * dh
    place = lax.axis_index("ctx")
    me = lax.axis_index("exp")
    blocks = [ref[base:, :].astype(f32) for ref in got_refs]
    uppers = [jnp.full((1, dh), (place >> bit) & 1, jnp.int32) == 1 for bit in range(bits)]
    for h in range(heads):
        cols = slice(h * dh, (h + 1) * dh)
        column, _ = cumulative(decay_ref[h : h + 1, :])
        incoming = jnp.zeros((dh, dh), f32)
        before = jnp.zeros((1, dh), f32)
        for bit in range(bits):
            got = got_refs[bit][h * dh : (h + 1) * dh, :].astype(f32)
            incoming += jnp.where(uppers[bit], jnp.exp(before), 0.0) * got
            before += jnp.where(uppers[bit], get_log(blocks[bit], heads, h), 0.0)
        high = incoming.astype(bf16)
        low = (incoming - high.astype(f32)).astype(bf16)
        outside = mm(q_ref[:, cols], high, NN) + mm(q_ref[:, cols], low, NN)
        attended[:, cols] = (inside_ref[:, cols] + jnp.exp(column) * outside).astype(bf16)
    share = q_ref.shape[0] // len(order)
    mixed = jnp.concatenate(
        [attended[pl.ds(pl.multiple_of((me ^ k) * share, share), share), :] for k in order], axis=0
    )
    half = mixed.shape[0] // 2
    width = weight_ref.shape[1]
    step = 1024 if width % 1024 == 0 else width
    for start in range(0, width, step):
        part = mm(mixed, weight_ref[:, start : start + step], NN).astype(bf16)
        keep_ref[:, start : start + step] = part[:half]
        send_ref[:, start : start + step] = part[half:]


def norm_kernel(got_ref, gain_ref, router_ref, ids_ref, slots_ref, msg_ref):
    wide = got_ref[...].astype(f32)
    tokens, width = wide.shape
    mean_sq = jnp.sum(wide * wide, axis=1, keepdims=True) * (1.0 / width)
    normed = (wide * lax.rsqrt(mean_sq + EPSILON) * gain_ref[...]).astype(bf16)
    msg_ref[:, :width] = normed
    logits = mm(normed, router_ref[...], NT)
    expert = iota(logits.shape, 1)
    picked = [
        jnp.sum(jnp.where(to_column(ids_ref[c : c + 1, :]) == expert, logits, 0.0), axis=1, keepdims=True)
        for c in range(2)
    ]
    first = 1.0 / (1.0 + jnp.exp(picked[1] - picked[0]))
    lane = iota((tokens, LANES), 1)
    slots = slots_ref[...].astype(f32)
    meta = jnp.where(lane == 2, first, jnp.where(lane == 3, 1.0 - first, slots))
    msg_ref[:, width:] = meta.astype(bf16)


def place_kernel(exp_count, *refs):
    groups, (rows_ref, gates_ref) = refs[:exp_count], refs[exp_count:]
    per_owner, _, cap, width = rows_ref.shape
    me = lax.axis_index("exp")
    tokens = groups[0].shape[0]
    slots = per_owner * exp_count * cap
    wheres, gates = [[], []], [[], []]
    for k in range(exp_count):
        sender = me ^ k
        meta = groups[k][:, width:].astype(f32)
        for c in range(2):
            place = meta[:, c : c + 1].astype(jnp.int32) - me * (per_owner * cap)
            expert, rank = place // cap, place % cap
            mine = (place >= 0) & (place < per_owner * cap)
            wheres[c].append(jnp.where(mine, (expert * exp_count + sender) * cap + rank, -1))
            gates[c].append(meta[:, 2 + c : 3 + c])
    wheres = [jnp.concatenate(w, axis=0) for w in wheres]
    gates = [jnp.concatenate(g, axis=0) for g in gates]
    total = tokens * exp_count
    slot = iota((total, slots), 1)
    chosen = ((wheres[0] == slot) | (wheres[1] == slot)).astype(f32).astype(bf16)
    hit_row = iota((total, per_owner * exp_count), 1)
    hit_rank = iota((total, LANES), 1)
    gate_rows = jnp.zeros((per_owner * exp_count, LANES), f32)
    for c in range(2):
        left = jnp.where((wheres[c] >= 0) & (wheres[c] // cap == hit_row), gates[c], 0.0).astype(bf16)
        right = jnp.where(wheres[c] % cap == hit_rank, 1.0, 0.0).astype(bf16)
        gate_rows += mm(left, right, TN)
    gate_rows = gate_rows.astype(bf16)
    for e in range(per_owner):
        gates_ref[e] = gate_rows[e * exp_count : (e + 1) * exp_count, :cap]
    step = 1024 if width % 1024 == 0 else width
    for start in range(0, width, step):
        block = jnp.concatenate([g[:, start : start + step] for g in groups], axis=0)
        out = mm(chosen, block, TN).astype(bf16)
        rows_ref[:, :, :, start : start + step] = out.reshape(per_owner, exp_count, cap, out.shape[1])


def swap(block, axis, mask):
    return lax.ppermute(block, axis, [(i, i ^ mask) for i in range(lax.axis_size(axis))])


def call(kernel, out, *args, specs=None, out_specs=None, scratch=(), flops=0, moved=0, limit=16 * MIB):
    single = not isinstance(out, (tuple, list))
    return pl.pallas_call(
        kernel,
        out_shape=out,
        in_specs=specs or [VMEM] * len(args),
        out_specs=out_specs or (VMEM if single else (VMEM,) * len(out)),
        scratch_shapes=scratch,
        compiler_params=pltpu.CompilerParams(vmem_limit_bytes=limit),
        cost_estimate=pl.CostEstimate(flops=flops, bytes_accessed=moved, transcendentals=0),
    )(*args)


def on_device(queries, keys_in, values, decay_rate, out_weight, residual, norm_gain, router, expert_ids):
    q, k, v, decay, weight = queries[0], keys_in[0], values[0], decay_rate[0], out_weight[0]
    ids = jnp.swapaxes(expert_ids[0], 0, 1)
    router_t = jnp.swapaxes(router[0], 0, 1)
    length, heads = q.shape[0], decay.shape[0]
    dh = q.shape[1] // heads
    width = weight.shape[1]
    tokens = residual.shape[1]
    exp_count, ctx_count = lax.axis_size("exp"), lax.axis_size("ctx")
    exp_bits, ctx_bits = exp_count.bit_length() - 1, ctx_count.bit_length() - 1
    per_owner = router.shape[2] // exp_count
    shape = jax.ShapeDtypeStruct

    msg_shape = shape((heads * dh + pad_rows(heads), dh), bf16)
    msg = call(state_kernel, msg_shape, k, v, decay)
    got = []
    for bit in range(ctx_bits):
        got.append(swap(msg, "ctx", (2 << bit) - 1))
        if bit < ctx_bits - 1:
            msg = call(functools.partial(join_kernel, heads, bit), msg_shape, msg, got[-1])

    inside, slots, weight_near = call(
        inside_kernel,
        (shape((length, heads * dh), f32), shape((tokens, LANES), jnp.int32), shape(weight.shape, bf16)),
        q, k, v, decay, ids, weight,
        specs=[VMEM] * 5 + [ANY],
        out_specs=(VMEM, VMEM, ANY),
        scratch=[pltpu.SemaphoreType.DMA],
        moved=2 * weight.size * 2,
    )
    order = [sum(((i >> b) & 1) << (exp_bits - 1 - b) for b in range(exp_bits)) for i in range(exp_count)]
    half = shape((length // 2, width), bf16)
    keep, send = call(
        functools.partial(project_kernel, ctx_bits, order),
        (half, half),
        q, decay, inside, weight_near, *got,
        scratch=[pltpu.VMEM((length, heads * dh), bf16)],
        flops=2 * length * weight.size,
        limit=32 * MIB,
    )
    total = keep.astype(f32)
    for bit in range(exp_bits):
        total = total + swap(send, "exp", 1 << bit).astype(f32)
        if bit < exp_bits - 1:
            middle = total.shape[0] // 2
            send, total = total[middle:].astype(bf16), total[:middle]
    hidden = (residual[0].astype(f32) + total).astype(bf16)
    sections = lax.axis_size("section")
    received = lax.ppermute(hidden, "section", [(i, (i + 1) % sections) for i in range(sections)])
    groups = [
        call(norm_kernel, shape((tokens, width + LANES), bf16), received, norm_gain, router_t, ids, slots)
    ]
    for index in range(1, exp_count):
        groups.append(swap(groups[index & (index - 1)], "exp", index & -index))
    rows, gates = call(
        functools.partial(place_kernel, exp_count),
        (shape((per_owner, exp_count, CAP, width), bf16), shape((per_owner, exp_count, CAP), bf16)),
        *groups,
    )
    return rows[None, None], gates[None, None]


def solution(mesh):
    placed = (
        P("section", "ctx", "exp"),
        P("section", "ctx", "exp"),
        P("section", "ctx", "exp"),
        P("section", "exp", "ctx"),
        P("section", "exp", None),
        P("section", ("ctx", "exp"), None),
        P("section", None),
        P("section", None, None),
        P("section", ("ctx", "exp"), None),
    )
    return jax.shard_map(
        on_device,
        mesh=mesh,
        in_specs=placed,
        out_specs=(
            P("section", "ctx", "exp", None, None, None),
            P("section", "ctx", "exp", None, None),
        ),
        check_vma=False,
    )
```

```python
import functools

import jax
import jax.numpy as jnp
from jax import lax
from jax.experimental import pallas as pl
from jax.experimental.pallas import tpu as pltpu
from jax.sharding import PartitionSpec as P

CAP = 4
EPSILON = 1e-05
LANES = 128
ROWS = 16
MIB = 1 << 20
PARTS = 2

VMEM = pl.BlockSpec(memory_space=pltpu.VMEM)
HBM = pl.BlockSpec(memory_space=pltpu.HBM)
bf16 = jnp.bfloat16
f32 = jnp.float32


def iota(shape, dim):
    return lax.broadcasted_iota(jnp.int32, shape, dim)


def mm(a, b, dims):
    return lax.dot_general(a, b, (dims, ((), ())), preferred_element_type=f32)


NN = ((1,), (0,))
NT = ((1,), (1,))
TN = ((0,), (0,))


def to_column(row):
    n = row.shape[1]
    square = jnp.broadcast_to(row, (n, n))
    return jnp.sum(jnp.where(iota((n, n), 0) == iota((n, n), 1), square, jnp.zeros_like(square)), axis=1, keepdims=True)


def cumulative(row):
    n = row.shape[1]
    at, of = iota((n, n), 0), iota((n, n), 1)
    column = -jnp.sum(jnp.where(of <= at, jnp.broadcast_to(row, (n, n)), 0.0), axis=1, keepdims=True)
    along = jnp.sum(jnp.where(at == of, jnp.broadcast_to(column, (n, n)), 0.0), axis=0, keepdims=True)
    return column, along


def pad_rows(heads):
    return -(-3 * heads // ROWS) * ROWS


def put_log(ref, base, heads, h, value):
    for part in range(3):
        piece = value.astype(bf16)
        ref[base + part * heads + h : base + part * heads + h + 1, :] = piece
        value = value - piece.astype(f32)


def get_log(block, heads, h):
    return block[h : h + 1] + block[heads + h : heads + h + 1] + block[2 * heads + h : 2 * heads + h + 1]


def fetch(sources, places, sems):
    copies = [pltpu.make_async_copy(s, p, sems.at[i]) for i, (s, p) in enumerate(zip(sources, places, strict=True))]
    for copy in copies:
        copy.start()
    return copies


def state_kernel(k_hbm, v_hbm, decay_hbm, msg_ref, k_ref, v_ref, decay_ref, sems):
    copies = fetch((decay_hbm, k_hbm, v_hbm), (decay_ref, k_ref, v_ref), sems)
    heads = decay_ref.shape[0]
    dh = k_ref.shape[1] // heads
    base = heads * dh
    msg_ref[base:, :] = jnp.zeros((msg_ref.shape[0] - base, dh), bf16)
    copies[0].wait()
    tails = []
    for h in range(heads):
        column, along = cumulative(decay_ref[h : h + 1, :])
        last = along[:, -1:]
        tails.append(jnp.exp(last - column))
        put_log(msg_ref, base, heads, h, jnp.broadcast_to(last, (1, dh)))
    copies[1].wait()
    copies[2].wait()
    for h in range(heads):
        keyed = (k_ref[:, h * dh : (h + 1) * dh].astype(f32) * tails[h]).astype(bf16)
        msg_ref[h * dh : (h + 1) * dh, :] = mm(keyed, v_ref[:, h * dh : (h + 1) * dh], TN).astype(bf16)


def joined(heads, bit, own_ref, got_ref):
    dh = own_ref.shape[1]
    base = heads * dh
    upper = (lax.axis_index("ctx") >> bit) & 1
    is_upper = jnp.full((1, dh), upper, jnp.int32) == 1
    own_block = own_ref[base:, :].astype(f32)
    got_block = got_ref[base:, :].astype(f32)
    for h in range(heads):
        own_log, got_log = get_log(own_block, heads, h), get_log(got_block, heads, h)
        own = own_ref[h * dh : (h + 1) * dh, :].astype(f32)
        got = got_ref[h * dh : (h + 1) * dh, :].astype(f32)
        scale_own = jnp.where(is_upper, 1.0, jnp.exp(got_log))
        scale_got = jnp.where(is_upper, jnp.exp(own_log), 1.0)
        yield scale_own * own + scale_got * got, own_log + got_log


def join_kernel(heads, bit, own_ref, got_ref, msg_ref):
    dh = own_ref.shape[1]
    base = heads * dh
    msg_ref[base:, :] = jnp.zeros((msg_ref.shape[0] - base, dh), bf16)
    for h, (state, log) in enumerate(joined(heads, bit, own_ref, got_ref)):
        msg_ref[h * dh : (h + 1) * dh, :] = state.astype(bf16)
        put_log(msg_ref, base, heads, h, log)


def split_mm(a, state):
    high = state.astype(bf16)
    low = (state - high.astype(f32)).astype(bf16)
    return mm(a, high, NN) + mm(a, low, NN)


def inside_kernel(q_hbm, k_hbm, v_hbm, decay_hbm, ids_hbm, weight_hbm, inside_ref, slots_ref, weight_ref, q_ref, growth_ref,
                  k_ref, v_ref, decay_ref, ids_ref, sems):
    copies = fetch(
        (decay_hbm, ids_hbm, q_hbm, k_hbm, v_hbm, weight_hbm), (decay_ref, ids_ref, q_ref, k_ref, v_ref, weight_ref), sems
    )
    for copy in copies[:-1]:
        copy.wait()
    heads = decay_ref.shape[0]
    length = q_ref.shape[0]
    dh = q_ref.shape[1] // heads
    causal = iota((length, length), 0) >= iota((length, length), 1)
    lane = iota((length, LANES), 1)
    growth = jnp.zeros((length, LANES), f32)
    for h in range(heads):
        cols = slice(h * dh, (h + 1) * dh)
        column, along = cumulative(decay_ref[h : h + 1, :])
        scores = mm(q_ref[:, cols], k_ref[:, cols], NT)
        weights = jnp.where(causal, scores * jnp.exp(jnp.minimum(column - along, 0.0)), 0.0).astype(bf16)
        inside_ref[:, cols] = mm(weights, v_ref[:, cols], NN)
        growth = jnp.where(lane == h, jnp.exp(column), growth)
    growth_ref[...] = growth
    n = ids_ref.shape[1]
    earlier = iota((n, n), 1) < iota((n, n), 0)
    rows = [ids_ref[c : c + 1, :] for c in range(2)]
    places = []
    for c in range(2):
        mine = to_column(rows[c])
        rank = jnp.zeros((n, 1), jnp.int32)
        for other in range(2):
            rank += jnp.sum(jnp.where(earlier & (mine == rows[other]), 1, 0), axis=1, keepdims=True)
        places.append(mine * CAP + rank)
    lane = iota((n, LANES), 1)
    slots_ref[...] = jnp.where(lane == 0, places[0], jnp.where(lane == 1, places[1], 0))
    copies[-1].wait()


def base_kernel(heads, q_ref, inside_ref, growth_ref, *rest):
    got_refs, (base_ref, scale_ref) = rest[:-2], rest[-2:]
    bits = len(got_refs)
    dh = q_ref.shape[1] // heads
    base = heads * dh
    place = lax.axis_index("ctx")
    blocks = [ref[base:, :].astype(f32) for ref in got_refs]
    uppers = [jnp.full((1, dh), (place >> bit) & 1, jnp.int32) == 1 for bit in range(bits + 1)]
    lane = iota(scale_ref.shape, 1)
    scale = jnp.zeros(scale_ref.shape, f32)
    for h in range(heads):
        cols = slice(h * dh, (h + 1) * dh)
        incoming = jnp.zeros((dh, dh), f32)
        before = jnp.zeros((1, dh), f32)
        for bit in range(bits):
            got = got_refs[bit][h * dh : (h + 1) * dh, :].astype(f32)
            incoming += jnp.where(uppers[bit], jnp.exp(before), 0.0) * got
            before += jnp.where(uppers[bit], get_log(blocks[bit], heads, h), 0.0)
        growth = growth_ref[:, h : h + 1]
        base_ref[:, cols] = inside_ref[:, cols] + growth * split_mm(q_ref[:, cols], incoming)
        factor = jnp.where(uppers[bits], jnp.exp(before), 0.0)
        scale = jnp.where(lane == h, growth * factor[:, :1], scale)
    scale_ref[...] = scale


def mix_kernel(heads, order, start, stop, q_ref, base_ref, scale_ref, got_ref, weight_ref, mixed_ref, keep_ref, send_ref, attended):
    dh = base_ref.shape[1] // heads
    me = lax.axis_index("exp")
    for h in range(heads):
        cols = slice(h * dh, (h + 1) * dh)
        outside = mm(q_ref[:, cols], got_ref[h * dh : (h + 1) * dh, :], NN)
        attended[:, cols] = (base_ref[:, cols] + scale_ref[:, h : h + 1] * outside).astype(bf16)
    share = base_ref.shape[0] // len(order)
    for i, k in enumerate(order):
        mixed_ref[i * share : (i + 1) * share, :] = attended[pl.ds(pl.multiple_of((me ^ k) * share, share), share), :]
    project_kernel(start, stop, mixed_ref, weight_ref, keep_ref, send_ref)


def project_kernel(start, stop, mixed_ref, weight_ref, keep_ref, send_ref):
    half = mixed_ref.shape[0] // 2
    mixed = mixed_ref[...]
    for at, to in pieces(start, stop):
        part = mm(mixed, weight_ref[:, at:to], NN).astype(bf16)
        keep_ref[:, at - start : to - start] = part[:half]
        send_ref[:, at - start : to - start] = part[half:]


def pieces(start, stop, step=1024):
    return [(at, min(at + step, stop)) for at in range(start, stop, step)]


def halve_kernel(keep_ref, got_ref, send_ref, own_ref):
    half = own_ref.shape[0]
    own_ref[...] = keep_ref[:half, :].astype(f32) + got_ref[:half, :].astype(f32)
    send_ref[...] = (keep_ref[half:, :].astype(f32) + got_ref[half:, :].astype(f32)).astype(bf16)


def hidden_kernel(start, own_ref, got_ref, residual_ref, out_ref):
    stop = start + own_ref.shape[1]
    total = own_ref[...].astype(f32) + got_ref[...].astype(f32)
    out_ref[...] = (residual_ref[:, start:stop].astype(f32) + total).astype(bf16)


def tag_kernel(got_ref, slots_ref, msg_ref):
    size = got_ref.shape[1]
    msg_ref[:, :size] = got_ref[...]
    msg_ref[:, size:] = slots_ref[...].astype(f32).astype(bf16)


def partial(groups, gain, router, start):
    square, logits = 0.0, 0.0
    for at, to in pieces(0, groups[0].shape[1] // LANES * LANES):
        wide = jnp.concatenate([g[:, at:to] for g in groups], axis=0).astype(f32)
        square += jnp.sum(wide * wide, axis=1, keepdims=True)
        gained = (wide * gain[:, start + at : start + to]).astype(bf16)
        logits += mm(gained, router[:, start + at : start + to], NT)
    return square, logits


def ahead_kernel(exp_count, experts, *refs):
    groups, (gain_ref, router_ref, chosen_ref, target_ref, square_ref, logits_ref) = refs[:exp_count], refs[exp_count:]
    size = groups[0].shape[1] - LANES
    per_owner = experts // exp_count
    me = lax.axis_index("exp")
    tokens = groups[0].shape[0]
    wheres, named = [[], []], [[], []]
    for k in range(exp_count):
        sender = me ^ k
        meta = groups[k][:, size:].astype(f32).astype(jnp.int32)
        for c in range(2):
            slot = meta[:, c : c + 1]
            place = slot - me * (per_owner * CAP)
            mine = (place >= 0) & (place < per_owner * CAP)
            wheres[c].append(jnp.where(mine, (place // CAP * exp_count + sender) * CAP + place % CAP, -1))
            named[c].append(slot // CAP)
    wheres = [jnp.concatenate(w, axis=0) for w in wheres]
    named = [jnp.concatenate(n, axis=0) for n in named]
    total = tokens * exp_count
    slot = iota(chosen_ref.shape, 1)
    chosen_ref[...] = ((wheres[0] == slot) | (wheres[1] == slot)).astype(f32).astype(bf16)
    lane = iota((total, LANES), 1)
    target = jnp.zeros((total, LANES), jnp.int32)
    for i, column in enumerate(wheres + named):
        target = jnp.where(lane == i, column, target)
    target_ref[...] = target
    square, logits = partial([g.at[:, :size] for g in groups], gain_ref, router_ref, 0)
    square_ref[...] = jnp.broadcast_to(square, square_ref.shape)
    logits_ref[...] = logits


def place_kernel(exp_count, parts, *refs):
    groups = [refs[i * exp_count : (i + 1) * exp_count] for i in range(parts)]
    chosen_ref, target_ref, square_ref, logits_ref, gain_ref, router_ref, rows_hbm, gates_ref, rows_ref, sems = refs[parts * exp_count :]
    per_owner, _, cap, width = rows_ref.shape
    sizes = [part[0].shape[1] for part in groups]
    sizes[0] -= LANES
    square, logits = square_ref[:, :1], logits_ref[...]
    at = sizes[0]
    for part, size in zip(groups[1:], sizes[1:]):
        more = partial(part, gain_ref, router_ref, at)
        square, logits = square + more[0], logits + more[1]
        at += size
    factor = lax.rsqrt(square * (1.0 / width) + EPSILON)
    chosen = chosen_ref[...]
    copies = []
    at = 0
    for part, size in zip(groups, sizes):
        for start, stop in pieces(0, size):
            wide = jnp.concatenate([g[:, start:stop] for g in part], axis=0).astype(f32)
            normed = (wide * factor * gain_ref[:, at + start : at + stop]).astype(bf16)
            out = mm(chosen, normed, TN).astype(bf16)
            window = (slice(None), slice(None), slice(None), slice(at + start, at + stop))
            rows_ref[window] = out.reshape(per_owner, exp_count, cap, stop - start)
            copies.append(pltpu.make_async_copy(rows_ref.at[window], rows_hbm.at[window], sems.at[len(copies)]))
            copies[-1].start()
        at += size
    logits = logits * factor
    target = target_ref[...]
    wheres, named = [target[:, c : c + 1] for c in range(2)], [target[:, 2 + c : 3 + c] for c in range(2)]
    expert = iota(logits.shape, 1)
    picked = [jnp.sum(jnp.where(named[c] == expert, logits, 0.0), axis=1, keepdims=True) for c in range(2)]
    first = 1.0 / (1.0 + jnp.exp(picked[1] - picked[0]))
    gates = [first, 1.0 - first]
    total = logits.shape[0]
    hit_row = iota((total, per_owner * exp_count), 1)
    hit_rank = iota((total, LANES), 1)
    gate_rows = jnp.zeros((per_owner * exp_count, LANES), f32)
    for c in range(2):
        left = jnp.where((wheres[c] >= 0) & (wheres[c] // cap == hit_row), gates[c], 0.0).astype(bf16)
        right = jnp.where(wheres[c] % cap == hit_rank, 1.0, 0.0).astype(bf16)
        gate_rows += mm(left, right, TN)
    gate_rows = gate_rows.astype(bf16)
    for e in range(per_owner):
        gates_ref[e] = gate_rows[e * exp_count : (e + 1) * exp_count, :cap]
    for copy in copies:
        copy.wait()


def swap(block, axis, mask):
    return lax.ppermute(block, axis, [(i, i ^ mask) for i in range(lax.axis_size(axis))])


def call(kernel, out, *args, specs=None, out_specs=None, scratch=(), flops=0, moved=0, limit=16 * MIB):
    single = not isinstance(out, (tuple, list))
    specs = specs or [VMEM] * len(args)
    args = [pltpu.with_memory_space_constraint(a, pltpu.HBM) if s is HBM else a for a, s in zip(args, specs, strict=True)]
    return pl.pallas_call(
        kernel,
        out_shape=out,
        in_specs=specs,
        out_specs=out_specs or (VMEM if single else (VMEM,) * len(out)),
        scratch_shapes=scratch,
        compiler_params=pltpu.CompilerParams(vmem_limit_bytes=limit),
        cost_estimate=pl.CostEstimate(flops=flops, bytes_accessed=moved, transcendentals=0),
    )(*args)


def on_device(queries, keys_in, values, decay_rate, out_weight, residual, norm_gain, router, expert_ids):
    q, k, v, decay, weight = queries[0], keys_in[0], values[0], decay_rate[0], out_weight[0]
    ids = jnp.swapaxes(expert_ids[0], 0, 1)
    router_t = jnp.swapaxes(router[0], 0, 1)
    length, heads = q.shape[0], decay.shape[0]
    dh = q.shape[1] // heads
    width = weight.shape[1]
    tokens = residual.shape[1]
    exp_count, ctx_count = lax.axis_size("exp"), lax.axis_size("ctx")
    exp_bits, ctx_bits = exp_count.bit_length() - 1, ctx_count.bit_length() - 1
    per_owner = router.shape[2] // exp_count
    shape = jax.ShapeDtypeStruct

    msg_shape = shape((heads * dh + pad_rows(heads), dh), bf16)
    part = pltpu.VMEM((length, heads * dh), bf16)
    small = pltpu.VMEM(decay.shape, f32)
    dma = pltpu.SemaphoreType.DMA
    msg = call(state_kernel, msg_shape, k, v, decay, specs=[HBM] * 3, scratch=[part, part, small, dma((3,))])
    got = []
    for bit in range(ctx_bits):
        got.append(swap(msg, "ctx", (2 << bit) - 1))
        if bit < ctx_bits - 1:
            msg = call(functools.partial(join_kernel, heads, bit), msg_shape, msg, got[-1])
    inside, slots, weight_near, q_near, growth = call(
        inside_kernel,
        (
            shape((length, heads * dh), f32),
            shape((tokens, LANES), jnp.int32),
            shape(weight.shape, bf16),
            shape(q.shape, bf16),
            shape((length, LANES), f32),
        ),
        q, k, v, decay, ids, weight,
        specs=[HBM] * 6,
        scratch=[part, part, small, pltpu.VMEM(ids.shape, jnp.int32), dma((6,))],
        moved=weight.size * 2,
    )
    base, scale = call(
        functools.partial(base_kernel, heads),
        (shape((length, heads * dh), f32), shape((length, LANES), f32)),
        q_near, inside, growth, *got[:-1],
    )
    order = [sum(((i >> b) & 1) << (exp_bits - 1 - b) for b in range(exp_bits)) for i in range(exp_count)]
    cuts = [width * i // PARTS // LANES * LANES for i in range(PARTS + 1)]
    mixed, groups = None, []
    for start, stop in zip(cuts, cuts[1:]):
        half = shape((length // 2, stop - start), bf16)
        if mixed is None:
            mixed, keep, send = call(
                functools.partial(mix_kernel, heads, order, start, stop),
                (shape((length, heads * dh), bf16), half, half),
                q_near, base, scale, got[-1], weight_near,
                scratch=[part],
                flops=2 * length * heads * dh * (stop - start),
            )
        else:
            keep, send = call(
                functools.partial(project_kernel, start, stop),
                (half, half),
                mixed, weight_near,
                flops=2 * length * heads * dh * (stop - start),
            )
        for bit in range(exp_bits - 1):
            rest = (keep.shape[0] // 2, stop - start)
            send, keep = call(halve_kernel, (shape(rest, bf16), shape(rest, f32)), keep, swap(send, "exp", 1 << bit))
        hidden = call(
            functools.partial(hidden_kernel, start),
            shape((tokens, stop - start), bf16),
            keep, swap(send, "exp", exp_count // 2), residual[0],
        )
        sections = lax.axis_size("section")
        received = lax.ppermute(hidden, "section", [(i, (i + 1) % sections) for i in range(sections)])
        if not groups:
            received = call(tag_kernel, shape((tokens, stop - start + LANES), bf16), received, slots)
        groups.append([received])
        for index in range(1, exp_count):
            groups[-1].append(swap(groups[-1][index & (index - 1)], "exp", index & -index))
    rows_shape = (per_owner, exp_count, CAP, width)
    count = sum(len(pieces(start, stop)) for start, stop in zip(cuts, cuts[1:]))
    all_tokens, experts = exp_count * tokens, per_owner * exp_count
    facts = call(
        functools.partial(ahead_kernel, exp_count, experts),
        (
            shape((all_tokens, experts * CAP), bf16),
            shape((all_tokens, LANES), jnp.int32),
            shape((all_tokens, LANES), f32),
            shape((all_tokens, experts), f32),
        ),
        *groups[0], norm_gain, router_t,
    )
    rows, gates = call(
        functools.partial(place_kernel, exp_count, PARTS),
        (shape(rows_shape, bf16), shape((per_owner, exp_count, CAP), bf16)),
        *[g for part_groups in groups for g in part_groups], *facts, norm_gain, router_t,
        out_specs=(HBM, VMEM),
        scratch=[pltpu.VMEM(rows_shape, bf16), dma((count,))],
    )
    return rows[None, None], gates[None, None]


def solution(mesh):
    placed = (
        P("section", "ctx", "exp"),
        P("section", "ctx", "exp"),
        P("section", "ctx", "exp"),
        P("section", "exp", "ctx"),
        P("section", "exp", None),
        P("section", ("ctx", "exp"), None),
        P("section", None),
        P("section", None, None),
        P("section", ("ctx", "exp"), None),
    )
    return jax.shard_map(
        on_device,
        mesh=mesh,
        in_specs=placed,
        out_specs=(
            P("section", "ctx", "exp", None, None, None),
            P("section", "ctx", "exp", None, None),
        ),
        check_vma=False,
    )
```

```python
import functools

import jax
import jax.numpy as jnp
from jax import lax
from jax.experimental import pallas as pl
from jax.experimental.pallas import tpu as pltpu
from jax.sharding import PartitionSpec as P

CAP = 4
EPSILON = 1e-05
LANES = 128
ROWS = 16
MIB = 1 << 20
PARTS = 2

VMEM = pl.BlockSpec(memory_space=pltpu.VMEM)
HBM = pl.BlockSpec(memory_space=pltpu.HBM)
bf16 = jnp.bfloat16
f32 = jnp.float32


def iota(shape, dim):
    return lax.broadcasted_iota(jnp.int32, shape, dim)


def mm(a, b, dims):
    return lax.dot_general(a, b, (dims, ((), ())), preferred_element_type=f32)


NN = ((1,), (0,))
NT = ((1,), (1,))
TN = ((0,), (0,))


def to_column(row):
    n = row.shape[1]
    square = jnp.broadcast_to(row, (n, n))
    return jnp.sum(jnp.where(iota((n, n), 0) == iota((n, n), 1), square, jnp.zeros_like(square)), axis=1, keepdims=True)


def cumulative(row):
    n = row.shape[1]
    at, of = iota((n, n), 0), iota((n, n), 1)
    column = -jnp.sum(jnp.where(of <= at, jnp.broadcast_to(row, (n, n)), 0.0), axis=1, keepdims=True)
    along = jnp.sum(jnp.where(at == of, jnp.broadcast_to(column, (n, n)), 0.0), axis=0, keepdims=True)
    return column, along


def pad_rows(heads):
    return -(-3 * heads // ROWS) * ROWS


def put_log(ref, base, heads, h, value):
    for part in range(3):
        piece = value.astype(bf16)
        ref[base + part * heads + h : base + part * heads + h + 1, :] = piece
        value = value - piece.astype(f32)


def get_log(block, heads, h):
    return block[h : h + 1] + block[heads + h : heads + h + 1] + block[2 * heads + h : 2 * heads + h + 1]


def fetch(sources, places, sems):
    copies = [pltpu.make_async_copy(s, p, sems.at[i]) for i, (s, p) in enumerate(zip(sources, places, strict=True))]
    for copy in copies:
        copy.start()
    return copies


def state_kernel(k_hbm, v_hbm, decay_hbm, msg_ref, k_ref, v_ref, decay_ref, sems):
    copies = fetch((decay_hbm, k_hbm, v_hbm), (decay_ref, k_ref, v_ref), sems)
    heads = decay_ref.shape[0]
    dh = k_ref.shape[1] // heads
    base = heads * dh
    msg_ref[base:, :] = jnp.zeros((msg_ref.shape[0] - base, dh), bf16)
    copies[0].wait()
    tails = []
    for h in range(heads):
        column, along = cumulative(decay_ref[h : h + 1, :])
        last = along[:, -1:]
        tails.append(jnp.exp(last - column))
        put_log(msg_ref, base, heads, h, jnp.broadcast_to(last, (1, dh)))
    copies[1].wait()
    copies[2].wait()
    for h in range(heads):
        keyed = (k_ref[:, h * dh : (h + 1) * dh].astype(f32) * tails[h]).astype(bf16)
        msg_ref[h * dh : (h + 1) * dh, :] = mm(keyed, v_ref[:, h * dh : (h + 1) * dh], TN).astype(bf16)


def joined(heads, bit, own_ref, got_ref):
    dh = own_ref.shape[1]
    base = heads * dh
    upper = (lax.axis_index("ctx") >> bit) & 1
    is_upper = jnp.full((1, dh), upper, jnp.int32) == 1
    own_block = own_ref[base:, :].astype(f32)
    got_block = got_ref[base:, :].astype(f32)
    for h in range(heads):
        own_log, got_log = get_log(own_block, heads, h), get_log(got_block, heads, h)
        own = own_ref[h * dh : (h + 1) * dh, :].astype(f32)
        got = got_ref[h * dh : (h + 1) * dh, :].astype(f32)
        scale_own = jnp.where(is_upper, 1.0, jnp.exp(got_log))
        scale_got = jnp.where(is_upper, jnp.exp(own_log), 1.0)
        yield scale_own * own + scale_got * got, own_log + got_log


def join_kernel(heads, bit, own_ref, got_ref, msg_ref):
    dh = own_ref.shape[1]
    base = heads * dh
    msg_ref[base:, :] = jnp.zeros((msg_ref.shape[0] - base, dh), bf16)
    for h, (state, log) in enumerate(joined(heads, bit, own_ref, got_ref)):
        msg_ref[h * dh : (h + 1) * dh, :] = state.astype(bf16)
        put_log(msg_ref, base, heads, h, log)


def split_mm(a, state):
    high = state.astype(bf16)
    low = (state - high.astype(f32)).astype(bf16)
    return mm(a, high, NN) + mm(a, low, NN)


def inside_kernel(q_hbm, k_hbm, v_hbm, decay_hbm, ids_hbm, weight_hbm, inside_ref, slots_ref, weight_ref, q_ref, growth_ref,
                  k_ref, v_ref, decay_ref, ids_ref, sems):
    copies = fetch(
        (decay_hbm, ids_hbm, q_hbm, k_hbm, v_hbm, weight_hbm), (decay_ref, ids_ref, q_ref, k_ref, v_ref, weight_ref), sems
    )
    for copy in copies[:-1]:
        copy.wait()
    heads = decay_ref.shape[0]
    length = q_ref.shape[0]
    dh = q_ref.shape[1] // heads
    causal = iota((length, length), 0) >= iota((length, length), 1)
    lane = iota((length, LANES), 1)
    growth = jnp.zeros((length, LANES), f32)
    for h in range(heads):
        cols = slice(h * dh, (h + 1) * dh)
        column, along = cumulative(decay_ref[h : h + 1, :])
        scores = mm(q_ref[:, cols], k_ref[:, cols], NT)
        weights = jnp.where(causal, scores * jnp.exp(jnp.minimum(column - along, 0.0)), 0.0).astype(bf16)
        inside_ref[:, cols] = mm(weights, v_ref[:, cols], NN)
        growth = jnp.where(lane == h, jnp.exp(column), growth)
    growth_ref[...] = growth
    n = ids_ref.shape[1]
    earlier = iota((n, n), 1) < iota((n, n), 0)
    rows = [ids_ref[c : c + 1, :] for c in range(2)]
    places = []
    for c in range(2):
        mine = to_column(rows[c])
        rank = jnp.zeros((n, 1), jnp.int32)
        for other in range(2):
            rank += jnp.sum(jnp.where(earlier & (mine == rows[other]), 1, 0), axis=1, keepdims=True)
        places.append(mine * CAP + rank)
    lane = iota((n, LANES), 1)
    slots_ref[...] = jnp.where(lane == 0, places[0], jnp.where(lane == 1, places[1], 0))
    copies[-1].wait()


def base_kernel(heads, q_ref, inside_ref, growth_ref, *rest):
    got_refs, (base_ref, scale_ref) = rest[:-2], rest[-2:]
    bits = len(got_refs)
    dh = q_ref.shape[1] // heads
    base = heads * dh
    place = lax.axis_index("ctx")
    blocks = [ref[base:, :].astype(f32) for ref in got_refs]
    uppers = [jnp.full((1, dh), (place >> bit) & 1, jnp.int32) == 1 for bit in range(bits + 1)]
    lane = iota(scale_ref.shape, 1)
    scale = jnp.zeros(scale_ref.shape, f32)
    for h in range(heads):
        cols = slice(h * dh, (h + 1) * dh)
        incoming = jnp.zeros((dh, dh), f32)
        before = jnp.zeros((1, dh), f32)
        for bit in range(bits):
            got = got_refs[bit][h * dh : (h + 1) * dh, :].astype(f32)
            incoming += jnp.where(uppers[bit], jnp.exp(before), 0.0) * got
            before += jnp.where(uppers[bit], get_log(blocks[bit], heads, h), 0.0)
        growth = growth_ref[:, h : h + 1]
        base_ref[:, cols] = inside_ref[:, cols] + growth * split_mm(q_ref[:, cols], incoming)
        factor = jnp.where(uppers[bits], jnp.exp(before), 0.0)
        scale = jnp.where(lane == h, growth * factor[:, :1], scale)
    scale_ref[...] = scale


def mix_kernel(heads, order, stop, q_ref, base_ref, scale_ref, got_ref, weight_ref, slots_ref, mixed_ref, keep_ref, send_ref, attended):
    dh = base_ref.shape[1] // heads
    me = lax.axis_index("exp")
    for h in range(heads):
        cols = slice(h * dh, (h + 1) * dh)
        outside = mm(q_ref[:, cols], got_ref[h * dh : (h + 1) * dh, :], NN)
        attended[:, cols] = (base_ref[:, cols] + scale_ref[:, h : h + 1] * outside).astype(bf16)
    share = base_ref.shape[0] // len(order)
    for i, k in enumerate(order):
        mixed_ref[i * share : (i + 1) * share, :] = attended[pl.ds(pl.multiple_of((me ^ k) * share, share), share), :]
    project_kernel(0, stop, mixed_ref, weight_ref, keep_ref, send_ref)
    put_lanes(send_ref, slots_ref[...].astype(f32))


def project_kernel(start, stop, mixed_ref, weight_ref, keep_ref, send_ref):
    half = mixed_ref.shape[0] // 2
    mixed = mixed_ref[...]
    for at, to in pieces(start, stop):
        part = mm(mixed, weight_ref[:, at:to], NN).astype(bf16)
        keep_ref[:, at - start : to - start] = part[:half]
        send_ref[:, at - start : to - start] = part[half:]


def pieces(start, stop, step=1024):
    return [(at, min(at + step, stop)) for at in range(start, stop, step)]


def put_lanes(ref, lanes):
    tokens = lanes.shape[0]
    ref[:tokens, -LANES:] = lanes.astype(bf16)
    if ref.shape[0] > tokens:
        ref[tokens:, -LANES:] = jnp.zeros((ref.shape[0] - tokens, LANES), bf16)


def widen_lanes(bit, tokens, sent_ref, got_ref):
    own, got = sent_ref[:tokens, -LANES:].astype(f32), got_ref[:tokens, -LANES:].astype(f32)
    filled = 2 << bit
    return jnp.where(iota(own.shape, 1) < filled, own, jnp.roll(got, filled, axis=1))


def halve_kernel(bit, tokens, tagged, keep_ref, sent_ref, got_ref, send_ref, own_ref):
    half, width = own_ref.shape
    own_ref[...] = keep_ref[:half, :].astype(f32) + got_ref[:half, :width].astype(f32)
    send_ref[:, :width] = (keep_ref[half:, :].astype(f32) + got_ref[half:, :width].astype(f32)).astype(bf16)
    if tagged:
        put_lanes(send_ref, widen_lanes(bit, tokens, sent_ref, got_ref))


def carry_kernel(bit, start, tagged, keep_ref, sent_ref, got_ref, residual_ref, out_ref):
    tokens = residual_ref.shape[0]
    width = keep_ref.shape[1]
    total = keep_ref[...].astype(f32) + got_ref[:, :width].astype(f32)
    own = total[:tokens] + residual_ref[:, start : start + width].astype(f32)
    out_ref[:tokens, :width] = own.astype(bf16)
    out_ref[tokens:, :width] = total[tokens:].astype(bf16)
    if tagged:
        put_lanes(out_ref, widen_lanes(bit, tokens, sent_ref, got_ref))


def combine_kernel(own_ref, got_ref, out_ref):
    rows, width = out_ref.shape
    half = rows // 2
    out_ref[:half, :] = (own_ref[:half, :width].astype(f32) + got_ref[half:, :width].astype(f32)).astype(bf16)
    out_ref[half:, :] = (own_ref[half:, :width].astype(f32) + got_ref[:half, :width].astype(f32)).astype(bf16)


def squares(groups, size):
    total = 0.0
    for at, to in pieces(0, size):
        wide = jnp.concatenate([g[:, at:to] for g in groups], axis=0).astype(f32)
        total += jnp.sum(wide * wide, axis=1, keepdims=True)
    return total


def products(groups, size, gain, router, start):
    total = 0.0
    for at, to in pieces(0, size):
        wide = jnp.concatenate([g[:, at:to] for g in groups], axis=0).astype(f32)
        gained = (wide * gain[:, start + at : start + to]).astype(bf16)
        total += mm(gained, router[:, start + at : start + to], NT)
    return total


def facts_kernel(exp_count, experts, tokens, own_ref, got_ref, chosen_ref, target_ref):
    per_owner = experts // exp_count
    top = exp_count // 2
    me = lax.axis_index("exp")
    lanes = [ref[:tokens, -LANES:].astype(f32).astype(jnp.int32) for ref in (own_ref, got_ref)]
    wheres, named = [[], []], [[], []]
    for j in range(top):
        for side in range(2):
            sender = me ^ (j + side * top)
            for c in range(2):
                slot = lanes[side][:, 2 * j + c : 2 * j + c + 1]
                place = slot - me * (per_owner * CAP)
                mine = (place >= 0) & (place < per_owner * CAP)
                wheres[c].append(jnp.where(mine, (place // CAP * exp_count + sender) * CAP + place % CAP, -1))
                named[c].append(slot // CAP)
    wheres = [jnp.concatenate(w, axis=0) for w in wheres]
    named = [jnp.concatenate(n, axis=0) for n in named]
    total = tokens * exp_count
    slot = iota(chosen_ref.shape, 1)
    chosen_ref[...] = ((wheres[0] == slot) | (wheres[1] == slot)).astype(f32).astype(bf16)
    lane = iota((total, LANES), 1)
    target = jnp.zeros((total, LANES), jnp.int32)
    for i, column in enumerate(wheres + named):
        target = jnp.where(lane == i, column, target)
    target_ref[...] = target


def ahead_kernel(count, *refs):
    blocks, (gain_ref, router_ref, square_ref, logits_ref) = refs[:count], refs[count:]
    size = blocks[0].shape[1]
    square_ref[...] = jnp.broadcast_to(squares(blocks, size), square_ref.shape)
    logits_ref[...] = products(blocks, size, gain_ref, router_ref, 0)


def place_kernel(count, parts, *refs):
    groups = [refs[i * count : (i + 1) * count] for i in range(parts)]
    exp_count = 2 * count
    chosen_ref, target_ref, square_ref, logits_ref, gain_ref, router_ref, *outs = refs[parts * count :]
    rows_hbm, gates_hbm, rows_ref, gates_ref, sems = outs
    per_owner, _, cap, width = rows_ref.shape
    sizes = [part[0].shape[1] for part in groups]
    square = square_ref[:, :1]
    for part, size in zip(groups[1:], sizes[1:]):
        square += squares(part, size)
    factor = lax.rsqrt(square * (1.0 / width) + EPSILON)
    chosen = chosen_ref[...]
    copies = []
    logits = logits_ref[...]
    at = sizes[0]
    for part, size in zip(groups[1:], sizes[1:]):
        logits += products(part, size, gain_ref, router_ref, at)
        at += size
    logits = logits * factor
    target = target_ref[...]
    wheres, named = [target[:, c : c + 1] for c in range(2)], [target[:, 2 + c : 3 + c] for c in range(2)]
    expert = iota(logits.shape, 1)
    picked = [jnp.sum(jnp.where(named[c] == expert, logits, 0.0), axis=1, keepdims=True) for c in range(2)]
    first = 1.0 / (1.0 + jnp.exp(picked[1] - picked[0]))
    gates = [first, 1.0 - first]
    total = logits.shape[0]
    hit_row = iota((total, per_owner * exp_count), 1)
    hit_rank = iota((total, LANES), 1)
    gate_rows = jnp.zeros((per_owner * exp_count, LANES), f32)
    for c in range(2):
        left = jnp.where((wheres[c] >= 0) & (wheres[c] // cap == hit_row), gates[c], 0.0).astype(bf16)
        right = jnp.where(wheres[c] % cap == hit_rank, 1.0, 0.0).astype(bf16)
        gate_rows += mm(left, right, TN)
    gate_rows = gate_rows.astype(bf16)
    for e in range(per_owner):
        gates_ref[e] = gate_rows[e * exp_count : (e + 1) * exp_count, :cap]
    copies.append(pltpu.make_async_copy(gates_ref, gates_hbm, sems.at[len(copies)]))
    copies[-1].start()
    at = 0
    for part, size in zip(groups, sizes):
        for start, stop in pieces(0, size):
            wide = jnp.concatenate([g[:, start:stop] for g in part], axis=0).astype(f32)
            normed = (wide * factor * gain_ref[:, at + start : at + stop]).astype(bf16)
            out = mm(chosen, normed, TN).astype(bf16)
            window = (slice(None), slice(None), slice(None), slice(at + start, at + stop))
            rows_ref[window] = out.reshape(per_owner, exp_count, cap, stop - start)
            copies.append(pltpu.make_async_copy(rows_ref.at[window], rows_hbm.at[window], sems.at[len(copies)]))
            copies[-1].start()
        at += size
    for copy in copies:
        copy.wait()


def swap(block, axis, mask):
    return lax.ppermute(block, axis, [(i, i ^ mask) for i in range(lax.axis_size(axis))])


def call(kernel, out, *args, specs=None, out_specs=None, scratch=(), flops=0, moved=0, limit=16 * MIB):
    single = not isinstance(out, (tuple, list))
    specs = specs or [VMEM] * len(args)
    args = [pltpu.with_memory_space_constraint(a, pltpu.HBM) if s is HBM else a for a, s in zip(args, specs, strict=True)]
    return pl.pallas_call(
        kernel,
        out_shape=out,
        in_specs=specs,
        out_specs=out_specs or (VMEM if single else (VMEM,) * len(out)),
        scratch_shapes=scratch,
        compiler_params=pltpu.CompilerParams(vmem_limit_bytes=limit),
        cost_estimate=pl.CostEstimate(flops=flops, bytes_accessed=moved, transcendentals=0),
    )(*args)


def on_device(queries, keys_in, values, decay_rate, out_weight, residual, norm_gain, router, expert_ids):
    q, k, v, decay, weight = queries[0], keys_in[0], values[0], decay_rate[0], out_weight[0]
    ids = jnp.swapaxes(expert_ids[0], 0, 1)
    router_t = jnp.swapaxes(router[0], 0, 1)
    length, heads = q.shape[0], decay.shape[0]
    dh = q.shape[1] // heads
    width = weight.shape[1]
    tokens = residual.shape[1]
    exp_count, ctx_count = lax.axis_size("exp"), lax.axis_size("ctx")
    exp_bits, ctx_bits = exp_count.bit_length() - 1, ctx_count.bit_length() - 1
    per_owner = router.shape[2] // exp_count
    shape = jax.ShapeDtypeStruct

    msg_shape = shape((heads * dh + pad_rows(heads), dh), bf16)
    part = pltpu.VMEM((length, heads * dh), bf16)
    small = pltpu.VMEM(decay.shape, f32)
    dma = pltpu.SemaphoreType.DMA
    msg = call(state_kernel, msg_shape, k, v, decay, specs=[HBM] * 3, scratch=[part, part, small, dma((3,))])
    got = []
    for bit in range(ctx_bits):
        got.append(swap(msg, "ctx", (2 << bit) - 1))
        if bit < ctx_bits - 1:
            msg = call(functools.partial(join_kernel, heads, bit), msg_shape, msg, got[-1])
    inside, slots, weight_near, q_near, growth = call(
        inside_kernel,
        (
            shape((length, heads * dh), f32),
            shape((tokens, LANES), jnp.int32),
            shape(weight.shape, bf16),
            shape(q.shape, bf16),
            shape((length, LANES), f32),
        ),
        q, k, v, decay, ids, weight,
        specs=[HBM] * 6,
        scratch=[part, part, small, pltpu.VMEM(ids.shape, jnp.int32), dma((6,))],
        moved=weight.size * 2,
    )
    base, scale = call(
        functools.partial(base_kernel, heads),
        (shape((length, heads * dh), f32), shape((length, LANES), f32)),
        q_near, inside, growth, *got[:-1],
    )
    order = [sum(((i >> b) & 1) << (exp_bits - 1 - b) for b in range(exp_bits)) for i in range(exp_count)]
    cuts = [width * i // PARTS // LANES * LANES for i in range(PARTS + 1)]
    sections = lax.axis_size("section")
    top = exp_count // 2

    def relay(block):
        return lax.ppermute(block, "section", [(i, (i + 1) % sections) for i in range(sections)])

    mixed, groups = None, []
    for start, stop in zip(cuts, cuts[1:]):
        first = mixed is None
        size = stop - start
        extra = LANES if first else 0
        halves = (shape((length // 2, size), bf16), shape((length // 2, size + extra), bf16))
        cost = 2 * length * heads * dh * size
        if first:
            mixed, keep, send = call(
                functools.partial(mix_kernel, heads, order, stop),
                (shape((length, heads * dh), bf16), *halves),
                q_near, base, scale, got[-1], weight_near, slots,
                scratch=[part],
                flops=cost,
            )
        else:
            keep, send = call(functools.partial(project_kernel, start, stop), halves, mixed, weight_near, flops=cost)
        for bit in range(exp_bits - 2):
            rest = keep.shape[0] // 2
            send, keep = call(
                functools.partial(halve_kernel, bit, tokens, first),
                (shape((rest, size + extra), bf16), shape((rest, size), f32)),
                keep, send, swap(send, "exp", 1 << bit),
            )
        own = call(
            functools.partial(carry_kernel, exp_bits - 2, start, first),
            shape((2 * tokens, size + extra), bf16),
            keep, send, swap(send, "exp", top // 2), residual[0],
        )
        whole = shape((2 * tokens, size), bf16)
        if first:
            other = swap(own, "exp", top)
            tagged = (own, other)
            block = relay(call(combine_kernel, whole, own, other))
        else:
            own = relay(own)
            block = call(combine_kernel, whole, own, swap(own, "exp", top))
        groups.append([block])
        for index in range(1, top):
            groups[-1].append(swap(groups[-1][index & (index - 1)], "exp", index & -index))
    rows_shape = (per_owner, exp_count, CAP, width)
    count = sum(len(pieces(start, stop)) for start, stop in zip(cuts, cuts[1:]))
    all_tokens, experts = exp_count * tokens, per_owner * exp_count
    facts = call(
        functools.partial(facts_kernel, exp_count, experts, tokens),
        (shape((all_tokens, per_owner * exp_count * CAP), bf16), shape((all_tokens, LANES), jnp.int32)),
        *tagged,
    )
    sums = call(
        functools.partial(ahead_kernel, top),
        (shape((all_tokens, LANES), f32), shape((all_tokens, experts), f32)),
        *groups[0], norm_gain, router_t,
    )
    rows, gates = call(
        functools.partial(place_kernel, top, PARTS),
        (shape(rows_shape, bf16), shape((per_owner, exp_count, CAP), bf16)),
        *[g for part_groups in groups for g in part_groups], *facts, *sums, norm_gain, router_t,
        out_specs=(HBM, HBM),
        scratch=[pltpu.VMEM(rows_shape, bf16), pltpu.VMEM(rows_shape[:-1], bf16), dma((count + 1,))],
    )
    return rows[None, None], gates[None, None]


def solution(mesh):
    placed = (
        P("section", "ctx", "exp"),
        P("section", "ctx", "exp"),
        P("section", "ctx", "exp"),
        P("section", "exp", "ctx"),
        P("section", "exp", None),
        P("section", ("ctx", "exp"), None),
        P("section", None),
        P("section", None, None),
        P("section", ("ctx", "exp"), None),
    )
    return jax.shard_map(
        on_device,
        mesh=mesh,
        in_specs=placed,
        out_specs=(
            P("section", "ctx", "exp", None, None, None),
            P("section", "ctx", "exp", None, None),
        ),
        check_vma=False,
    )
```

```python
import functools

import jax
import jax.numpy as jnp
from jax import lax
from jax.experimental import pallas as pl
from jax.experimental.pallas import tpu as pltpu
from jax.sharding import PartitionSpec as P

CAP = 4
EPSILON = 1e-05
LANES = 128
ROWS = 16
MIB = 1 << 20
PARTS = 2

VMEM = pl.BlockSpec(memory_space=pltpu.VMEM)
HBM = pl.BlockSpec(memory_space=pltpu.HBM)
bf16 = jnp.bfloat16
f32 = jnp.float32


def iota(shape, dim):
    return lax.broadcasted_iota(jnp.int32, shape, dim)


def mm(a, b, dims):
    return lax.dot_general(a, b, (dims, ((), ())), preferred_element_type=f32)


NN = ((1,), (0,))
NT = ((1,), (1,))
TN = ((0,), (0,))


def to_column(row):
    n = row.shape[1]
    square = jnp.broadcast_to(row, (n, n))
    return jnp.sum(jnp.where(iota((n, n), 0) == iota((n, n), 1), square, jnp.zeros_like(square)), axis=1, keepdims=True)


def cumulative(row):
    n = row.shape[1]
    at, of = iota((n, n), 0), iota((n, n), 1)
    column = -jnp.sum(jnp.where(of <= at, jnp.broadcast_to(row, (n, n)), 0.0), axis=1, keepdims=True)
    along = jnp.sum(jnp.where(at == of, jnp.broadcast_to(column, (n, n)), 0.0), axis=0, keepdims=True)
    return column, along


def pad_rows(heads):
    return -(-3 * heads // ROWS) * ROWS


def put_log(ref, base, heads, h, value):
    for part in range(3):
        piece = value.astype(bf16)
        ref[base + part * heads + h : base + part * heads + h + 1, :] = piece
        value = value - piece.astype(f32)


def get_log(block, heads, h):
    return block[h : h + 1] + block[heads + h : heads + h + 1] + block[2 * heads + h : 2 * heads + h + 1]


def fetch(sources, places, sems):
    copies = [pltpu.make_async_copy(s, p, sems.at[i]) for i, (s, p) in enumerate(zip(sources, places, strict=True))]
    for copy in copies:
        copy.start()
    return copies


def state_kernel(k_hbm, v_hbm, decay_hbm, msg_ref, k_ref, v_ref, decay_ref, sems):
    copies = fetch((decay_hbm, k_hbm, v_hbm), (decay_ref, k_ref, v_ref), sems)
    heads = decay_ref.shape[0]
    dh = k_ref.shape[1] // heads
    base = heads * dh
    msg_ref[base:, :] = jnp.zeros((msg_ref.shape[0] - base, dh), bf16)
    copies[0].wait()
    tails = []
    for h in range(heads):
        column, along = cumulative(decay_ref[h : h + 1, :])
        last = along[:, -1:]
        tails.append(jnp.exp(last - column))
        put_log(msg_ref, base, heads, h, jnp.broadcast_to(last, (1, dh)))
    copies[1].wait()
    copies[2].wait()
    for h in range(heads):
        keyed = (k_ref[:, h * dh : (h + 1) * dh].astype(f32) * tails[h]).astype(bf16)
        msg_ref[h * dh : (h + 1) * dh, :] = mm(keyed, v_ref[:, h * dh : (h + 1) * dh], TN).astype(bf16)


def joined(heads, bit, own_ref, got_ref):
    dh = own_ref.shape[1]
    base = heads * dh
    upper = (lax.axis_index("ctx") >> bit) & 1
    is_upper = jnp.full((1, dh), upper, jnp.int32) == 1
    own_block = own_ref[base:, :].astype(f32)
    got_block = got_ref[base:, :].astype(f32)
    for h in range(heads):
        own_log, got_log = get_log(own_block, heads, h), get_log(got_block, heads, h)
        own = own_ref[h * dh : (h + 1) * dh, :].astype(f32)
        got = got_ref[h * dh : (h + 1) * dh, :].astype(f32)
        scale_own = jnp.where(is_upper, 1.0, jnp.exp(got_log))
        scale_got = jnp.where(is_upper, jnp.exp(own_log), 1.0)
        yield scale_own * own + scale_got * got, own_log + got_log


def join_kernel(heads, bit, own_ref, got_ref, msg_ref):
    dh = own_ref.shape[1]
    base = heads * dh
    with_logs = msg_ref.shape[0] > base
    if with_logs:
        msg_ref[base:, :] = jnp.zeros((msg_ref.shape[0] - base, dh), bf16)
    for h, (state, log) in enumerate(joined(heads, bit, own_ref, got_ref)):
        msg_ref[h * dh : (h + 1) * dh, :] = state.astype(bf16)
        if with_logs:
            put_log(msg_ref, base, heads, h, log)


def split_mm(a, state):
    high = state.astype(bf16)
    low = (state - high.astype(f32)).astype(bf16)
    return mm(a, high, NN) + mm(a, low, NN)


def inside_kernel(q_hbm, k_hbm, v_hbm, decay_hbm, ids_hbm, weight_hbm, inside_ref, slots_ref, weight_ref, q_ref, growth_ref,
                  k_ref, v_ref, decay_ref, ids_ref, sems):
    copies = fetch(
        (decay_hbm, ids_hbm, q_hbm, k_hbm, v_hbm, weight_hbm), (decay_ref, ids_ref, q_ref, k_ref, v_ref, weight_ref), sems
    )
    for copy in copies[:-1]:
        copy.wait()
    heads = decay_ref.shape[0]
    length = q_ref.shape[0]
    dh = q_ref.shape[1] // heads
    causal = iota((length, length), 0) >= iota((length, length), 1)
    lane = iota((length, LANES), 1)
    growth = jnp.zeros((length, LANES), f32)
    for h in range(heads):
        cols = slice(h * dh, (h + 1) * dh)
        column, along = cumulative(decay_ref[h : h + 1, :])
        scores = mm(q_ref[:, cols], k_ref[:, cols], NT)
        weights = jnp.where(causal, scores * jnp.exp(jnp.minimum(column - along, 0.0)), 0.0).astype(bf16)
        inside_ref[:, cols] = mm(weights, v_ref[:, cols], NN)
        growth = jnp.where(lane == h, jnp.exp(column), growth)
    growth_ref[...] = growth
    n = ids_ref.shape[1]
    earlier = iota((n, n), 1) < iota((n, n), 0)
    rows = [ids_ref[c : c + 1, :] for c in range(2)]
    places = []
    for c in range(2):
        mine = to_column(rows[c])
        rank = jnp.zeros((n, 1), jnp.int32)
        for other in range(2):
            rank += jnp.sum(jnp.where(earlier & (mine == rows[other]), 1, 0), axis=1, keepdims=True)
        places.append(mine * CAP + rank)
    lane = iota((n, LANES), 1)
    slots_ref[...] = jnp.where(lane == 0, places[0], jnp.where(lane == 1, places[1], 0))
    copies[-1].wait()


def base_kernel(heads, q_ref, inside_ref, growth_ref, *rest):
    got_refs, (base_ref, scale_ref) = rest[:-2], rest[-2:]
    bits = len(got_refs)
    dh = q_ref.shape[1] // heads
    base = heads * dh
    place = lax.axis_index("ctx")
    blocks = [ref[base:, :].astype(f32) for ref in got_refs]
    uppers = [jnp.full((1, dh), (place >> bit) & 1, jnp.int32) == 1 for bit in range(bits + 1)]
    lane = iota(scale_ref.shape, 1)
    scale = jnp.zeros(scale_ref.shape, f32)
    for h in range(heads):
        cols = slice(h * dh, (h + 1) * dh)
        incoming = jnp.zeros((dh, dh), f32)
        before = jnp.zeros((1, dh), f32)
        for bit in range(bits):
            got = got_refs[bit][h * dh : (h + 1) * dh, :].astype(f32)
            incoming += jnp.where(uppers[bit], jnp.exp(before), 0.0) * got
            before += jnp.where(uppers[bit], get_log(blocks[bit], heads, h), 0.0)
        growth = growth_ref[:, h : h + 1]
        base_ref[:, cols] = inside_ref[:, cols] + growth * split_mm(q_ref[:, cols], incoming)
        factor = jnp.where(uppers[bits], jnp.exp(before), 0.0)
        scale = jnp.where(lane == h, growth * factor[:, :1], scale)
    scale_ref[...] = scale


def mix_kernel(heads, order, stop, q_ref, base_ref, scale_ref, got_ref, weight_ref, slots_ref, mixed_ref, keep_ref, send_ref, attended):
    dh = base_ref.shape[1] // heads
    me = lax.axis_index("exp")
    for h in range(heads):
        cols = slice(h * dh, (h + 1) * dh)
        outside = mm(q_ref[:, cols], got_ref[h * dh : (h + 1) * dh, :], NN)
        attended[:, cols] = (base_ref[:, cols] + scale_ref[:, h : h + 1] * outside).astype(bf16)
    share = base_ref.shape[0] // len(order)
    for i, k in enumerate(order):
        mixed_ref[i * share : (i + 1) * share, :] = attended[pl.ds(pl.multiple_of((me ^ k) * share, share), share), :]
    project_kernel(0, stop, mixed_ref, weight_ref, keep_ref, send_ref)
    put_lanes(send_ref, slots_ref[...].astype(f32))


def project_kernel(start, stop, mixed_ref, weight_ref, keep_ref, send_ref):
    half = mixed_ref.shape[0] // 2
    mixed = mixed_ref[...]
    for at, to in pieces(start, stop):
        part = mm(mixed, weight_ref[:, at:to], NN).astype(bf16)
        keep_ref[:, at - start : to - start] = part[:half]
        send_ref[:, at - start : to - start] = part[half:]


def pieces(start, stop, step=1024):
    return [(at, min(at + step, stop)) for at in range(start, stop, step)]


def put_lanes(ref, lanes):
    tokens = lanes.shape[0]
    ref[:tokens, -LANES:] = lanes.astype(bf16)
    if ref.shape[0] > tokens:
        ref[tokens:, -LANES:] = jnp.zeros((ref.shape[0] - tokens, LANES), bf16)


def widen_lanes(bit, tokens, sent_ref, got_ref):
    own, got = sent_ref[:tokens, -LANES:].astype(f32), got_ref[:tokens, -LANES:].astype(f32)
    filled = 2 << bit
    return jnp.where(iota(own.shape, 1) < filled, own, jnp.roll(got, filled, axis=1))


def halve_kernel(bit, tokens, tagged, keep_ref, sent_ref, got_ref, send_ref, own_ref):
    half, width = own_ref.shape
    own_ref[...] = keep_ref[:half, :].astype(f32) + got_ref[:half, :width].astype(f32)
    send_ref[:, :width] = (keep_ref[half:, :].astype(f32) + got_ref[half:, :width].astype(f32)).astype(bf16)
    if tagged:
        put_lanes(send_ref, widen_lanes(bit, tokens, sent_ref, got_ref))


def carry_kernel(bit, start, tagged, keep_ref, sent_ref, got_ref, residual_ref, out_ref):
    tokens = residual_ref.shape[0]
    width = keep_ref.shape[1]
    total = keep_ref[...].astype(f32) + got_ref[:, :width].astype(f32)
    own = total[:tokens] + residual_ref[:, start : start + width].astype(f32)
    out_ref[:tokens, :width] = own.astype(bf16)
    out_ref[tokens:, :width] = total[tokens:].astype(bf16)
    if tagged:
        put_lanes(out_ref, widen_lanes(bit, tokens, sent_ref, got_ref))


def combine_kernel(own_ref, got_ref, out_ref):
    rows, width = out_ref.shape
    half = rows // 2
    out_ref[:half, :] = (own_ref[:half, :width].astype(f32) + got_ref[half:, :width].astype(f32)).astype(bf16)
    out_ref[half:, :] = (own_ref[half:, :width].astype(f32) + got_ref[:half, :width].astype(f32)).astype(bf16)


def sums(refs, gain, router):
    square, logits, start = 0.0, 0.0, 0
    for ref in refs:
        for at, to in pieces(0, ref.shape[1]):
            wide = ref[:, at:to].astype(f32)
            square += jnp.sum(wide * wide, axis=1, keepdims=True)
            cols = slice(start + at, start + to)
            logits += mm((wide * gain[:, cols]).astype(bf16), router[:, cols], NT)
        start += ref.shape[1]
    return square, logits


def facts_kernel(exp_count, experts, tokens, own_ref, got_ref, chosen_ref, target_ref):
    per_owner = experts // exp_count
    top = exp_count // 2
    me = lax.axis_index("exp")
    lanes = [ref[:tokens, -LANES:].astype(f32).astype(jnp.int32) for ref in (own_ref, got_ref)]
    places, wheres, named = [[], []], [[], []], [[], []]
    for j in range(top):
        for side in range(2):
            sender = me ^ (j + side * top)
            for c in range(2):
                slot = lanes[side][:, 2 * j + c : 2 * j + c + 1]
                place = slot - me * (per_owner * CAP)
                mine = (place >= 0) & (place < per_owner * CAP)
                places[c].append(jnp.where(mine, side * (per_owner * CAP) + place, -1))
                wheres[c].append(jnp.where(mine, (place // CAP * exp_count + sender) * CAP + place % CAP, -1))
                named[c].append(slot // CAP)
    places, wheres, named = [[jnp.concatenate(column, axis=0) for column in pair] for pair in (places, wheres, named)]
    slot = iota(chosen_ref.shape, 1)
    chosen_ref[...] = ((places[0] == slot) | (places[1] == slot)).astype(f32).astype(bf16)
    lane = iota(target_ref.shape, 1)
    target = jnp.zeros(target_ref.shape, jnp.int32)
    for i, column in enumerate(wheres + named):
        target = jnp.where(lane == i, column, target)
    target_ref[...] = target


def place_rows(block, parts, factor, chosen, gain, top, held, rows_hbm, sems):
    me = lax.axis_index("exp")
    _, per_owner, cap, _ = held.shape
    copies, start = [], 0
    for ref in parts:
        for at, to in pieces(0, ref.shape[1]):
            cols = slice(start + at, start + to)
            normed = (ref[:, at:to].astype(f32) * factor * gain[:, cols]).astype(bf16)
            held[:, :, :, cols] = mm(chosen, normed, TN).astype(bf16).reshape(2, per_owner, cap, to - at)
            for side in range(2):
                place = rows_hbm.at[:, me ^ (block + side * top), :, cols]
                copies.append(pltpu.make_async_copy(held.at[side, :, :, cols], place, sems.at[len(copies)]))
                copies[-1].start()
        start += ref.shape[1]
    return copies


def gates_of(logits, target, rows, cap):
    wheres, named = [target[:, c : c + 1] for c in range(2)], [target[:, 2 + c : 3 + c] for c in range(2)]
    expert = iota(logits.shape, 1)
    toward = jnp.where(named[1] == expert, 1.0, 0.0) - jnp.where(named[0] == expert, 1.0, 0.0)
    first = 1.0 / (1.0 + jnp.exp(jnp.sum(toward * logits, axis=1, keepdims=True)))
    gates = [first, 1.0 - first]
    total = logits.shape[0]
    hit_row, hit_rank = iota((total, rows), 1), iota((total, LANES), 1)
    out = jnp.zeros((rows, LANES), f32)
    for c in range(2):
        left = jnp.where((wheres[c] >= 0) & (wheres[c] // cap == hit_row), gates[c], 0.0).astype(bf16)
        right = jnp.where(wheres[c] % cap == hit_rank, 1.0, 0.0).astype(bf16)
        out += mm(left, right, TN)
    return out


def near_kernel(parts, top, *refs):
    own, refs = refs[:parts], refs[parts:]
    early, refs = refs[: -10], refs[-10:]
    chosen_ref, target_ref, gain_ref, router_ref, rows_hbm, gates_ref, square_ref, logits_ref, held, sems = refs
    width = gain_ref.shape[1]
    tokens = own[0].shape[0]
    square, logits = sums(own, gain_ref, router_ref)
    factor = lax.rsqrt(square * (1.0 / width) + EPSILON)
    copies = place_rows(0, own, factor, chosen_ref[:tokens, :], gain_ref, top, held, rows_hbm, sems)
    gates_ref[...] = gates_of(logits * factor, target_ref[:tokens, :], gates_ref.shape[0], held.shape[2])
    for i in range(top - 1):
        square, logits = sums(early[i * (parts - 1) : (i + 1) * (parts - 1)], gain_ref, router_ref)
        square_ref[i * tokens : (i + 1) * tokens, :] = jnp.broadcast_to(square, (tokens, square_ref.shape[1]))
        logits_ref[i * tokens : (i + 1) * tokens, :] = logits
    for copy in copies:
        copy.wait()


def far_kernel(parts, top, *refs):
    late, refs = refs[: parts * (top - 1)], refs[parts * (top - 1) :]
    chosen_ref, target_ref, gain_ref, router_ref, near_gates, square_ref, logits_ref, _, rows_hbm, gates_hbm, held, gates_ref, sems, last = refs
    width = gain_ref.shape[1]
    tokens = late[0].shape[0]
    before = width - late[parts - 1].shape[1]
    gates = near_gates[...]
    copies = []
    for i in range(top - 1):
        block = late[i * parts : (i + 1) * parts]
        rows = slice(i * tokens, (i + 1) * tokens)
        token_rows = slice((i + 1) * tokens, (i + 2) * tokens)
        square, logits = sums(block[-1:], gain_ref.at[:, before:], router_ref.at[:, before:])
        factor = lax.rsqrt((square_ref[rows, :1] + square) * (1.0 / width) + EPSILON)
        copies += place_rows(
            i + 1, block, factor, chosen_ref[token_rows, :], gain_ref, top, held.at[i], rows_hbm, sems.at[i]
        )
        logits = (logits_ref[rows, :] + logits) * factor
        gates += gates_of(logits, target_ref[token_rows, :], gates.shape[0], held.shape[3])
    per_owner, exp_count, cap = gates_ref.shape
    gates = gates.astype(bf16)
    for e in range(per_owner):
        gates_ref[e] = gates[e * exp_count : (e + 1) * exp_count, :cap]
    copies.append(pltpu.make_async_copy(gates_ref, gates_hbm, last))
    copies[-1].start()
    for copy in copies:
        copy.wait()


def swap(block, axis, mask):
    return lax.ppermute(block, axis, [(i, i ^ mask) for i in range(lax.axis_size(axis))])


def call(kernel, out, *args, specs=None, out_specs=None, scratch=(), flops=0, moved=0, limit=16 * MIB, aliases=None):
    single = not isinstance(out, (tuple, list))
    specs = specs or [VMEM] * len(args)
    args = [pltpu.with_memory_space_constraint(a, pltpu.HBM) if s is HBM else a for a, s in zip(args, specs, strict=True)]
    return pl.pallas_call(
        kernel,
        out_shape=out,
        in_specs=specs,
        out_specs=out_specs or (VMEM if single else (VMEM,) * len(out)),
        scratch_shapes=scratch,
        input_output_aliases=aliases or {},
        compiler_params=pltpu.CompilerParams(vmem_limit_bytes=limit),
        cost_estimate=pl.CostEstimate(flops=flops, bytes_accessed=moved, transcendentals=0),
    )(*args)


def on_device(queries, keys_in, values, decay_rate, out_weight, residual, norm_gain, router, expert_ids):
    q, k, v, decay, weight = queries[0], keys_in[0], values[0], decay_rate[0], out_weight[0]
    ids = jnp.swapaxes(expert_ids[0], 0, 1)
    router_t = jnp.swapaxes(router[0], 0, 1)
    length, heads = q.shape[0], decay.shape[0]
    dh = q.shape[1] // heads
    width = weight.shape[1]
    tokens = residual.shape[1]
    exp_count, ctx_count = lax.axis_size("exp"), lax.axis_size("ctx")
    exp_bits, ctx_bits = exp_count.bit_length() - 1, ctx_count.bit_length() - 1
    per_owner = router.shape[2] // exp_count
    shape = jax.ShapeDtypeStruct

    msg_shape = shape((heads * dh + pad_rows(heads), dh), bf16)
    part = pltpu.VMEM((length, heads * dh), bf16)
    small = pltpu.VMEM(decay.shape, f32)
    dma = pltpu.SemaphoreType.DMA
    msg = call(state_kernel, msg_shape, k, v, decay, specs=[HBM] * 3, scratch=[part, part, small, dma((3,))])
    got = []
    for bit in range(ctx_bits):
        got.append(swap(msg, "ctx", (2 << bit) - 1))
        if bit < ctx_bits - 1:
            last_shape = shape((heads * dh, dh), bf16)
            out = msg_shape if bit < ctx_bits - 2 else last_shape
            msg = call(functools.partial(join_kernel, heads, bit), out, msg, got[-1])
    inside, slots, weight_near, q_near, growth = call(
        inside_kernel,
        (
            shape((length, heads * dh), f32),
            shape((tokens, LANES), jnp.int32),
            shape(weight.shape, bf16),
            shape(q.shape, bf16),
            shape((length, LANES), f32),
        ),
        q, k, v, decay, ids, weight,
        specs=[HBM] * 6,
        scratch=[part, part, small, pltpu.VMEM(ids.shape, jnp.int32), dma((6,))],
        moved=weight.size * 2,
    )
    base, scale = call(
        functools.partial(base_kernel, heads),
        (shape((length, heads * dh), f32), shape((length, LANES), f32)),
        q_near, inside, growth, *got[:-1],
    )
    order = [sum(((i >> b) & 1) << (exp_bits - 1 - b) for b in range(exp_bits)) for i in range(exp_count)]
    cuts = [width * i // PARTS // LANES * LANES for i in range(PARTS + 1)]
    sections = lax.axis_size("section")
    top = exp_count // 2

    def relay(block):
        return lax.ppermute(block, "section", [(i, (i + 1) % sections) for i in range(sections)])

    all_tokens, experts = exp_count * tokens, per_owner * exp_count
    mixed, groups = None, []
    for start, stop in zip(cuts, cuts[1:]):
        first = mixed is None
        size = stop - start
        extra = LANES if first else 0
        halves = (shape((length // 2, size), bf16), shape((length // 2, size + extra), bf16))
        cost = 2 * length * heads * dh * size
        if first:
            mixed, keep, send = call(
                functools.partial(mix_kernel, heads, order, stop),
                (shape((length, heads * dh), bf16), *halves),
                q_near, base, scale, got[-1], weight_near, slots,
                scratch=[part],
                flops=cost,
            )
        else:
            keep, send = call(functools.partial(project_kernel, start, stop), halves, mixed, weight_near, flops=cost)
        for bit in range(exp_bits - 2):
            rest = keep.shape[0] // 2
            send, keep = call(
                functools.partial(halve_kernel, bit, tokens, first),
                (shape((rest, size + extra), bf16), shape((rest, size), f32)),
                keep, send, swap(send, "exp", 1 << bit),
            )
        own = call(
            functools.partial(carry_kernel, exp_bits - 2, start, first),
            shape((2 * tokens, size + extra), bf16),
            keep, send, swap(send, "exp", top // 2), residual[0],
        )
        whole = shape((2 * tokens, size), bf16)
        if first:
            other = swap(own, "exp", top)
            facts = call(
                functools.partial(facts_kernel, exp_count, experts, tokens),
                (shape((all_tokens, 2 * per_owner * CAP), bf16), shape((all_tokens, LANES), jnp.int32)),
                own, other,
            )
            block = relay(call(combine_kernel, whole, own, other))
        else:
            own = relay(own)
            other, *facts = lax.optimization_barrier((swap(own, "exp", top), *facts))
            block = call(combine_kernel, whole, own, other)
        groups.append([block])
        for index in range(1, top):
            groups[-1].append(swap(groups[-1][index & (index - 1)], "exp", index & -index))
    rows_shape = (per_owner, exp_count, CAP, width)
    count = 2 * sum(len(pieces(0, part_groups[0].shape[1])) for part_groups in groups)
    late_tokens = all_tokens - 2 * tokens
    held = (2, per_owner, CAP, width)
    rows, *near = call(
        functools.partial(near_kernel, PARTS, top),
        (
            shape(rows_shape, bf16),
            shape((experts, LANES), f32),
            shape((late_tokens, LANES), f32),
            shape((late_tokens, experts), f32),
        ),
        *[part_groups[0] for part_groups in groups],
        *[part_groups[i] for i in range(1, top) for part_groups in groups[:-1]],
        *facts, norm_gain, router_t,
        out_specs=(HBM, VMEM, VMEM, VMEM),
        scratch=[pltpu.VMEM(held, bf16), dma((count,))],
    )
    rows, gates = call(
        functools.partial(far_kernel, PARTS, top),
        (shape(rows_shape, bf16), shape(rows_shape[:-1], bf16)),
        *[part_groups[i] for i in range(1, top) for part_groups in groups],
        *facts, norm_gain, router_t, *near, rows,
        specs=[VMEM] * (PARTS * (top - 1) + 7) + [HBM],
        out_specs=(HBM, HBM),
        scratch=[
            pltpu.VMEM((top - 1, *held), bf16),
            pltpu.VMEM(rows_shape[:-1], bf16),
            dma((top - 1, count)),
            dma,
        ],
        aliases={PARTS * (top - 1) + 7: 0},
    )
    return rows[None, None], gates[None, None]


def solution(mesh):
    placed = (
        P("section", "ctx", "exp"),
        P("section", "ctx", "exp"),
        P("section", "ctx", "exp"),
        P("section", "exp", "ctx"),
        P("section", "exp", None),
        P("section", ("ctx", "exp"), None),
        P("section", None),
        P("section", None, None),
        P("section", ("ctx", "exp"), None),
    )
    return jax.shard_map(
        on_device,
        mesh=mesh,
        in_specs=placed,
        out_specs=(
            P("section", "ctx", "exp", None, None, None),
            P("section", "ctx", "exp", None, None),
        ),
        check_vma=False,
    )
```

```python
import functools

import jax
import jax.numpy as jnp
from jax import lax
from jax.experimental import pallas as pl
from jax.experimental.pallas import tpu as pltpu
from jax.sharding import PartitionSpec as P

CAP = 4
EPSILON = 1e-05
LANES = 128
ROWS = 16
MIB = 1 << 20
PARTS = 2

VMEM = pl.BlockSpec(memory_space=pltpu.VMEM)
HBM = pl.BlockSpec(memory_space=pltpu.HBM)
bf16 = jnp.bfloat16
f32 = jnp.float32


def iota(shape, dim):
    return lax.broadcasted_iota(jnp.int32, shape, dim)


def mm(a, b, dims):
    return lax.dot_general(a, b, (dims, ((), ())), preferred_element_type=f32)


NN = ((1,), (0,))
NT = ((1,), (1,))
TN = ((0,), (0,))


def to_column(row):
    n = row.shape[1]
    square = jnp.broadcast_to(row, (n, n))
    return jnp.sum(jnp.where(iota((n, n), 0) == iota((n, n), 1), square, jnp.zeros_like(square)), axis=1, keepdims=True)


def cumulative(row):
    n = row.shape[1]
    at, of = iota((n, n), 0), iota((n, n), 1)
    column = -jnp.sum(jnp.where(of <= at, jnp.broadcast_to(row, (n, n)), 0.0), axis=1, keepdims=True)
    along = jnp.sum(jnp.where(at == of, jnp.broadcast_to(column, (n, n)), 0.0), axis=0, keepdims=True)
    return column, along


def pad_rows(heads):
    return -(-3 * heads // ROWS) * ROWS


def log_rows(values):
    heads, shape = len(values), (pad_rows(len(values)), values[0].shape[1])
    row, out = iota(shape, 0), jnp.zeros(shape, f32)
    for h, value in enumerate(values):
        for part in range(3):
            piece = value.astype(bf16).astype(f32)
            out = jnp.where(row == part * heads + h, piece, out)
            value = value - piece
    return out.astype(bf16)


def get_log(block, heads, h):
    return block[h : h + 1] + block[heads + h : heads + h + 1] + block[2 * heads + h : 2 * heads + h + 1]


def fetch(sources, places, sems):
    copies = [pltpu.make_async_copy(s, p, sems.at[i]) for i, (s, p) in enumerate(zip(sources, places, strict=True))]
    for copy in copies:
        copy.start()
    return copies


def state_kernel(k_hbm, v_hbm, decay_hbm, msg_ref, k_ref, v_ref, decay_ref, sems):
    copies = fetch((decay_hbm, k_hbm, v_hbm), (decay_ref, k_ref, v_ref), sems)
    heads = decay_ref.shape[0]
    dh = k_ref.shape[1] // heads
    base = heads * dh
    copies[0].wait()
    tails, lasts = [], []
    for h in range(heads):
        column, along = cumulative(decay_ref[h : h + 1, :])
        last = along[:, -1:]
        tails.append(jnp.exp(last - column))
        lasts.append(jnp.broadcast_to(last, (1, dh)))
    msg_ref[base:, :] = log_rows(lasts)
    copies[1].wait()
    copies[2].wait()
    for h in range(heads):
        keyed = (k_ref[:, h * dh : (h + 1) * dh].astype(f32) * tails[h]).astype(bf16)
        msg_ref[h * dh : (h + 1) * dh, :] = mm(keyed, v_ref[:, h * dh : (h + 1) * dh], TN).astype(bf16)


def joined(heads, bit, own_ref, got_ref):
    dh = own_ref.shape[1]
    base = heads * dh
    upper = (lax.axis_index("ctx") >> bit) & 1
    is_upper = jnp.full((1, dh), upper, jnp.int32) == 1
    own_block = own_ref[base:, :].astype(f32)
    got_block = got_ref[base:, :].astype(f32)
    for h in range(heads):
        own_log, got_log = get_log(own_block, heads, h), get_log(got_block, heads, h)
        own = own_ref[h * dh : (h + 1) * dh, :].astype(f32)
        got = got_ref[h * dh : (h + 1) * dh, :].astype(f32)
        scale_own = jnp.where(is_upper, 1.0, jnp.exp(got_log))
        scale_got = jnp.where(is_upper, jnp.exp(own_log), 1.0)
        yield scale_own * own + scale_got * got, own_log + got_log


def join_kernel(heads, bit, own_ref, got_ref, msg_ref):
    dh = own_ref.shape[1]
    logs = []
    for h, (state, log) in enumerate(joined(heads, bit, own_ref, got_ref)):
        msg_ref[h * dh : (h + 1) * dh, :] = state.astype(bf16)
        logs.append(log)
    if msg_ref.shape[0] > heads * dh:
        msg_ref[heads * dh :, :] = log_rows(logs)


def split_mm(a, state):
    high = state.astype(bf16)
    low = (state - high.astype(f32)).astype(bf16)
    return mm(a, high, NN) + mm(a, low, NN)


def inside_kernel(q_hbm, k_hbm, v_hbm, decay_hbm, ids_hbm, weight_hbm, inside_ref, slots_ref, weight_ref, q_ref, growth_ref,
                  k_ref, v_ref, decay_ref, ids_ref, sems):
    copies = fetch(
        (decay_hbm, ids_hbm, q_hbm, k_hbm, v_hbm, weight_hbm), (decay_ref, ids_ref, q_ref, k_ref, v_ref, weight_ref), sems
    )
    for copy in copies[:-1]:
        copy.wait()
    heads = decay_ref.shape[0]
    length = q_ref.shape[0]
    dh = q_ref.shape[1] // heads
    causal = iota((length, length), 0) >= iota((length, length), 1)
    lane = iota((length, LANES), 1)
    growth = jnp.zeros((length, LANES), f32)
    for h in range(heads):
        cols = slice(h * dh, (h + 1) * dh)
        column, along = cumulative(decay_ref[h : h + 1, :])
        scores = mm(q_ref[:, cols], k_ref[:, cols], NT)
        weights = jnp.where(causal, scores * jnp.exp(jnp.minimum(column - along, 0.0)), 0.0).astype(bf16)
        inside_ref[:, cols] = mm(weights, v_ref[:, cols], NN)
        growth = jnp.where(lane == h, jnp.exp(column), growth)
    growth_ref[...] = growth
    n = ids_ref.shape[1]
    earlier = iota((n, n), 1) < iota((n, n), 0)
    rows = [ids_ref[c : c + 1, :] for c in range(2)]
    places = []
    for c in range(2):
        mine = to_column(rows[c])
        rank = jnp.zeros((n, 1), jnp.int32)
        for other in range(2):
            rank += jnp.sum(jnp.where(earlier & (mine == rows[other]), 1, 0), axis=1, keepdims=True)
        places.append(mine * CAP + rank)
    lane = iota((n, LANES), 1)
    slots_ref[...] = jnp.where(lane == 0, places[0], jnp.where(lane == 1, places[1], 0))
    copies[-1].wait()


def base_kernel(heads, q_ref, inside_ref, growth_ref, *rest):
    got_refs, (base_ref, scale_ref) = rest[:-2], rest[-2:]
    bits = len(got_refs)
    dh = q_ref.shape[1] // heads
    base = heads * dh
    place = lax.axis_index("ctx")
    blocks = [ref[base:, :].astype(f32) for ref in got_refs]
    uppers = [jnp.full((1, dh), (place >> bit) & 1, jnp.int32) == 1 for bit in range(bits + 1)]
    lane = iota(scale_ref.shape, 1)
    scale = jnp.zeros(scale_ref.shape, f32)
    for h in range(heads):
        cols = slice(h * dh, (h + 1) * dh)
        incoming = jnp.zeros((dh, dh), f32)
        before = jnp.zeros((1, dh), f32)
        for bit in range(bits):
            got = got_refs[bit][h * dh : (h + 1) * dh, :].astype(f32)
            incoming += jnp.where(uppers[bit], jnp.exp(before), 0.0) * got
            before += jnp.where(uppers[bit], get_log(blocks[bit], heads, h), 0.0)
        growth = growth_ref[:, h : h + 1]
        base_ref[:, cols] = inside_ref[:, cols] + growth * split_mm(q_ref[:, cols], incoming)
        factor = jnp.where(uppers[bits], jnp.exp(before), 0.0)
        scale = jnp.where(lane == h, growth * factor[:, :1], scale)
    scale_ref[...] = scale


def mix_kernel(heads, order, stop, q_ref, base_ref, scale_ref, got_ref, weight_ref, slots_ref, mixed_ref, keep_ref, send_ref, attended):
    dh = base_ref.shape[1] // heads
    me = lax.axis_index("exp")
    for h in range(heads):
        cols = slice(h * dh, (h + 1) * dh)
        outside = mm(q_ref[:, cols], got_ref[h * dh : (h + 1) * dh, :], NN)
        attended[:, cols] = (base_ref[:, cols] + scale_ref[:, h : h + 1] * outside).astype(bf16)
    share = base_ref.shape[0] // len(order)
    for i, k in enumerate(order):
        mixed_ref[i * share : (i + 1) * share, :] = attended[pl.ds(pl.multiple_of((me ^ k) * share, share), share), :]
    project_kernel(0, stop, mixed_ref, weight_ref, keep_ref, send_ref)
    put_lanes(send_ref, slots_ref[...].astype(f32))


def project_kernel(start, stop, mixed_ref, weight_ref, keep_ref, send_ref):
    half = mixed_ref.shape[0] // 2
    mixed = mixed_ref[...]
    for at, to in pieces(start, stop):
        part = mm(mixed, weight_ref[:, at:to], NN).astype(bf16)
        keep_ref[:, at - start : to - start] = part[:half]
        send_ref[:, at - start : to - start] = part[half:]


def pieces(start, stop, step=3072):
    return [(at, min(at + step, stop)) for at in range(start, stop, step)]


def put_lanes(ref, lanes):
    tokens = lanes.shape[0]
    ref[:tokens, -LANES:] = lanes.astype(bf16)
    if ref.shape[0] > tokens:
        ref[tokens:, -LANES:] = jnp.zeros((ref.shape[0] - tokens, LANES), bf16)


def widen_lanes(bit, tokens, sent_ref, got_ref):
    own, got = sent_ref[:tokens, -LANES:].astype(f32), got_ref[:tokens, -LANES:].astype(f32)
    filled = 2 << bit
    return jnp.where(iota(own.shape, 1) < filled, own, jnp.roll(got, filled, axis=1))


def halve_kernel(bit, tokens, tagged, keep_ref, sent_ref, got_ref, send_ref, own_ref):
    half, width = own_ref.shape
    own_ref[...] = keep_ref[:half, :].astype(f32) + got_ref[:half, :width].astype(f32)
    send_ref[:, :width] = (keep_ref[half:, :].astype(f32) + got_ref[half:, :width].astype(f32)).astype(bf16)
    if tagged:
        put_lanes(send_ref, widen_lanes(bit, tokens, sent_ref, got_ref))


def carry_kernel(bit, start, tagged, keep_ref, sent_ref, got_ref, residual_ref, out_ref):
    tokens = residual_ref.shape[0]
    width = keep_ref.shape[1]
    total = keep_ref[...].astype(f32) + got_ref[:, :width].astype(f32)
    own = total[:tokens] + residual_ref[:, start : start + width].astype(f32)
    out_ref[:tokens, :width] = own.astype(bf16)
    out_ref[tokens:, :width] = total[tokens:].astype(bf16)
    if tagged:
        put_lanes(out_ref, widen_lanes(bit, tokens, sent_ref, got_ref))


def combine_kernel(own_ref, got_ref, out_ref):
    rows, width = out_ref.shape
    half = rows // 2
    out_ref[:half, :] = (own_ref[:half, :width].astype(f32) + got_ref[half:, :width].astype(f32)).astype(bf16)
    out_ref[half:, :] = (own_ref[half:, :width].astype(f32) + got_ref[:half, :width].astype(f32)).astype(bf16)


def sums(refs, gain, router):
    square, logits, start = 0.0, 0.0, 0
    for ref in refs:
        for at, to in pieces(0, ref.shape[1]):
            wide = ref[:, at:to].astype(f32)
            square += jnp.sum(wide * wide, axis=1, keepdims=True)
            cols = slice(start + at, start + to)
            logits += mm((wide * gain[:, cols]).astype(bf16), router[:, cols], NT)
        start += ref.shape[1]
    return square, logits


def facts_kernel(exp_count, experts, tokens, own_ref, got_ref, chosen_ref, target_ref):
    per_owner = experts // exp_count
    top = exp_count // 2
    me = lax.axis_index("exp")
    lanes = [ref[:tokens, -LANES:].astype(f32).astype(jnp.int32) for ref in (own_ref, got_ref)]
    places, wheres, named = [[], []], [[], []], [[], []]
    for j in range(top):
        for side in range(2):
            sender = me ^ (j + side * top)
            for c in range(2):
                slot = lanes[side][:, 2 * j + c : 2 * j + c + 1]
                place = slot - me * (per_owner * CAP)
                mine = (place >= 0) & (place < per_owner * CAP)
                places[c].append(jnp.where(mine, side * (per_owner * CAP) + place, -1))
                wheres[c].append(jnp.where(mine, (place // CAP * exp_count + sender) * CAP + place % CAP, -1))
                named[c].append(slot // CAP)
    places, wheres, named = [[jnp.concatenate(column, axis=0) for column in pair] for pair in (places, wheres, named)]
    slot = iota(chosen_ref.shape, 1)
    chosen_ref[...] = ((places[0] == slot) | (places[1] == slot)).astype(f32).astype(bf16)
    lane = iota(target_ref.shape, 1)
    target = jnp.zeros(target_ref.shape, jnp.int32)
    for i, column in enumerate(wheres + named):
        target = jnp.where(lane == i, column, target)
    target_ref[...] = target


def place_rows(block, parts, factor, chosen, gain, top, held, rows_hbm, sems):
    me = lax.axis_index("exp")
    _, per_owner, cap, _ = held.shape
    copies, start = [], 0
    for ref in parts:
        for at, to in pieces(0, ref.shape[1]):
            cols = slice(start + at, start + to)
            normed = (ref[:, at:to].astype(f32) * factor * gain[:, cols]).astype(bf16)
            held[:, :, :, cols] = mm(chosen, normed, TN).astype(bf16).reshape(2, per_owner, cap, to - at)
            for side in range(2):
                place = rows_hbm.at[:, me ^ (block + side * top), :, cols]
                copies.append(pltpu.make_async_copy(held.at[side, :, :, cols], place, sems.at[len(copies)]))
                copies[-1].start()
        start += ref.shape[1]
    return copies


def gates_of(logits, target, rows, cap):
    wheres, named = [target[:, c : c + 1] for c in range(2)], [target[:, 2 + c : 3 + c] for c in range(2)]
    expert = iota(logits.shape, 1)
    toward = jnp.where(named[1] == expert, 1.0, 0.0) - jnp.where(named[0] == expert, 1.0, 0.0)
    first = 1.0 / (1.0 + jnp.exp(jnp.sum(toward * logits, axis=1, keepdims=True)))
    gates = [first, 1.0 - first]
    total = logits.shape[0]
    hit_row, hit_rank = iota((total, rows), 1), iota((total, LANES), 1)
    out = jnp.zeros((rows, LANES), f32)
    for c in range(2):
        left = jnp.where((wheres[c] >= 0) & (wheres[c] // cap == hit_row), gates[c], 0.0).astype(bf16)
        right = jnp.where(wheres[c] % cap == hit_rank, 1.0, 0.0).astype(bf16)
        out += mm(left, right, TN)
    return out


def near_kernel(parts, top, *refs):
    own, refs = refs[:parts], refs[parts:]
    early, refs = refs[: -10], refs[-10:]
    chosen_ref, target_ref, gain_ref, router_ref, rows_hbm, gates_ref, square_ref, logits_ref, held, sems = refs
    width = gain_ref.shape[1]
    tokens = own[0].shape[0]
    square, logits = sums(own, gain_ref, router_ref)
    factor = lax.rsqrt(square * (1.0 / width) + EPSILON)
    copies = place_rows(0, own, factor, chosen_ref[:tokens, :], gain_ref, top, held, rows_hbm, sems)
    gates_ref[...] = gates_of(logits * factor, target_ref[:tokens, :], gates_ref.shape[0], held.shape[2])
    for i in range(top - 1):
        square, logits = sums(early[i * (parts - 1) : (i + 1) * (parts - 1)], gain_ref, router_ref)
        square_ref[i * tokens : (i + 1) * tokens, :] = jnp.broadcast_to(square, (tokens, square_ref.shape[1]))
        logits_ref[i * tokens : (i + 1) * tokens, :] = logits
    for copy in copies:
        copy.wait()


def far_kernel(parts, top, *refs):
    late, refs = refs[: parts * (top - 1)], refs[parts * (top - 1) :]
    chosen_ref, target_ref, gain_ref, router_ref, near_gates, square_ref, logits_ref, _, rows_hbm, gates_hbm, held, gates_ref, sems, last = refs
    width = gain_ref.shape[1]
    tokens = late[0].shape[0]
    before = width - late[parts - 1].shape[1]
    gates = near_gates[...]
    copies = []
    for i in range(top - 1):
        block = late[i * parts : (i + 1) * parts]
        rows = slice(i * tokens, (i + 1) * tokens)
        token_rows = slice((i + 1) * tokens, (i + 2) * tokens)
        square, logits = sums(block[-1:], gain_ref.at[:, before:], router_ref.at[:, before:])
        factor = lax.rsqrt((square_ref[rows, :1] + square) * (1.0 / width) + EPSILON)
        copies += place_rows(
            i + 1, block, factor, chosen_ref[token_rows, :], gain_ref, top, held.at[i], rows_hbm, sems.at[i]
        )
        logits = (logits_ref[rows, :] + logits) * factor
        gates += gates_of(logits, target_ref[token_rows, :], gates.shape[0], held.shape[3])
    per_owner, exp_count, cap = gates_ref.shape
    for e in range(per_owner):
        gates_ref[e] = gates[e * exp_count : (e + 1) * exp_count, :cap].astype(bf16)
    copies.append(pltpu.make_async_copy(gates_ref, gates_hbm, last))
    copies[-1].start()
    for copy in copies:
        copy.wait()


def swap(block, axis, mask):
    return lax.ppermute(block, axis, [(i, i ^ mask) for i in range(lax.axis_size(axis))])


def call(kernel, out, *args, specs=None, out_specs=None, scratch=(), flops=0, moved=0, limit=16 * MIB, aliases=None):
    single = not isinstance(out, (tuple, list))
    specs = specs or [VMEM] * len(args)
    args = [pltpu.with_memory_space_constraint(a, pltpu.HBM) if s is HBM else a for a, s in zip(args, specs, strict=True)]
    return pl.pallas_call(
        kernel,
        out_shape=out,
        in_specs=specs,
        out_specs=out_specs or (VMEM if single else (VMEM,) * len(out)),
        scratch_shapes=scratch,
        input_output_aliases=aliases or {},
        compiler_params=pltpu.CompilerParams(vmem_limit_bytes=limit),
        cost_estimate=pl.CostEstimate(flops=flops, bytes_accessed=moved, transcendentals=0),
    )(*args)


def on_device(queries, keys_in, values, decay_rate, out_weight, residual, norm_gain, router, expert_ids):
    q, k, v, decay, weight = queries[0], keys_in[0], values[0], decay_rate[0], out_weight[0]
    ids = jnp.swapaxes(expert_ids[0], 0, 1)
    router_t = jnp.swapaxes(router[0], 0, 1)
    length, heads = q.shape[0], decay.shape[0]
    dh = q.shape[1] // heads
    width = weight.shape[1]
    tokens = residual.shape[1]
    exp_count, ctx_count = lax.axis_size("exp"), lax.axis_size("ctx")
    exp_bits, ctx_bits = exp_count.bit_length() - 1, ctx_count.bit_length() - 1
    per_owner = router.shape[2] // exp_count
    shape = jax.ShapeDtypeStruct

    msg_shape = shape((heads * dh + pad_rows(heads), dh), bf16)
    part = pltpu.VMEM((length, heads * dh), bf16)
    small = pltpu.VMEM(decay.shape, f32)
    dma = pltpu.SemaphoreType.DMA
    msg = call(state_kernel, msg_shape, k, v, decay, specs=[HBM] * 3, scratch=[part, part, small, dma((3,))])
    got = []
    for bit in range(ctx_bits):
        got.append(swap(msg, "ctx", (2 << bit) - 1))
        if bit < ctx_bits - 1:
            last_shape = shape((heads * dh, dh), bf16)
            out = msg_shape if bit < ctx_bits - 2 else last_shape
            msg = call(functools.partial(join_kernel, heads, bit), out, msg, got[-1])
    inside, slots, weight_near, q_near, growth = call(
        inside_kernel,
        (
            shape((length, heads * dh), f32),
            shape((tokens, LANES), jnp.int32),
            shape(weight.shape, bf16),
            shape(q.shape, bf16),
            shape((length, LANES), f32),
        ),
        q, k, v, decay, ids, weight,
        specs=[HBM] * 6,
        scratch=[part, part, small, pltpu.VMEM(ids.shape, jnp.int32), dma((6,))],
        moved=weight.size * 2,
    )
    base, scale = call(
        functools.partial(base_kernel, heads),
        (shape((length, heads * dh), f32), shape((length, LANES), f32)),
        q_near, inside, growth, *got[:-1],
    )
    order = [sum(((i >> b) & 1) << (exp_bits - 1 - b) for b in range(exp_bits)) for i in range(exp_count)]
    cuts = [width * i // PARTS // LANES * LANES for i in range(PARTS + 1)]
    sections = lax.axis_size("section")
    top = exp_count // 2

    def relay(block):
        return lax.ppermute(block, "section", [(i, (i + 1) % sections) for i in range(sections)])

    all_tokens, experts = exp_count * tokens, per_owner * exp_count
    mixed, groups = None, []
    for start, stop in zip(cuts, cuts[1:]):
        first = mixed is None
        size = stop - start
        extra = LANES if first else 0
        halves = (shape((length // 2, size), bf16), shape((length // 2, size + extra), bf16))
        cost = 2 * length * heads * dh * size
        if first:
            mixed, keep, send = call(
                functools.partial(mix_kernel, heads, order, stop),
                (shape((length, heads * dh), bf16), *halves),
                q_near, base, scale, got[-1], weight_near, slots,
                scratch=[part],
                flops=cost,
            )
        else:
            keep, send = call(functools.partial(project_kernel, start, stop), halves, mixed, weight_near, flops=cost)
        for bit in range(exp_bits - 2):
            rest = keep.shape[0] // 2
            send, keep = call(
                functools.partial(halve_kernel, bit, tokens, first),
                (shape((rest, size + extra), bf16), shape((rest, size), f32)),
                keep, send, swap(send, "exp", 1 << bit),
            )
        own = call(
            functools.partial(carry_kernel, exp_bits - 2, start, first),
            shape((2 * tokens, size + extra), bf16),
            keep, send, swap(send, "exp", top // 2), residual[0],
        )
        whole = shape((2 * tokens, size), bf16)
        if first:
            other = swap(own, "exp", top)
            facts = call(
                functools.partial(facts_kernel, exp_count, experts, tokens),
                (shape((all_tokens, 2 * per_owner * CAP), bf16), shape((all_tokens, LANES), jnp.int32)),
                own, other,
            )
            block = relay(call(combine_kernel, whole, own, other))
        else:
            own = relay(own)
            other, *facts = lax.optimization_barrier((swap(own, "exp", top), *facts))
            block = call(combine_kernel, whole, own, other)
        groups.append([block])
        for index in range(1, top):
            groups[-1].append(swap(groups[-1][index & (index - 1)], "exp", index & -index))
    rows_shape = (per_owner, exp_count, CAP, width)
    count = 2 * sum(len(pieces(0, part_groups[0].shape[1])) for part_groups in groups)
    late_tokens = all_tokens - 2 * tokens
    held = (2, per_owner, CAP, width)
    rows, *near = call(
        functools.partial(near_kernel, PARTS, top),
        (
            shape(rows_shape, bf16),
            shape((experts, LANES), f32),
            shape((late_tokens, LANES), f32),
            shape((late_tokens, experts), f32),
        ),
        *[part_groups[0] for part_groups in groups],
        *[part_groups[i] for i in range(1, top) for part_groups in groups[:-1]],
        *facts, norm_gain, router_t,
        out_specs=(HBM, VMEM, VMEM, VMEM),
        scratch=[pltpu.VMEM(held, bf16), dma((count,))],
    )
    rows, gates = call(
        functools.partial(far_kernel, PARTS, top),
        (shape(rows_shape, bf16), shape(rows_shape[:-1], bf16)),
        *[part_groups[i] for i in range(1, top) for part_groups in groups],
        *facts, norm_gain, router_t, *near, rows,
        specs=[VMEM] * (PARTS * (top - 1) + 7) + [HBM],
        out_specs=(HBM, HBM),
        scratch=[
            pltpu.VMEM((top - 1, *held), bf16),
            pltpu.VMEM(rows_shape[:-1], bf16),
            dma((top - 1, count)),
            dma,
        ],
        aliases={PARTS * (top - 1) + 7: 0},
    )
    return rows[None, None], gates[None, None]


def solution(mesh):
    placed = (
        P("section", "ctx", "exp"),
        P("section", "ctx", "exp"),
        P("section", "ctx", "exp"),
        P("section", "exp", "ctx"),
        P("section", "exp", None),
        P("section", ("ctx", "exp"), None),
        P("section", None),
        P("section", None, None),
        P("section", ("ctx", "exp"), None),
    )
    return jax.shard_map(
        on_device,
        mesh=mesh,
        in_specs=placed,
        out_specs=(
            P("section", "ctx", "exp", None, None, None),
            P("section", "ctx", "exp", None, None),
        ),
        check_vma=False,
    )
```

```python
import functools

import jax
import jax.numpy as jnp
from jax import lax
from jax.experimental import pallas as pl
from jax.experimental.pallas import tpu as pltpu
from jax.sharding import PartitionSpec as P

CAP = 4
EPSILON = 1e-05
LANES = 128
ROWS = 16
MIB = 1 << 20
PARTS = 2

VMEM = pl.BlockSpec(memory_space=pltpu.VMEM)
HBM = pl.BlockSpec(memory_space=pltpu.HBM)
bf16 = jnp.bfloat16
f32 = jnp.float32


def iota(shape, dim):
    return lax.broadcasted_iota(jnp.int32, shape, dim)


def mm(a, b, dims):
    return lax.dot_general(a, b, (dims, ((), ())), preferred_element_type=f32)


NN = ((1,), (0,))
NT = ((1,), (1,))
TN = ((0,), (0,))


def to_column(row):
    n = row.shape[1]
    square = jnp.broadcast_to(row, (n, n))
    return jnp.sum(jnp.where(iota((n, n), 0) == iota((n, n), 1), square, jnp.zeros_like(square)), axis=1, keepdims=True)


def cumulative(row):
    n = row.shape[1]
    at, of = iota((n, n), 0), iota((n, n), 1)
    column = -jnp.sum(jnp.where(of <= at, jnp.broadcast_to(row, (n, n)), 0.0), axis=1, keepdims=True)
    along = jnp.sum(jnp.where(at == of, jnp.broadcast_to(column, (n, n)), 0.0), axis=0, keepdims=True)
    return column, along


def pad_rows(heads):
    return -(-3 * heads // ROWS) * ROWS


def log_rows(values):
    heads, shape = len(values), (pad_rows(len(values)), values[0].shape[1])
    row, out = iota(shape, 0), jnp.zeros(shape, f32)
    for h, value in enumerate(values):
        for part in range(3):
            piece = value.astype(bf16).astype(f32)
            out = jnp.where(row == part * heads + h, piece, out)
            value = value - piece
    return out.astype(bf16)


def get_log(block, heads, h):
    return block[h : h + 1] + block[heads + h : heads + h + 1] + block[2 * heads + h : 2 * heads + h + 1]


def fetch(sources, places, sems):
    copies = [pltpu.make_async_copy(s, p, sems.at[i]) for i, (s, p) in enumerate(zip(sources, places, strict=True))]
    for copy in copies:
        copy.start()
    return copies


def state_kernel(k_hbm, v_hbm, decay_hbm, msg_ref, k_ref, v_ref, decay_ref, sems):
    copies = fetch((decay_hbm, k_hbm, v_hbm), (decay_ref, k_ref, v_ref), sems)
    heads = decay_ref.shape[0]
    dh = k_ref.shape[1] // heads
    base = heads * dh
    copies[0].wait()
    tails, lasts = [], []
    for h in range(heads):
        column, along = cumulative(decay_ref[h : h + 1, :])
        last = along[:, -1:]
        tails.append(jnp.exp(last - column))
        lasts.append(jnp.broadcast_to(last, (1, dh)))
    msg_ref[base:, :] = log_rows(lasts)
    copies[1].wait()
    copies[2].wait()
    for h in range(heads):
        keyed = (k_ref[:, h * dh : (h + 1) * dh].astype(f32) * tails[h]).astype(bf16)
        msg_ref[h * dh : (h + 1) * dh, :] = mm(keyed, v_ref[:, h * dh : (h + 1) * dh], TN).astype(bf16)


def joined(heads, bit, own_ref, got_ref):
    dh = own_ref.shape[1]
    base = heads * dh
    upper = (lax.axis_index("ctx") >> bit) & 1
    is_upper = jnp.full((1, dh), upper, jnp.int32) == 1
    own_block = own_ref[base:, :].astype(f32)
    got_block = got_ref[base:, :].astype(f32)
    for h in range(heads):
        own_log, got_log = get_log(own_block, heads, h), get_log(got_block, heads, h)
        own = own_ref[h * dh : (h + 1) * dh, :].astype(f32)
        got = got_ref[h * dh : (h + 1) * dh, :].astype(f32)
        scale_own = jnp.where(is_upper, 1.0, jnp.exp(got_log))
        scale_got = jnp.where(is_upper, jnp.exp(own_log), 1.0)
        yield scale_own * own + scale_got * got, own_log + got_log


def join_kernel(heads, bit, own_ref, got_ref, msg_ref):
    dh = own_ref.shape[1]
    logs = []
    for h, (state, log) in enumerate(joined(heads, bit, own_ref, got_ref)):
        msg_ref[h * dh : (h + 1) * dh, :] = state.astype(bf16)
        logs.append(log)
    if msg_ref.shape[0] > heads * dh:
        msg_ref[heads * dh :, :] = log_rows(logs)


def split_mm(a, state):
    high = state.astype(bf16)
    low = (state - high.astype(f32)).astype(bf16)
    return mm(a, high, NN) + mm(a, low, NN)


def weight_kernel(weight_hbm, out_ref, sem):
    copy = pltpu.make_async_copy(weight_hbm.at[:, : out_ref.shape[1]], out_ref, sem)
    copy.start()
    copy.wait()


def inside_kernel(q_hbm, k_hbm, v_hbm, decay_hbm, ids_hbm, weight_hbm, inside_ref, slots_ref, weight_ref, q_ref, growth_ref,
                  k_ref, v_ref, decay_ref, ids_ref, sems):
    copies = fetch(
        (decay_hbm, ids_hbm, q_hbm, k_hbm, v_hbm, weight_hbm.at[:, -weight_ref.shape[1] :]),
        (decay_ref, ids_ref, q_ref, k_ref, v_ref, weight_ref),
        sems,
    )
    for copy in copies[:-1]:
        copy.wait()
    heads = decay_ref.shape[0]
    length = q_ref.shape[0]
    dh = q_ref.shape[1] // heads
    causal = iota((length, length), 0) >= iota((length, length), 1)
    lane = iota((length, LANES), 1)
    growth = jnp.zeros((length, LANES), f32)
    for h in range(heads):
        cols = slice(h * dh, (h + 1) * dh)
        column, along = cumulative(decay_ref[h : h + 1, :])
        scores = mm(q_ref[:, cols], k_ref[:, cols], NT)
        weights = jnp.where(causal, scores * jnp.exp(jnp.minimum(column - along, 0.0)), 0.0).astype(bf16)
        inside_ref[:, cols] = mm(weights, v_ref[:, cols], NN)
        growth = jnp.where(lane == h, jnp.exp(column), growth)
    growth_ref[...] = growth
    n = ids_ref.shape[1]
    earlier = iota((n, n), 1) < iota((n, n), 0)
    rows = [ids_ref[c : c + 1, :] for c in range(2)]
    places = []
    for c in range(2):
        mine = to_column(rows[c])
        rank = jnp.zeros((n, 1), jnp.int32)
        for other in range(2):
            rank += jnp.sum(jnp.where(earlier & (mine == rows[other]), 1, 0), axis=1, keepdims=True)
        places.append(mine * CAP + rank)
    lane = iota((n, LANES), 1)
    slots_ref[...] = jnp.where(lane == 0, places[0], jnp.where(lane == 1, places[1], 0))
    copies[-1].wait()


def base_kernel(heads, q_ref, inside_ref, growth_ref, *rest):
    got_refs, (base_ref, scale_ref) = rest[:-2], rest[-2:]
    bits = len(got_refs)
    dh = q_ref.shape[1] // heads
    base = heads * dh
    place = lax.axis_index("ctx")
    blocks = [ref[base:, :].astype(f32) for ref in got_refs]
    uppers = [jnp.full((1, dh), (place >> bit) & 1, jnp.int32) == 1 for bit in range(bits + 1)]
    lane = iota(scale_ref.shape, 1)
    scale = jnp.zeros(scale_ref.shape, f32)
    for h in range(heads):
        cols = slice(h * dh, (h + 1) * dh)
        incoming = jnp.zeros((dh, dh), f32)
        before = jnp.zeros((1, dh), f32)
        for bit in range(bits):
            got = got_refs[bit][h * dh : (h + 1) * dh, :].astype(f32)
            incoming += jnp.where(uppers[bit], jnp.exp(before), 0.0) * got
            before += jnp.where(uppers[bit], get_log(blocks[bit], heads, h), 0.0)
        growth = growth_ref[:, h : h + 1]
        base_ref[:, cols] = inside_ref[:, cols] + growth * split_mm(q_ref[:, cols], incoming)
        factor = jnp.where(uppers[bits], jnp.exp(before), 0.0)
        scale = jnp.where(lane == h, growth * factor[:, :1], scale)
    scale_ref[...] = scale


def answer_kernel(heads, asked_ref, state_ref, out_ref):
    dh = state_ref.shape[1]
    for h in range(heads):
        cols = slice(h * dh, (h + 1) * dh)
        out_ref[:, cols] = mm(asked_ref[:, cols], state_ref[h * dh : (h + 1) * dh, :], NN).astype(bf16)


def mix_kernel(heads, order, stop, q_ref, base_ref, scale_ref, state_ref, *rest):
    *answers, weight_ref, slots_ref, mixed_ref, keep_ref, send_ref, attended = rest
    dh = base_ref.shape[1] // heads
    me = lax.axis_index("exp")
    last = jnp.full((base_ref.shape[0], dh), lax.axis_index("ctx"), jnp.int32) == 3
    for h in range(heads):
        cols = slice(h * dh, (h + 1) * dh)
        outside = mm(q_ref[:, cols], state_ref[h * dh : (h + 1) * dh, :], NN)
        for answer_ref in answers:
            outside = jnp.where(last, answer_ref[:, cols].astype(f32), outside)
        attended[:, cols] = (base_ref[:, cols] + scale_ref[:, h : h + 1] * outside).astype(bf16)
    share = base_ref.shape[0] // len(order)
    for i, k in enumerate(order):
        mixed_ref[i * share : (i + 1) * share, :] = attended[pl.ds(pl.multiple_of((me ^ k) * share, share), share), :]
    project_kernel(0, stop, mixed_ref, weight_ref, keep_ref, send_ref)
    put_lanes(send_ref, slots_ref[...].astype(f32))


def project_kernel(start, stop, mixed_ref, weight_ref, keep_ref, send_ref):
    half = mixed_ref.shape[0] // 2
    mixed = mixed_ref[...]
    for at, to in pieces(start, stop):
        part = mm(mixed, weight_ref[:, at:to], NN).astype(bf16)
        keep_ref[:, at - start : to - start] = part[:half]
        send_ref[:, at - start : to - start] = part[half:]


def pieces(start, stop, step=3072):
    return [(at, min(at + step, stop)) for at in range(start, stop, step)]


def put_lanes(ref, lanes):
    tokens = lanes.shape[0]
    ref[:tokens, -LANES:] = lanes.astype(bf16)
    if ref.shape[0] > tokens:
        ref[tokens:, -LANES:] = jnp.zeros((ref.shape[0] - tokens, LANES), bf16)


def widen_lanes(bit, tokens, sent_ref, got_ref):
    own, got = sent_ref[:tokens, -LANES:].astype(f32), got_ref[:tokens, -LANES:].astype(f32)
    filled = 2 << bit
    return jnp.where(iota(own.shape, 1) < filled, own, jnp.roll(got, filled, axis=1))


def halve_kernel(bit, tokens, tagged, keep_ref, sent_ref, got_ref, send_ref, own_ref):
    half, width = own_ref.shape
    own_ref[...] = keep_ref[:half, :].astype(f32) + got_ref[:half, :width].astype(f32)
    send_ref[:, :width] = (keep_ref[half:, :].astype(f32) + got_ref[half:, :width].astype(f32)).astype(bf16)
    if tagged:
        put_lanes(send_ref, widen_lanes(bit, tokens, sent_ref, got_ref))


def carry_kernel(bit, start, tagged, keep_ref, sent_ref, got_ref, residual_ref, out_ref):
    tokens = residual_ref.shape[0]
    width = keep_ref.shape[1]
    total = keep_ref[...].astype(f32) + got_ref[:, :width].astype(f32)
    own = total[:tokens] + residual_ref[:, start : start + width].astype(f32)
    out_ref[:tokens, :width] = own.astype(bf16)
    out_ref[tokens:, :width] = total[tokens:].astype(bf16)
    if tagged:
        put_lanes(out_ref, widen_lanes(bit, tokens, sent_ref, got_ref))


def combine_kernel(own_ref, got_ref, out_ref):
    rows, width = out_ref.shape
    half = rows // 2
    out_ref[:half, :] = (own_ref[:half, :width].astype(f32) + got_ref[half:, :width].astype(f32)).astype(bf16)
    out_ref[half:, :] = (own_ref[half:, :width].astype(f32) + got_ref[:half, :width].astype(f32)).astype(bf16)


def sums(refs, gain, router):
    square, logits, start = 0.0, 0.0, 0
    for ref in refs:
        for at, to in pieces(0, ref.shape[1]):
            wide = ref[:, at:to].astype(f32)
            square += jnp.sum(wide * wide, axis=1, keepdims=True)
            cols = slice(start + at, start + to)
            logits += mm((wide * gain[:, cols]).astype(bf16), router[:, cols], NT)
        start += ref.shape[1]
    return square, logits


def facts_kernel(exp_count, experts, tokens, own_ref, got_ref, chosen_ref, target_ref):
    per_owner = experts // exp_count
    top = exp_count // 2
    me = lax.axis_index("exp")
    lanes = [ref[:tokens, -LANES:].astype(f32).astype(jnp.int32) for ref in (own_ref, got_ref)]
    places, wheres, named = [[], []], [[], []], [[], []]
    for j in range(top):
        for side in range(2):
            sender = me ^ (j + side * top)
            for c in range(2):
                slot = lanes[side][:, 2 * j + c : 2 * j + c + 1]
                place = slot - me * (per_owner * CAP)
                mine = (place >= 0) & (place < per_owner * CAP)
                places[c].append(jnp.where(mine, side * (per_owner * CAP) + place, -1))
                wheres[c].append(jnp.where(mine, (place // CAP * exp_count + sender) * CAP + place % CAP, -1))
                named[c].append(slot // CAP)
    places, wheres, named = [[jnp.concatenate(column, axis=0) for column in pair] for pair in (places, wheres, named)]
    slot = iota(chosen_ref.shape, 1)
    chosen_ref[...] = ((places[0] == slot) | (places[1] == slot)).astype(f32).astype(bf16)
    lane = iota(target_ref.shape, 1)
    target = jnp.zeros(target_ref.shape, jnp.int32)
    for i, column in enumerate(wheres + named):
        target = jnp.where(lane == i, column, target)
    target_ref[...] = target


def place_rows(block, parts, factor, chosen, gain, top, held, rows_hbm, sems):
    me = lax.axis_index("exp")
    _, per_owner, cap, _ = held.shape
    copies, start = [], 0
    for ref in parts:
        for at, to in pieces(0, ref.shape[1]):
            cols = slice(start + at, start + to)
            normed = (ref[:, at:to].astype(f32) * factor * gain[:, cols]).astype(bf16)
            held[:, :, :, cols] = mm(chosen, normed, TN).astype(bf16).reshape(2, per_owner, cap, to - at)
            for side in range(2):
                place = rows_hbm.at[:, me ^ (block + side * top), :, cols]
                copies.append(pltpu.make_async_copy(held.at[side, :, :, cols], place, sems.at[len(copies)]))
                copies[-1].start()
        start += ref.shape[1]
    return copies


def gates_of(logits, target, rows, cap):
    wheres, named = [target[:, c : c + 1] for c in range(2)], [target[:, 2 + c : 3 + c] for c in range(2)]
    expert = iota(logits.shape, 1)
    toward = jnp.where(named[1] == expert, 1.0, 0.0) - jnp.where(named[0] == expert, 1.0, 0.0)
    first = 1.0 / (1.0 + jnp.exp(jnp.sum(toward * logits, axis=1, keepdims=True)))
    gates = [first, 1.0 - first]
    total = logits.shape[0]
    hit_row, hit_rank = iota((total, rows), 1), iota((total, LANES), 1)
    out = jnp.zeros((rows, LANES), f32)
    for c in range(2):
        left = jnp.where((wheres[c] >= 0) & (wheres[c] // cap == hit_row), gates[c], 0.0).astype(bf16)
        right = jnp.where(wheres[c] % cap == hit_rank, 1.0, 0.0).astype(bf16)
        out += mm(left, right, TN)
    return out


def near_kernel(parts, top, *refs):
    own, refs = refs[:parts], refs[parts:]
    early, refs = refs[: -10], refs[-10:]
    chosen_ref, target_ref, gain_ref, router_ref, rows_hbm, gates_ref, square_ref, logits_ref, held, sems = refs
    width = gain_ref.shape[1]
    tokens = own[0].shape[0]
    square, logits = sums(own, gain_ref, router_ref)
    factor = lax.rsqrt(square * (1.0 / width) + EPSILON)
    copies = place_rows(0, own, factor, chosen_ref[:tokens, :], gain_ref, top, held, rows_hbm, sems)
    gates_ref[...] = gates_of(logits * factor, target_ref[:tokens, :], gates_ref.shape[0], held.shape[2])
    for i in range(top - 1):
        square, logits = sums(early[i * (parts - 1) : (i + 1) * (parts - 1)], gain_ref, router_ref)
        square_ref[i * tokens : (i + 1) * tokens, :] = jnp.broadcast_to(square, (tokens, square_ref.shape[1]))
        logits_ref[i * tokens : (i + 1) * tokens, :] = logits
    for copy in copies:
        copy.wait()


def far_kernel(parts, top, *refs):
    late, refs = refs[: parts * (top - 1)], refs[parts * (top - 1) :]
    chosen_ref, target_ref, gain_ref, router_ref, near_gates, square_ref, logits_ref, _, rows_hbm, gates_hbm, held, gates_ref, sems, last = refs
    width = gain_ref.shape[1]
    tokens = late[0].shape[0]
    before = width - late[parts - 1].shape[1]
    gates = near_gates[...]
    copies = []
    for i in range(top - 1):
        block = late[i * parts : (i + 1) * parts]
        rows = slice(i * tokens, (i + 1) * tokens)
        token_rows = slice((i + 1) * tokens, (i + 2) * tokens)
        square, logits = sums(block[-1:], gain_ref.at[:, before:], router_ref.at[:, before:])
        factor = lax.rsqrt((square_ref[rows, :1] + square) * (1.0 / width) + EPSILON)
        copies += place_rows(
            i + 1, block, factor, chosen_ref[token_rows, :], gain_ref, top, held.at[i], rows_hbm, sems.at[i]
        )
        logits = (logits_ref[rows, :] + logits) * factor
        gates += gates_of(logits, target_ref[token_rows, :], gates.shape[0], held.shape[3])
    per_owner, exp_count, cap = gates_ref.shape
    for e in range(per_owner):
        gates_ref[e] = gates[e * exp_count : (e + 1) * exp_count, :cap].astype(bf16)
    copies.append(pltpu.make_async_copy(gates_ref, gates_hbm, last))
    copies[-1].start()
    for copy in copies:
        copy.wait()


def swap(block, axis, mask):
    return lax.ppermute(block, axis, [(i, i ^ mask) for i in range(lax.axis_size(axis))])


def hop(block, axis, route):
    places, exps = lax.axis_size(axis), lax.axis_size("exp")
    pairs = [(c * exps + e, to * exps + to_e) for c in range(places) for e in range(exps) for to, to_e in [route(c, e)]]
    return lax.ppermute(block, (axis, "exp"), pairs)


def around(place, index):
    return ({1: 3, 3: 2, 2: 1}[place], index) if place else (place, index ^ 1)


def between(pair, place, index):
    return (sum(pair) - place, index) if place in pair else (place, index ^ 1)


def call(kernel, out, *args, specs=None, out_specs=None, scratch=(), flops=0, moved=0, limit=16 * MIB, aliases=None):
    single = not isinstance(out, (tuple, list))
    specs = specs or [VMEM] * len(args)
    args = [pltpu.with_memory_space_constraint(a, pltpu.HBM) if s is HBM else a for a, s in zip(args, specs, strict=True)]
    return pl.pallas_call(
        kernel,
        out_shape=out,
        in_specs=specs,
        out_specs=out_specs or (VMEM if single else (VMEM,) * len(out)),
        scratch_shapes=scratch,
        input_output_aliases=aliases or {},
        compiler_params=pltpu.CompilerParams(vmem_limit_bytes=limit),
        cost_estimate=pl.CostEstimate(flops=flops, bytes_accessed=moved, transcendentals=0),
    )(*args)


def on_device(queries, keys_in, values, decay_rate, out_weight, residual, norm_gain, router, expert_ids):
    q, k, v, decay, weight = queries[0], keys_in[0], values[0], decay_rate[0], out_weight[0]
    ids = jnp.swapaxes(expert_ids[0], 0, 1)
    router_t = jnp.swapaxes(router[0], 0, 1)
    length, heads = q.shape[0], decay.shape[0]
    dh = q.shape[1] // heads
    width = weight.shape[1]
    tokens = residual.shape[1]
    exp_count, ctx_count = lax.axis_size("exp"), lax.axis_size("ctx")
    exp_bits, ctx_bits = exp_count.bit_length() - 1, ctx_count.bit_length() - 1
    per_owner = router.shape[2] // exp_count
    shape = jax.ShapeDtypeStruct

    msg_shape = shape((heads * dh + pad_rows(heads), dh), bf16)
    part = pltpu.VMEM((length, heads * dh), bf16)
    small = pltpu.VMEM(decay.shape, f32)
    dma = pltpu.SemaphoreType.DMA
    msg = call(state_kernel, msg_shape, k, v, decay, specs=[HBM] * 3, scratch=[part, part, small, dma((3,))])
    cuts = [width * i // PARTS // LANES * LANES for i in range(PARTS + 1)]
    weight_after, msg = lax.optimization_barrier((weight, msg))
    weight_early = call(
        weight_kernel, shape((heads * dh, cuts[1]), bf16), weight_after, specs=[HBM], scratch=[dma], moved=weight.size
    )
    got = []
    for bit in range(ctx_bits - 1):
        got.append(swap(msg, "ctx", (2 << bit) - 1))
        if bit == 0:
            msg, weight_early = lax.optimization_barrier((msg, weight_early))
        outs = msg_shape if bit < ctx_bits - 2 else shape((heads * dh, dh), bf16)
        msg = call(functools.partial(join_kernel, heads, bit), outs, msg, got[-1])
    if ctx_bits == 2:
        asked = hop(q, "ctx", functools.partial(between, (1, 3)))
        near = hop(msg, "ctx", functools.partial(between, (1, 2)))
        answer = call(functools.partial(answer_kernel, heads), shape(q.shape, bf16), asked, msg)
        latest = [near, hop(answer, "ctx", around)]
    else:
        latest = [swap(msg, "ctx", ctx_count - 1)]
    inside, slots, weight_late, q_near, growth = call(
        inside_kernel,
        (
            shape((length, heads * dh), f32),
            shape((tokens, LANES), jnp.int32),
            shape((heads * dh, width - cuts[1]), bf16),
            shape(q.shape, bf16),
            shape((length, LANES), f32),
        ),
        q, k, v, decay, ids, weight,
        specs=[HBM] * 6,
        scratch=[part, part, small, pltpu.VMEM(ids.shape, jnp.int32), dma((6,))],
        moved=weight.size * 2,
    )
    base, scale = call(
        functools.partial(base_kernel, heads),
        (shape((length, heads * dh), f32), shape((length, LANES), f32)),
        q_near, inside, growth, *got,
    )
    order = [sum(((i >> b) & 1) << (exp_bits - 1 - b) for b in range(exp_bits)) for i in range(exp_count)]
    sections = lax.axis_size("section")
    top = exp_count // 2

    def relay(block):
        return lax.ppermute(block, "section", [(i, (i + 1) % sections) for i in range(sections)])

    all_tokens, experts = exp_count * tokens, per_owner * exp_count
    mixed, groups = None, []
    for start, stop in zip(cuts, cuts[1:]):
        first = mixed is None
        size = stop - start
        extra = LANES if first else 0
        halves = (shape((length // 2, size), bf16), shape((length // 2, size + extra), bf16))
        cost = 2 * length * heads * dh * size
        if first:
            mixed, keep, send = call(
                functools.partial(mix_kernel, heads, order, stop),
                (shape((length, heads * dh), bf16), *halves),
                q_near, base, scale, *latest, weight_early, slots,
                scratch=[part],
                flops=cost,
            )
        else:
            keep, send = call(functools.partial(project_kernel, 0, size), halves, mixed, weight_late, flops=cost)
        for bit in range(exp_bits - 2):
            rest = keep.shape[0] // 2
            send, keep = call(
                functools.partial(halve_kernel, bit, tokens, first),
                (shape((rest, size + extra), bf16), shape((rest, size), f32)),
                keep, send, swap(send, "exp", 1 << bit),
            )
        own = call(
            functools.partial(carry_kernel, exp_bits - 2, start, first),
            shape((2 * tokens, size + extra), bf16),
            keep, send, swap(send, "exp", top // 2), residual[0],
        )
        whole = shape((2 * tokens, size), bf16)
        if first:
            other = swap(own, "exp", top)
            facts = call(
                functools.partial(facts_kernel, exp_count, experts, tokens),
                (shape((all_tokens, 2 * per_owner * CAP), bf16), shape((all_tokens, LANES), jnp.int32)),
                own, other,
            )
            block = relay(call(combine_kernel, whole, own, other))
        else:
            own = relay(own)
            other, *facts = lax.optimization_barrier((swap(own, "exp", top), *facts))
            block = call(combine_kernel, whole, own, other)
        groups.append([block])
        for index in range(1, top):
            groups[-1].append(swap(groups[-1][index & (index - 1)], "exp", index & -index))
    rows_shape = (per_owner, exp_count, CAP, width)
    count = 2 * sum(len(pieces(0, part_groups[0].shape[1])) for part_groups in groups)
    late_tokens = all_tokens - 2 * tokens
    held = (2, per_owner, CAP, width)
    rows, *near = call(
        functools.partial(near_kernel, PARTS, top),
        (
            shape(rows_shape, bf16),
            shape((experts, LANES), f32),
            shape((late_tokens, LANES), f32),
            shape((late_tokens, experts), f32),
        ),
        *[part_groups[0] for part_groups in groups],
        *[part_groups[i] for i in range(1, top) for part_groups in groups[:-1]],
        *facts, norm_gain, router_t,
        out_specs=(HBM, VMEM, VMEM, VMEM),
        scratch=[pltpu.VMEM(held, bf16), dma((count,))],
    )
    rows, gates = call(
        functools.partial(far_kernel, PARTS, top),
        (shape(rows_shape, bf16), shape(rows_shape[:-1], bf16)),
        *[part_groups[i] for i in range(1, top) for part_groups in groups],
        *facts, norm_gain, router_t, *near, rows,
        specs=[VMEM] * (PARTS * (top - 1) + 7) + [HBM],
        out_specs=(HBM, HBM),
        scratch=[
            pltpu.VMEM((top - 1, *held), bf16),
            pltpu.VMEM(rows_shape[:-1], bf16),
            dma((top - 1, count)),
            dma,
        ],
        aliases={PARTS * (top - 1) + 7: 0},
    )
    return rows[None, None], gates[None, None]


def solution(mesh):
    placed = (
        P("section", "ctx", "exp"),
        P("section", "ctx", "exp"),
        P("section", "ctx", "exp"),
        P("section", "exp", "ctx"),
        P("section", "exp", None),
        P("section", ("ctx", "exp"), None),
        P("section", None),
        P("section", None, None),
        P("section", ("ctx", "exp"), None),
    )
    return jax.shard_map(
        on_device,
        mesh=mesh,
        in_specs=placed,
        out_specs=(
            P("section", "ctx", "exp", None, None, None),
            P("section", "ctx", "exp", None, None),
        ),
        check_vma=False,
    )
```

```python
import functools

import jax
import jax.numpy as jnp
from jax import lax
from jax.experimental import pallas as pl
from jax.experimental.pallas import tpu as pltpu
from jax.sharding import PartitionSpec as P

CAP = 4
EPSILON = 1e-05
LANES = 128
ROWS = 16
MIB = 1 << 20
PARTS = 2

VMEM = pl.BlockSpec(memory_space=pltpu.VMEM)
HBM = pl.BlockSpec(memory_space=pltpu.HBM)
bf16 = jnp.bfloat16
f32 = jnp.float32


def iota(shape, dim):
    return lax.broadcasted_iota(jnp.int32, shape, dim)


def mm(a, b, dims):
    return lax.dot_general(a, b, (dims, ((), ())), preferred_element_type=f32)


NN = ((1,), (0,))
NT = ((1,), (1,))
TN = ((0,), (0,))


def to_column(row):
    n = row.shape[1]
    square = jnp.broadcast_to(row, (n, n))
    return jnp.sum(jnp.where(iota((n, n), 0) == iota((n, n), 1), square, jnp.zeros_like(square)), axis=1, keepdims=True)


def cumulative(row):
    n = row.shape[1]
    at, of = iota((n, n), 0), iota((n, n), 1)
    column = -jnp.sum(jnp.where(of <= at, jnp.broadcast_to(row, (n, n)), 0.0), axis=1, keepdims=True)
    along = jnp.sum(jnp.where(at == of, jnp.broadcast_to(column, (n, n)), 0.0), axis=0, keepdims=True)
    return column, along


def pad_rows(heads):
    return -(-3 * heads // ROWS) * ROWS


def log_rows(values):
    heads, shape = len(values), (pad_rows(len(values)), values[0].shape[1])
    row, out = iota(shape, 0), jnp.zeros(shape, f32)
    for h, value in enumerate(values):
        for part in range(3):
            piece = value.astype(bf16).astype(f32)
            out = jnp.where(row == part * heads + h, piece, out)
            value = value - piece
    return out.astype(bf16)


def get_log(block, heads, h):
    return block[h : h + 1] + block[heads + h : heads + h + 1] + block[2 * heads + h : 2 * heads + h + 1]


def fetch(sources, places, sems):
    copies = [pltpu.make_async_copy(s, p, sems.at[i]) for i, (s, p) in enumerate(zip(sources, places, strict=True))]
    for copy in copies:
        copy.start()
    return copies


def state_kernel(k_hbm, v_hbm, decay_hbm, msg_ref, k_ref, v_ref, decay_ref, sems):
    copies = fetch((decay_hbm, k_hbm, v_hbm), (decay_ref, k_ref, v_ref), sems)
    heads = decay_ref.shape[0]
    dh = k_ref.shape[1] // heads
    base = heads * dh
    copies[0].wait()
    tails, lasts = [], []
    for h in range(heads):
        column, along = cumulative(decay_ref[h : h + 1, :])
        last = along[:, -1:]
        tails.append(jnp.exp(last - column))
        lasts.append(jnp.broadcast_to(last, (1, dh)))
    msg_ref[base:, :] = log_rows(lasts)
    copies[1].wait()
    copies[2].wait()
    for h in range(heads):
        keyed = (k_ref[:, h * dh : (h + 1) * dh].astype(f32) * tails[h]).astype(bf16)
        msg_ref[h * dh : (h + 1) * dh, :] = mm(keyed, v_ref[:, h * dh : (h + 1) * dh], TN).astype(bf16)


def joined(heads, bit, own_ref, got_ref):
    dh = own_ref.shape[1]
    base = heads * dh
    upper = (lax.axis_index("ctx") >> bit) & 1
    is_upper = jnp.full((1, dh), upper, jnp.int32) == 1
    own_block = own_ref[base:, :].astype(f32)
    got_block = got_ref[base:, :].astype(f32)
    for h in range(heads):
        own_log, got_log = get_log(own_block, heads, h), get_log(got_block, heads, h)
        own = own_ref[h * dh : (h + 1) * dh, :].astype(f32)
        got = got_ref[h * dh : (h + 1) * dh, :].astype(f32)
        scale_own = jnp.where(is_upper, 1.0, jnp.exp(got_log))
        scale_got = jnp.where(is_upper, jnp.exp(own_log), 1.0)
        yield scale_own * own + scale_got * got, own_log + got_log


def join_kernel(heads, bit, own_ref, got_ref, msg_ref):
    dh = own_ref.shape[1]
    logs = []
    for h, (state, log) in enumerate(joined(heads, bit, own_ref, got_ref)):
        msg_ref[h * dh : (h + 1) * dh, :] = state.astype(bf16)
        logs.append(log)
    if msg_ref.shape[0] > heads * dh:
        msg_ref[heads * dh :, :] = log_rows(logs)


def split_mm(a, state):
    high = state.astype(bf16)
    low = (state - high.astype(f32)).astype(bf16)
    return mm(a, high, NN) + mm(a, low, NN)


def weight_kernel(weight_hbm, out_ref, sem):
    copy = pltpu.make_async_copy(weight_hbm.at[:, : out_ref.shape[1]], out_ref, sem)
    copy.start()
    copy.wait()


def inside_kernel(q_hbm, k_hbm, v_hbm, decay_hbm, ids_hbm, weight_hbm, *refs):
    got_refs, refs = refs[:-12], refs[-12:]
    base_ref, scale_ref, slots_ref, weight_ref, q_ref, inside_ref, growth_ref, k_ref, v_ref, decay_ref, ids_ref, sems = refs
    copies = fetch(
        (decay_hbm, ids_hbm, q_hbm, k_hbm, v_hbm, weight_hbm.at[:, -weight_ref.shape[1] :]),
        (decay_ref, ids_ref, q_ref, k_ref, v_ref, weight_ref),
        sems,
    )
    for copy in copies[:-1]:
        copy.wait()
    heads = decay_ref.shape[0]
    length = q_ref.shape[0]
    dh = q_ref.shape[1] // heads
    causal = iota((length, length), 0) >= iota((length, length), 1)
    lane = iota((length, LANES), 1)
    growth = jnp.zeros((length, LANES), f32)
    for h in range(heads):
        cols = slice(h * dh, (h + 1) * dh)
        column, along = cumulative(decay_ref[h : h + 1, :])
        scores = mm(q_ref[:, cols], k_ref[:, cols], NT)
        weights = jnp.where(causal, scores * jnp.exp(jnp.minimum(column - along, 0.0)), 0.0).astype(bf16)
        inside_ref[:, cols] = mm(weights, v_ref[:, cols], NN)
        growth = jnp.where(lane == h, jnp.exp(column), growth)
    growth_ref[...] = growth
    base_kernel(heads, q_ref, inside_ref, growth_ref, *got_refs, base_ref, scale_ref)
    n = ids_ref.shape[1]
    earlier = iota((n, n), 1) < iota((n, n), 0)
    rows = [ids_ref[c : c + 1, :] for c in range(2)]
    places = []
    for c in range(2):
        mine = to_column(rows[c])
        rank = jnp.zeros((n, 1), jnp.int32)
        for other in range(2):
            rank += jnp.sum(jnp.where(earlier & (mine == rows[other]), 1, 0), axis=1, keepdims=True)
        places.append(mine * CAP + rank)
    lane = iota((n, LANES), 1)
    slots_ref[...] = jnp.where(lane == 0, places[0], jnp.where(lane == 1, places[1], 0))
    copies[-1].wait()


def base_kernel(heads, q_ref, inside_ref, growth_ref, *rest):
    got_refs, (base_ref, scale_ref) = rest[:-2], rest[-2:]
    bits = len(got_refs)
    dh = q_ref.shape[1] // heads
    base = heads * dh
    place = lax.axis_index("ctx")
    blocks = [ref[base:, :].astype(f32) for ref in got_refs]
    uppers = [jnp.full((1, dh), (place >> bit) & 1, jnp.int32) == 1 for bit in range(bits + 1)]
    lane = iota(scale_ref.shape, 1)
    scale = jnp.zeros(scale_ref.shape, f32)
    for h in range(heads):
        cols = slice(h * dh, (h + 1) * dh)
        incoming = jnp.zeros((dh, dh), f32)
        before = jnp.zeros((1, dh), f32)
        for bit in range(bits):
            got = got_refs[bit][h * dh : (h + 1) * dh, :].astype(f32)
            incoming += jnp.where(uppers[bit], jnp.exp(before), 0.0) * got
            before += jnp.where(uppers[bit], get_log(blocks[bit], heads, h), 0.0)
        growth = growth_ref[:, h : h + 1]
        base_ref[:, cols] = inside_ref[:, cols] + growth * split_mm(q_ref[:, cols], incoming)
        factor = jnp.where(uppers[bits], jnp.exp(before), 0.0)
        scale = jnp.where(lane == h, growth * factor[:, :1], scale)
    scale_ref[...] = scale


def answer_kernel(heads, asked_ref, state_ref, out_ref):
    dh = state_ref.shape[1]
    for h in range(heads):
        cols = slice(h * dh, (h + 1) * dh)
        out_ref[:, cols] = mm(asked_ref[:, cols], state_ref[h * dh : (h + 1) * dh, :], NN).astype(bf16)


def mix_kernel(heads, order, stop, q_ref, base_ref, scale_ref, state_ref, *rest):
    *answers, weight_ref, slots_ref, mixed_ref, keep_ref, send_ref, attended = rest
    dh = base_ref.shape[1] // heads
    me = lax.axis_index("exp")
    last = jnp.full((base_ref.shape[0], dh), lax.axis_index("ctx"), jnp.int32) == 3
    for h in range(heads):
        cols = slice(h * dh, (h + 1) * dh)
        outside = mm(q_ref[:, cols], state_ref[h * dh : (h + 1) * dh, :], NN)
        for answer_ref in answers:
            outside = jnp.where(last, answer_ref[:, cols].astype(f32), outside)
        attended[:, cols] = (base_ref[:, cols] + scale_ref[:, h : h + 1] * outside).astype(bf16)
    share = base_ref.shape[0] // len(order)
    for i, k in enumerate(order):
        mixed_ref[i * share : (i + 1) * share, :] = attended[pl.ds(pl.multiple_of((me ^ k) * share, share), share), :]
    project_kernel(0, stop, mixed_ref, weight_ref, keep_ref, send_ref)
    put_lanes(send_ref, slots_ref[...].astype(f32))


def project_kernel(start, stop, mixed_ref, weight_ref, keep_ref, send_ref):
    half = mixed_ref.shape[0] // 2
    mixed = mixed_ref[...]
    for at, to in pieces(start, stop):
        part = mm(mixed, weight_ref[:, at:to], NN).astype(bf16)
        keep_ref[:, at - start : to - start] = part[:half]
        send_ref[:, at - start : to - start] = part[half:]


def pieces(start, stop, step=3072):
    return [(at, min(at + step, stop)) for at in range(start, stop, step)]


def put_lanes(ref, lanes):
    tokens = lanes.shape[0]
    ref[:tokens, -LANES:] = lanes.astype(bf16)
    if ref.shape[0] > tokens:
        ref[tokens:, -LANES:] = jnp.zeros((ref.shape[0] - tokens, LANES), bf16)


def widen_lanes(bit, tokens, sent_ref, got_ref):
    own, got = sent_ref[:tokens, -LANES:].astype(f32), got_ref[:tokens, -LANES:].astype(f32)
    filled = 2 << bit
    return jnp.where(iota(own.shape, 1) < filled, own, jnp.roll(got, filled, axis=1))


def halve_kernel(bit, tokens, tagged, keep_ref, sent_ref, got_ref, send_ref, own_ref):
    half, width = own_ref.shape
    own_ref[...] = keep_ref[:half, :].astype(f32) + got_ref[:half, :width].astype(f32)
    send_ref[:, :width] = (keep_ref[half:, :].astype(f32) + got_ref[half:, :width].astype(f32)).astype(bf16)
    if tagged:
        put_lanes(send_ref, widen_lanes(bit, tokens, sent_ref, got_ref))


def carry_kernel(bit, start, tagged, keep_ref, sent_ref, got_ref, residual_ref, out_ref):
    tokens = residual_ref.shape[0]
    width = keep_ref.shape[1]
    total = keep_ref[...].astype(f32) + got_ref[:, :width].astype(f32)
    own = total[:tokens] + residual_ref[:, start : start + width].astype(f32)
    out_ref[:tokens, :width] = own.astype(bf16)
    out_ref[tokens:, :width] = total[tokens:].astype(bf16)
    if tagged:
        put_lanes(out_ref, widen_lanes(bit, tokens, sent_ref, got_ref))


def combine_kernel(own_ref, got_ref, out_ref):
    rows, width = out_ref.shape
    half = rows // 2
    out_ref[:half, :] = (own_ref[:half, :width].astype(f32) + got_ref[half:, :width].astype(f32)).astype(bf16)
    out_ref[half:, :] = (own_ref[half:, :width].astype(f32) + got_ref[:half, :width].astype(f32)).astype(bf16)


def sums(refs, gain, router):
    square, logits, start = 0.0, 0.0, 0
    for ref in refs:
        for at, to in pieces(0, ref.shape[1]):
            wide = ref[:, at:to].astype(f32)
            square += jnp.sum(wide * wide, axis=1, keepdims=True)
            cols = slice(start + at, start + to)
            logits += mm((wide * gain[:, cols]).astype(bf16), router[:, cols], NT)
        start += ref.shape[1]
    return square, logits


def facts_kernel(exp_count, experts, tokens, own_ref, got_ref, chosen_ref, target_ref):
    per_owner = experts // exp_count
    top = exp_count // 2
    me = lax.axis_index("exp")
    lanes = [ref[:tokens, -LANES:].astype(f32).astype(jnp.int32) for ref in (own_ref, got_ref)]
    places, wheres, named = [[], []], [[], []], [[], []]
    for j in range(top):
        for side in range(2):
            sender = me ^ (j + side * top)
            for c in range(2):
                slot = lanes[side][:, 2 * j + c : 2 * j + c + 1]
                place = slot - me * (per_owner * CAP)
                mine = (place >= 0) & (place < per_owner * CAP)
                places[c].append(jnp.where(mine, side * (per_owner * CAP) + place, -1))
                wheres[c].append(jnp.where(mine, (place // CAP * exp_count + sender) * CAP + place % CAP, -1))
                named[c].append(slot // CAP)
    places, wheres, named = [[jnp.concatenate(column, axis=0) for column in pair] for pair in (places, wheres, named)]
    slot = iota(chosen_ref.shape, 1)
    chosen_ref[...] = ((places[0] == slot) | (places[1] == slot)).astype(f32).astype(bf16)
    lane = iota(target_ref.shape, 1)
    target = jnp.zeros(target_ref.shape, jnp.int32)
    for i, column in enumerate(wheres + named):
        target = jnp.where(lane == i, column, target)
    target_ref[...] = target


def place_rows(block, parts, factor, chosen, gain, top, held, rows_hbm, sems):
    me = lax.axis_index("exp")
    _, per_owner, cap, _ = held.shape
    copies, start = [], 0
    for ref in parts:
        for at, to in pieces(0, ref.shape[1]):
            cols = slice(start + at, start + to)
            normed = (ref[:, at:to].astype(f32) * factor * gain[:, cols]).astype(bf16)
            held[:, :, :, cols] = mm(chosen, normed, TN).astype(bf16).reshape(2, per_owner, cap, to - at)
            for side in range(2):
                place = rows_hbm.at[:, me ^ (block + side * top), :, cols]
                copies.append(pltpu.make_async_copy(held.at[side, :, :, cols], place, sems.at[len(copies)]))
                copies[-1].start()
        start += ref.shape[1]
    return copies


def gates_of(logits, target, rows, cap):
    wheres, named = [target[:, c : c + 1] for c in range(2)], [target[:, 2 + c : 3 + c] for c in range(2)]
    expert = iota(logits.shape, 1)
    toward = jnp.where(named[1] == expert, 1.0, 0.0) - jnp.where(named[0] == expert, 1.0, 0.0)
    first = 1.0 / (1.0 + jnp.exp(jnp.sum(toward * logits, axis=1, keepdims=True)))
    gates = [first, 1.0 - first]
    total = logits.shape[0]
    hit_row, hit_rank = iota((total, rows), 1), iota((total, LANES), 1)
    out = jnp.zeros((rows, LANES), f32)
    for c in range(2):
        left = jnp.where((wheres[c] >= 0) & (wheres[c] // cap == hit_row), gates[c], 0.0).astype(bf16)
        right = jnp.where(wheres[c] % cap == hit_rank, 1.0, 0.0).astype(bf16)
        out += mm(left, right, TN)
    return out


def near_kernel(parts, top, *refs):
    own, refs = refs[:parts], refs[parts:]
    early, refs = refs[: -10], refs[-10:]
    chosen_ref, target_ref, gain_ref, router_ref, rows_hbm, gates_ref, square_ref, logits_ref, held, sems = refs
    width = gain_ref.shape[1]
    tokens = own[0].shape[0]
    square, logits = sums(own, gain_ref, router_ref)
    factor = lax.rsqrt(square * (1.0 / width) + EPSILON)
    copies = place_rows(0, own, factor, chosen_ref[:tokens, :], gain_ref, top, held, rows_hbm, sems)
    gates_ref[...] = gates_of(logits * factor, target_ref[:tokens, :], gates_ref.shape[0], held.shape[2])
    for i in range(top - 1):
        square, logits = sums(early[i * (parts - 1) : (i + 1) * (parts - 1)], gain_ref, router_ref)
        square_ref[i * tokens : (i + 1) * tokens, :] = jnp.broadcast_to(square, (tokens, square_ref.shape[1]))
        logits_ref[i * tokens : (i + 1) * tokens, :] = logits
    for copy in copies:
        copy.wait()


def far_kernel(parts, top, *refs):
    late, refs = refs[: parts * (top - 1)], refs[parts * (top - 1) :]
    chosen_ref, target_ref, gain_ref, router_ref, near_gates, square_ref, logits_ref, _, rows_hbm, gates_hbm, held, gates_ref, sems, last = refs
    width = gain_ref.shape[1]
    tokens = late[0].shape[0]
    before = width - late[parts - 1].shape[1]
    gates = near_gates[...]
    copies = []
    for i in range(top - 1):
        block = late[i * parts : (i + 1) * parts]
        rows = slice(i * tokens, (i + 1) * tokens)
        token_rows = slice((i + 1) * tokens, (i + 2) * tokens)
        square, logits = sums(block[-1:], gain_ref.at[:, before:], router_ref.at[:, before:])
        factor = lax.rsqrt((square_ref[rows, :1] + square) * (1.0 / width) + EPSILON)
        copies += place_rows(
            i + 1, block, factor, chosen_ref[token_rows, :], gain_ref, top, held.at[i], rows_hbm, sems.at[i]
        )
        logits = (logits_ref[rows, :] + logits) * factor
        gates += gates_of(logits, target_ref[token_rows, :], gates.shape[0], held.shape[3])
    per_owner, exp_count, cap = gates_ref.shape
    for e in range(per_owner):
        gates_ref[e] = gates[e * exp_count : (e + 1) * exp_count, :cap].astype(bf16)
    copies.append(pltpu.make_async_copy(gates_ref, gates_hbm, last))
    copies[-1].start()
    for copy in copies:
        copy.wait()


def swap(block, axis, mask):
    return lax.ppermute(block, axis, [(i, i ^ mask) for i in range(lax.axis_size(axis))])


def hop(block, axis, route):
    places, exps = lax.axis_size(axis), lax.axis_size("exp")
    pairs = [(c * exps + e, to * exps + to_e) for c in range(places) for e in range(exps) for to, to_e in [route(c, e)]]
    return lax.ppermute(block, (axis, "exp"), pairs)


def around(ring, place, index):
    return (ring[(ring.index(place) + 1) % len(ring)], index) if place in ring else (place, index ^ 1)


def between(pair, place, index):
    return (sum(pair) - place, index) if place in pair else (place, index ^ 1)


def call(kernel, out, *args, specs=None, out_specs=None, scratch=(), flops=0, moved=0, limit=16 * MIB, aliases=None):
    single = not isinstance(out, (tuple, list))
    specs = specs or [VMEM] * len(args)
    args = [pltpu.with_memory_space_constraint(a, pltpu.HBM) if s is HBM else a for a, s in zip(args, specs, strict=True)]
    return pl.pallas_call(
        kernel,
        out_shape=out,
        in_specs=specs,
        out_specs=out_specs or (VMEM if single else (VMEM,) * len(out)),
        scratch_shapes=scratch,
        input_output_aliases=aliases or {},
        compiler_params=pltpu.CompilerParams(vmem_limit_bytes=limit),
        cost_estimate=pl.CostEstimate(flops=flops, bytes_accessed=moved, transcendentals=0),
    )(*args)


def on_device(queries, keys_in, values, decay_rate, out_weight, residual, norm_gain, router, expert_ids):
    q, k, v, decay, weight = queries[0], keys_in[0], values[0], decay_rate[0], out_weight[0]
    ids = jnp.swapaxes(expert_ids[0], 0, 1)
    router_t = jnp.swapaxes(router[0], 0, 1)
    length, heads = q.shape[0], decay.shape[0]
    dh = q.shape[1] // heads
    width = weight.shape[1]
    tokens = residual.shape[1]
    exp_count, ctx_count = lax.axis_size("exp"), lax.axis_size("ctx")
    exp_bits, ctx_bits = exp_count.bit_length() - 1, ctx_count.bit_length() - 1
    per_owner = router.shape[2] // exp_count
    shape = jax.ShapeDtypeStruct

    msg_shape = shape((heads * dh + pad_rows(heads), dh), bf16)
    part = pltpu.VMEM((length, heads * dh), bf16)
    small = pltpu.VMEM(decay.shape, f32)
    dma = pltpu.SemaphoreType.DMA
    msg = call(state_kernel, msg_shape, k, v, decay, specs=[HBM] * 3, scratch=[part, part, small, dma((3,))])
    cuts = [width * i // PARTS // LANES * LANES for i in range(PARTS + 1)]
    weight_after, msg = lax.optimization_barrier((weight, msg))
    weight_early = call(
        weight_kernel, shape((heads * dh, cuts[1]), bf16), weight_after, specs=[HBM], scratch=[dma], moved=weight.size
    )
    got = []
    for bit in range(ctx_bits - 1):
        if ctx_bits == 2:
            got.append(lax.ppermute(msg, "ctx", [(c, (c + 1) % ctx_count) for c in range(ctx_count)]))
        else:
            got.append(swap(msg, "ctx", (2 << bit) - 1))
        if bit == 0:
            msg, weight_early = lax.optimization_barrier((msg, weight_early))
        outs = msg_shape if bit < ctx_bits - 2 else shape((heads * dh, dh), bf16)
        msg = call(functools.partial(join_kernel, heads, bit), outs, msg, got[-1])
    if ctx_bits == 2:
        asked = hop(q, "ctx", functools.partial(around, (3, 1, 2)))
        near = hop(msg, "ctx", functools.partial(between, (1, 2)))
        answer = call(functools.partial(answer_kernel, heads), shape(q.shape, bf16), asked, msg)
        latest = [near, hop(answer, "ctx", functools.partial(around, (1, 3, 2)))]
    else:
        latest = [swap(msg, "ctx", ctx_count - 1)]
    base, scale, slots, weight_late, q_near = call(
        inside_kernel,
        (
            shape((length, heads * dh), f32),
            shape((length, LANES), f32),
            shape((tokens, LANES), jnp.int32),
            shape((heads * dh, width - cuts[1]), bf16),
            shape(q.shape, bf16),
        ),
        q, k, v, decay, ids, weight, *got,
        specs=[HBM] * 6 + [VMEM] * len(got),
        scratch=[
            pltpu.VMEM((length, heads * dh), f32),
            pltpu.VMEM((length, LANES), f32),
            part, part, small, pltpu.VMEM(ids.shape, jnp.int32), dma((6,)),
        ],
        moved=weight.size * 2,
    )
    order = [sum(((i >> b) & 1) << (exp_bits - 1 - b) for b in range(exp_bits)) for i in range(exp_count)]
    sections = lax.axis_size("section")
    top = exp_count // 2

    def relay(block):
        return lax.ppermute(block, "section", [(i, (i + 1) % sections) for i in range(sections)])

    all_tokens, experts = exp_count * tokens, per_owner * exp_count
    mixed, groups = None, []
    for start, stop in zip(cuts, cuts[1:]):
        first = mixed is None
        size = stop - start
        extra = LANES if first else 0
        halves = (shape((length // 2, size), bf16), shape((length // 2, size + extra), bf16))
        cost = 2 * length * heads * dh * size
        if first:
            mixed, keep, send = call(
                functools.partial(mix_kernel, heads, order, stop),
                (shape((length, heads * dh), bf16), *halves),
                q_near, base, scale, *latest, weight_early, slots,
                scratch=[part],
                flops=cost,
            )
        else:
            keep, send = call(functools.partial(project_kernel, 0, size), halves, mixed, weight_late, flops=cost)
        for bit in range(exp_bits - 2):
            rest = keep.shape[0] // 2
            send, keep = call(
                functools.partial(halve_kernel, bit, tokens, first),
                (shape((rest, size + extra), bf16), shape((rest, size), f32)),
                keep, send, swap(send, "exp", 1 << bit),
            )
        own = call(
            functools.partial(carry_kernel, exp_bits - 2, start, first),
            shape((2 * tokens, size + extra), bf16),
            keep, send, swap(send, "exp", top // 2), residual[0],
        )
        whole = shape((2 * tokens, size), bf16)
        if first:
            other = swap(own, "exp", top)
            facts = call(
                functools.partial(facts_kernel, exp_count, experts, tokens),
                (shape((all_tokens, 2 * per_owner * CAP), bf16), shape((all_tokens, LANES), jnp.int32)),
                own, other,
            )
            block = relay(call(combine_kernel, whole, own, other))
        else:
            own = relay(own)
            other, *facts = lax.optimization_barrier((swap(own, "exp", top), *facts))
            block = call(combine_kernel, whole, own, other)
        groups.append([block])
        for index in range(1, top):
            groups[-1].append(swap(groups[-1][index & (index - 1)], "exp", index & -index))
    rows_shape = (per_owner, exp_count, CAP, width)
    count = 2 * sum(len(pieces(0, part_groups[0].shape[1])) for part_groups in groups)
    late_tokens = all_tokens - 2 * tokens
    held = (2, per_owner, CAP, width)
    rows, *near = call(
        functools.partial(near_kernel, PARTS, top),
        (
            shape(rows_shape, bf16),
            shape((experts, LANES), f32),
            shape((late_tokens, LANES), f32),
            shape((late_tokens, experts), f32),
        ),
        *[part_groups[0] for part_groups in groups],
        *[part_groups[i] for i in range(1, top) for part_groups in groups[:-1]],
        *facts, norm_gain, router_t,
        out_specs=(HBM, VMEM, VMEM, VMEM),
        scratch=[pltpu.VMEM(held, bf16), dma((count,))],
    )
    rows, gates = call(
        functools.partial(far_kernel, PARTS, top),
        (shape(rows_shape, bf16), shape(rows_shape[:-1], bf16)),
        *[part_groups[i] for i in range(1, top) for part_groups in groups],
        *facts, norm_gain, router_t, *near, rows,
        specs=[VMEM] * (PARTS * (top - 1) + 7) + [HBM],
        out_specs=(HBM, HBM),
        scratch=[
            pltpu.VMEM((top - 1, *held), bf16),
            pltpu.VMEM(rows_shape[:-1], bf16),
            dma((top - 1, count)),
            dma,
        ],
        aliases={PARTS * (top - 1) + 7: 0},
    )
    return rows[None, None], gates[None, None]


def solution(mesh):
    placed = (
        P("section", "ctx", "exp"),
        P("section", "ctx", "exp"),
        P("section", "ctx", "exp"),
        P("section", "exp", "ctx"),
        P("section", "exp", None),
        P("section", ("ctx", "exp"), None),
        P("section", None),
        P("section", None, None),
        P("section", ("ctx", "exp"), None),
    )
    return jax.shard_map(
        on_device,
        mesh=mesh,
        in_specs=placed,
        out_specs=(
            P("section", "ctx", "exp", None, None, None),
            P("section", "ctx", "exp", None, None),
        ),
        check_vma=False,
    )
```

```python
import functools

import jax
import jax.numpy as jnp
from jax import lax
from jax.experimental import pallas as pl
from jax.experimental.pallas import tpu as pltpu
from jax.sharding import PartitionSpec as P

CAP = 4
EPSILON = 1e-05
LANES = 128
ROWS = 16
MIB = 1 << 20
PARTS = 2

VMEM = pl.BlockSpec(memory_space=pltpu.VMEM)
HBM = pl.BlockSpec(memory_space=pltpu.HBM)
bf16 = jnp.bfloat16
f32 = jnp.float32


def iota(shape, dim):
    return lax.broadcasted_iota(jnp.int32, shape, dim)


def mm(a, b, dims):
    return lax.dot_general(a, b, (dims, ((), ())), preferred_element_type=f32)


NN = ((1,), (0,))
NT = ((1,), (1,))
TN = ((0,), (0,))


def to_column(row):
    n = row.shape[1]
    square = jnp.broadcast_to(row, (n, n))
    return jnp.sum(jnp.where(iota((n, n), 0) == iota((n, n), 1), square, jnp.zeros_like(square)), axis=1, keepdims=True)


def cumulative(row):
    n = row.shape[1]
    at, of = iota((n, n), 0), iota((n, n), 1)
    column = -jnp.sum(jnp.where(of <= at, jnp.broadcast_to(row, (n, n)), 0.0), axis=1, keepdims=True)
    along = jnp.sum(jnp.where(at == of, jnp.broadcast_to(column, (n, n)), 0.0), axis=0, keepdims=True)
    return column, along


def pad_rows(heads):
    return -(-3 * heads // ROWS) * ROWS


def log_rows(values):
    heads, shape = len(values), (pad_rows(len(values)), values[0].shape[1])
    row, out = iota(shape, 0), jnp.zeros(shape, f32)
    for h, value in enumerate(values):
        for part in range(3):
            piece = value.astype(bf16).astype(f32)
            out = jnp.where(row == part * heads + h, piece, out)
            value = value - piece
    return out.astype(bf16)


def get_log(block, heads, h):
    return block[h : h + 1] + block[heads + h : heads + h + 1] + block[2 * heads + h : 2 * heads + h + 1]


def fetch(sources, places, sems):
    copies = [pltpu.make_async_copy(s, p, sems.at[i]) for i, (s, p) in enumerate(zip(sources, places, strict=True))]
    for copy in copies:
        copy.start()
    return copies


def state_kernel(k_hbm, v_hbm, decay_hbm, msg_ref, k_ref, v_ref, decay_ref, sems):
    copies = fetch((decay_hbm, k_hbm, v_hbm), (decay_ref, k_ref, v_ref), sems)
    heads = decay_ref.shape[0]
    dh = k_ref.shape[1] // heads
    base = heads * dh
    copies[0].wait()
    tails, lasts = [], []
    for h in range(heads):
        column, along = cumulative(decay_ref[h : h + 1, :])
        last = along[:, -1:]
        tails.append(jnp.exp(last - column))
        lasts.append(jnp.broadcast_to(last, (1, dh)))
    msg_ref[base:, :] = log_rows(lasts)
    copies[1].wait()
    copies[2].wait()
    for h in range(heads):
        keyed = (k_ref[:, h * dh : (h + 1) * dh].astype(f32) * tails[h]).astype(bf16)
        msg_ref[h * dh : (h + 1) * dh, :] = mm(keyed, v_ref[:, h * dh : (h + 1) * dh], TN).astype(bf16)


def joined(heads, bit, own_ref, got_ref):
    dh = own_ref.shape[1]
    base = heads * dh
    upper = (lax.axis_index("ctx") >> bit) & 1
    is_upper = jnp.full((1, dh), upper, jnp.int32) == 1
    own_block = own_ref[base:, :].astype(f32)
    got_block = got_ref[base:, :].astype(f32)
    for h in range(heads):
        own_log, got_log = get_log(own_block, heads, h), get_log(got_block, heads, h)
        own = own_ref[h * dh : (h + 1) * dh, :].astype(f32)
        got = got_ref[h * dh : (h + 1) * dh, :].astype(f32)
        scale_own = jnp.where(is_upper, 1.0, jnp.exp(got_log))
        scale_got = jnp.where(is_upper, jnp.exp(own_log), 1.0)
        yield scale_own * own + scale_got * got, own_log + got_log


def join_kernel(heads, bit, own_ref, got_ref, msg_ref):
    dh = own_ref.shape[1]
    logs = []
    for h, (state, log) in enumerate(joined(heads, bit, own_ref, got_ref)):
        msg_ref[h * dh : (h + 1) * dh, :] = state.astype(bf16)
        logs.append(log)
    if msg_ref.shape[0] > heads * dh:
        msg_ref[heads * dh :, :] = log_rows(logs)


def split_mm(a, state):
    high = state.astype(bf16)
    low = (state - high.astype(f32)).astype(bf16)
    return mm(a, high, NN) + mm(a, low, NN)


def inside_kernel(q_hbm, k_hbm, v_hbm, decay_hbm, ids_hbm, weight_hbm, *refs):
    inside_ref, growth_ref, slots_ref, weight_ref, q_ref, k_ref, v_ref, decay_ref, ids_ref, sems = refs
    copies = fetch(
        (decay_hbm, ids_hbm, q_hbm, k_hbm, v_hbm, weight_hbm.at[:, : weight_ref.shape[1]]),
        (decay_ref, ids_ref, q_ref, k_ref, v_ref, weight_ref),
        sems,
    )
    for copy in copies[:-1]:
        copy.wait()
    heads = decay_ref.shape[0]
    length = q_ref.shape[0]
    dh = q_ref.shape[1] // heads
    causal = iota((length, length), 0) >= iota((length, length), 1)
    lane = iota((length, LANES), 1)
    growth = jnp.zeros((length, LANES), f32)
    for h in range(heads):
        cols = slice(h * dh, (h + 1) * dh)
        column, along = cumulative(decay_ref[h : h + 1, :])
        scores = mm(q_ref[:, cols], k_ref[:, cols], NT)
        weights = jnp.where(causal, scores * jnp.exp(jnp.minimum(column - along, 0.0)), 0.0).astype(bf16)
        inside_ref[:, cols] = mm(weights, v_ref[:, cols], NN)
        growth = jnp.where(lane == h, jnp.exp(column), growth)
    growth_ref[...] = growth
    n = ids_ref.shape[1]
    earlier = iota((n, n), 1) < iota((n, n), 0)
    rows = [ids_ref[c : c + 1, :] for c in range(2)]
    places = []
    for c in range(2):
        mine = to_column(rows[c])
        rank = jnp.zeros((n, 1), jnp.int32)
        for other in range(2):
            rank += jnp.sum(jnp.where(earlier & (mine == rows[other]), 1, 0), axis=1, keepdims=True)
        places.append(mine * CAP + rank)
    lane = iota((n, LANES), 1)
    slots_ref[...] = jnp.where(lane == 0, places[0], jnp.where(lane == 1, places[1], 0))
    copies[-1].wait()


def late_kernel(heads, weight_hbm, *refs):
    *refs, weight_ref, sem = refs
    copy = pltpu.make_async_copy(weight_hbm.at[:, -weight_ref.shape[1] :], weight_ref, sem)
    copy.start()
    base_kernel(heads, *refs)
    copy.wait()


def base_kernel(heads, q_ref, inside_ref, growth_ref, *rest):
    got_refs, (base_ref, scale_ref) = rest[:-2], rest[-2:]
    bits = len(got_refs)
    dh = q_ref.shape[1] // heads
    base = heads * dh
    place = lax.axis_index("ctx")
    blocks = [ref[base:, :].astype(f32) for ref in got_refs]
    uppers = [jnp.full((1, dh), (place >> bit) & 1, jnp.int32) == 1 for bit in range(bits + 1)]
    lane = iota(scale_ref.shape, 1)
    scale = jnp.zeros(scale_ref.shape, f32)
    for h in range(heads):
        cols = slice(h * dh, (h + 1) * dh)
        incoming = jnp.zeros((dh, dh), f32)
        before = jnp.zeros((1, dh), f32)
        for bit in range(bits):
            got = got_refs[bit][h * dh : (h + 1) * dh, :].astype(f32)
            incoming += jnp.where(uppers[bit], jnp.exp(before), 0.0) * got
            before += jnp.where(uppers[bit], get_log(blocks[bit], heads, h), 0.0)
        growth = growth_ref[:, h : h + 1]
        base_ref[:, cols] = inside_ref[:, cols] + growth * split_mm(q_ref[:, cols], incoming)
        factor = jnp.where(uppers[bits], jnp.exp(before), 0.0)
        scale = jnp.where(lane == h, growth * factor[:, :1], scale)
    scale_ref[...] = scale


def answer_kernel(heads, asked_ref, state_ref, out_ref):
    dh = state_ref.shape[1]
    for h in range(heads):
        cols = slice(h * dh, (h + 1) * dh)
        out_ref[:, cols] = mm(asked_ref[:, cols], state_ref[h * dh : (h + 1) * dh, :], NN).astype(bf16)


def mix_kernel(heads, order, stop, q_ref, base_ref, scale_ref, state_ref, *rest):
    *answers, weight_ref, slots_ref, mixed_ref, keep_ref, send_ref, attended = rest
    dh = base_ref.shape[1] // heads
    me = lax.axis_index("exp")
    last = jnp.full((base_ref.shape[0], dh), lax.axis_index("ctx"), jnp.int32) == 3
    for h in range(heads):
        cols = slice(h * dh, (h + 1) * dh)
        outside = mm(q_ref[:, cols], state_ref[h * dh : (h + 1) * dh, :], NN)
        for answer_ref in answers:
            outside = jnp.where(last, answer_ref[:, cols].astype(f32), outside)
        attended[:, cols] = (base_ref[:, cols] + scale_ref[:, h : h + 1] * outside).astype(bf16)
    share = base_ref.shape[0] // len(order)
    for i, k in enumerate(order):
        mixed_ref[i * share : (i + 1) * share, :] = attended[pl.ds(pl.multiple_of((me ^ k) * share, share), share), :]
    project_kernel(0, stop, mixed_ref, weight_ref, keep_ref, send_ref)
    put_lanes(send_ref, slots_ref[...].astype(f32))


def project_kernel(start, stop, mixed_ref, weight_ref, keep_ref, send_ref):
    half = mixed_ref.shape[0] // 2
    mixed = mixed_ref[...]
    for at, to in pieces(start, stop):
        part = mm(mixed, weight_ref[:, at:to], NN).astype(bf16)
        keep_ref[:, at - start : to - start] = part[:half]
        send_ref[:, at - start : to - start] = part[half:]


def pieces(start, stop, step=3072):
    return [(at, min(at + step, stop)) for at in range(start, stop, step)]


def put_lanes(ref, lanes):
    tokens = lanes.shape[0]
    ref[:tokens, -LANES:] = lanes.astype(bf16)
    if ref.shape[0] > tokens:
        ref[tokens:, -LANES:] = jnp.zeros((ref.shape[0] - tokens, LANES), bf16)


def widen_lanes(bit, tokens, sent_ref, got_ref):
    own, got = sent_ref[:tokens, -LANES:].astype(f32), got_ref[:tokens, -LANES:].astype(f32)
    filled = 2 << bit
    return jnp.where(iota(own.shape, 1) < filled, own, jnp.roll(got, filled, axis=1))


def halve_kernel(bit, tokens, tagged, keep_ref, sent_ref, got_ref, send_ref, own_ref):
    half, width = own_ref.shape
    own_ref[...] = keep_ref[:half, :].astype(f32) + got_ref[:half, :width].astype(f32)
    send_ref[:, :width] = (keep_ref[half:, :].astype(f32) + got_ref[half:, :width].astype(f32)).astype(bf16)
    if tagged:
        put_lanes(send_ref, widen_lanes(bit, tokens, sent_ref, got_ref))


def carry_kernel(bit, start, tagged, keep_ref, sent_ref, got_ref, residual_ref, out_ref):
    tokens = residual_ref.shape[0]
    width = keep_ref.shape[1]
    total = keep_ref[...].astype(f32) + got_ref[:, :width].astype(f32)
    own = total[:tokens] + residual_ref[:, start : start + width].astype(f32)
    out_ref[:tokens, :width] = own.astype(bf16)
    out_ref[tokens:, :width] = total[tokens:].astype(bf16)
    if tagged:
        put_lanes(out_ref, widen_lanes(bit, tokens, sent_ref, got_ref))


def combine_kernel(own_ref, got_ref, out_ref):
    rows, width = out_ref.shape
    half = rows // 2
    out_ref[:half, :] = (own_ref[:half, :width].astype(f32) + got_ref[half:, :width].astype(f32)).astype(bf16)
    out_ref[half:, :] = (own_ref[half:, :width].astype(f32) + got_ref[:half, :width].astype(f32)).astype(bf16)


def sums(refs, gain, router):
    square, logits, start = 0.0, 0.0, 0
    for ref in refs:
        for at, to in pieces(0, ref.shape[1]):
            wide = ref[:, at:to].astype(f32)
            square += jnp.sum(wide * wide, axis=1, keepdims=True)
            cols = slice(start + at, start + to)
            logits += mm((wide * gain[:, cols]).astype(bf16), router[:, cols], NT)
        start += ref.shape[1]
    return square, logits


def facts_kernel(exp_count, experts, tokens, own_ref, got_ref, chosen_ref, target_ref):
    per_owner = experts // exp_count
    top = exp_count // 2
    me = lax.axis_index("exp")
    lanes = [ref[:tokens, -LANES:].astype(f32).astype(jnp.int32) for ref in (own_ref, got_ref)]
    places, wheres, named = [[], []], [[], []], [[], []]
    for j in range(top):
        for side in range(2):
            sender = me ^ (j + side * top)
            for c in range(2):
                slot = lanes[side][:, 2 * j + c : 2 * j + c + 1]
                place = slot - me * (per_owner * CAP)
                mine = (place >= 0) & (place < per_owner * CAP)
                places[c].append(jnp.where(mine, side * (per_owner * CAP) + place, -1))
                wheres[c].append(jnp.where(mine, (place // CAP * exp_count + sender) * CAP + place % CAP, -1))
                named[c].append(slot // CAP)
    places, wheres, named = [[jnp.concatenate(column, axis=0) for column in pair] for pair in (places, wheres, named)]
    slot = iota(chosen_ref.shape, 1)
    chosen_ref[...] = ((places[0] == slot) | (places[1] == slot)).astype(f32).astype(bf16)
    lane = iota(target_ref.shape, 1)
    target = jnp.zeros(target_ref.shape, jnp.int32)
    for i, column in enumerate(wheres + named):
        target = jnp.where(lane == i, column, target)
    target_ref[...] = target


def place_rows(block, parts, factor, chosen, gain, top, held, rows_hbm, sems):
    me = lax.axis_index("exp")
    _, per_owner, cap, _ = held.shape
    copies, start = [], 0
    for ref in parts:
        for at, to in pieces(0, ref.shape[1]):
            cols = slice(start + at, start + to)
            normed = (ref[:, at:to].astype(f32) * factor * gain[:, cols]).astype(bf16)
            held[:, :, :, cols] = mm(chosen, normed, TN).astype(bf16).reshape(2, per_owner, cap, to - at)
            for side in range(2):
                place = rows_hbm.at[:, me ^ (block + side * top), :, cols]
                copies.append(pltpu.make_async_copy(held.at[side, :, :, cols], place, sems.at[len(copies)]))
                copies[-1].start()
        start += ref.shape[1]
    return copies


def gates_of(logits, target, rows, cap):
    wheres, named = [target[:, c : c + 1] for c in range(2)], [target[:, 2 + c : 3 + c] for c in range(2)]
    expert = iota(logits.shape, 1)
    toward = jnp.where(named[1] == expert, 1.0, 0.0) - jnp.where(named[0] == expert, 1.0, 0.0)
    first = 1.0 / (1.0 + jnp.exp(jnp.sum(toward * logits, axis=1, keepdims=True)))
    gates = [first, 1.0 - first]
    total = logits.shape[0]
    hit_row, hit_rank = iota((total, rows), 1), iota((total, LANES), 1)
    out = jnp.zeros((rows, LANES), f32)
    for c in range(2):
        left = jnp.where((wheres[c] >= 0) & (wheres[c] // cap == hit_row), gates[c], 0.0).astype(bf16)
        right = jnp.where(wheres[c] % cap == hit_rank, 1.0, 0.0).astype(bf16)
        out += mm(left, right, TN)
    return out


def near_kernel(parts, top, *refs):
    own, refs = refs[:parts], refs[parts:]
    early, refs = refs[: -10], refs[-10:]
    chosen_ref, target_ref, gain_ref, router_ref, rows_hbm, gates_ref, square_ref, logits_ref, held, sems = refs
    width = gain_ref.shape[1]
    tokens = own[0].shape[0]
    square, logits = sums(own, gain_ref, router_ref)
    factor = lax.rsqrt(square * (1.0 / width) + EPSILON)
    copies = place_rows(0, own, factor, chosen_ref[:tokens, :], gain_ref, top, held, rows_hbm, sems)
    gates_ref[...] = gates_of(logits * factor, target_ref[:tokens, :], gates_ref.shape[0], held.shape[2])
    for i in range(top - 1):
        square, logits = sums(early[i * (parts - 1) : (i + 1) * (parts - 1)], gain_ref, router_ref)
        square_ref[i * tokens : (i + 1) * tokens, :] = jnp.broadcast_to(square, (tokens, square_ref.shape[1]))
        logits_ref[i * tokens : (i + 1) * tokens, :] = logits
    for copy in copies:
        copy.wait()


def far_kernel(parts, top, *refs):
    late, refs = refs[: parts * (top - 1)], refs[parts * (top - 1) :]
    chosen_ref, target_ref, gain_ref, router_ref, near_gates, square_ref, logits_ref, _, rows_hbm, gates_hbm, held, gates_ref, sems, last = refs
    width = gain_ref.shape[1]
    tokens = late[0].shape[0]
    before = width - late[parts - 1].shape[1]
    gates = near_gates[...]
    copies = []
    for i in range(top - 1):
        block = late[i * parts : (i + 1) * parts]
        rows = slice(i * tokens, (i + 1) * tokens)
        token_rows = slice((i + 1) * tokens, (i + 2) * tokens)
        square, logits = sums(block[-1:], gain_ref.at[:, before:], router_ref.at[:, before:])
        factor = lax.rsqrt((square_ref[rows, :1] + square) * (1.0 / width) + EPSILON)
        copies += place_rows(
            i + 1, block, factor, chosen_ref[token_rows, :], gain_ref, top, held.at[i], rows_hbm, sems.at[i]
        )
        logits = (logits_ref[rows, :] + logits) * factor
        gates += gates_of(logits, target_ref[token_rows, :], gates.shape[0], held.shape[3])
    per_owner, exp_count, cap = gates_ref.shape
    for e in range(per_owner):
        gates_ref[e] = gates[e * exp_count : (e + 1) * exp_count, :cap].astype(bf16)
    copies.append(pltpu.make_async_copy(gates_ref, gates_hbm, last))
    copies[-1].start()
    for copy in copies:
        copy.wait()


def swap(block, axis, mask):
    return lax.ppermute(block, axis, [(i, i ^ mask) for i in range(lax.axis_size(axis))])


def hop(block, axis, route):
    places, exps = lax.axis_size(axis), lax.axis_size("exp")
    pairs = [(c * exps + e, to * exps + to_e) for c in range(places) for e in range(exps) for to, to_e in [route(c, e)]]
    return lax.ppermute(block, (axis, "exp"), pairs)


def around(ring, place, index):
    return (ring[(ring.index(place) + 1) % len(ring)], index) if place in ring else (place, index ^ 1)


def between(pair, place, index):
    return (sum(pair) - place, index) if place in pair else (place, index ^ 1)


def call(kernel, out, *args, specs=None, out_specs=None, scratch=(), flops=0, moved=0, limit=16 * MIB, aliases=None):
    single = not isinstance(out, (tuple, list))
    specs = specs or [VMEM] * len(args)
    args = [pltpu.with_memory_space_constraint(a, pltpu.HBM) if s is HBM else a for a, s in zip(args, specs, strict=True)]
    return pl.pallas_call(
        kernel,
        out_shape=out,
        in_specs=specs,
        out_specs=out_specs or (VMEM if single else (VMEM,) * len(out)),
        scratch_shapes=scratch,
        input_output_aliases=aliases or {},
        compiler_params=pltpu.CompilerParams(vmem_limit_bytes=limit),
        cost_estimate=pl.CostEstimate(flops=flops, bytes_accessed=moved, transcendentals=0),
    )(*args)


def on_device(queries, keys_in, values, decay_rate, out_weight, residual, norm_gain, router, expert_ids):
    q, k, v, decay, weight = queries[0], keys_in[0], values[0], decay_rate[0], out_weight[0]
    ids = jnp.swapaxes(expert_ids[0], 0, 1)
    router_t = jnp.swapaxes(router[0], 0, 1)
    length, heads = q.shape[0], decay.shape[0]
    dh = q.shape[1] // heads
    width = weight.shape[1]
    tokens = residual.shape[1]
    exp_count, ctx_count = lax.axis_size("exp"), lax.axis_size("ctx")
    exp_bits, ctx_bits = exp_count.bit_length() - 1, ctx_count.bit_length() - 1
    per_owner = router.shape[2] // exp_count
    shape = jax.ShapeDtypeStruct

    msg_shape = shape((heads * dh + pad_rows(heads), dh), bf16)
    part = pltpu.VMEM((length, heads * dh), bf16)
    small = pltpu.VMEM(decay.shape, f32)
    dma = pltpu.SemaphoreType.DMA
    msg = call(state_kernel, msg_shape, k, v, decay, specs=[HBM] * 3, scratch=[part, part, small, dma((3,))])
    cuts = [width * i // PARTS // LANES * LANES for i in range(PARTS + 1)]
    decay_after, msg = lax.optimization_barrier((decay, msg))
    inside, growth, slots, weight_early, q_near = call(
        inside_kernel,
        (
            shape((length, heads * dh), f32),
            shape((length, LANES), f32),
            shape((tokens, LANES), jnp.int32),
            shape((heads * dh, cuts[1]), bf16),
            shape(q.shape, bf16),
        ),
        q, k, v, decay_after, ids, weight,
        specs=[HBM] * 6,
        scratch=[part, part, small, pltpu.VMEM(ids.shape, jnp.int32), dma((6,))],
        moved=weight.size,
    )
    got = []
    for bit in range(ctx_bits - 1):
        if ctx_bits == 2:
            got.append(lax.ppermute(msg, "ctx", [(c, (c + 1) % ctx_count) for c in range(ctx_count)]))
        else:
            got.append(swap(msg, "ctx", (2 << bit) - 1))
        if bit == 0:
            msg, weight_early = lax.optimization_barrier((msg, weight_early))
        outs = msg_shape if bit < ctx_bits - 2 else shape((heads * dh, dh), bf16)
        msg = call(functools.partial(join_kernel, heads, bit), outs, msg, got[-1])
    if ctx_bits == 2:
        asked = hop(q, "ctx", functools.partial(around, (3, 1, 2)))
        near = hop(msg, "ctx", functools.partial(between, (1, 2)))
        answer = call(functools.partial(answer_kernel, heads), shape(q.shape, bf16), asked, msg)
        latest = [near, hop(answer, "ctx", functools.partial(around, (1, 3, 2)))]
    else:
        latest = [swap(msg, "ctx", ctx_count - 1)]
    base, scale, weight_late = call(
        functools.partial(late_kernel, heads),
        (
            shape((length, heads * dh), f32),
            shape((length, LANES), f32),
            shape((heads * dh, width - cuts[1]), bf16),
        ),
        weight, q_near, inside, growth, *got,
        specs=[HBM] + [VMEM] * (3 + len(got)),
        scratch=[dma],
        moved=weight.size,
    )
    order = [sum(((i >> b) & 1) << (exp_bits - 1 - b) for b in range(exp_bits)) for i in range(exp_count)]
    sections = lax.axis_size("section")
    top = exp_count // 2

    def relay(block):
        return lax.ppermute(block, "section", [(i, (i + 1) % sections) for i in range(sections)])

    all_tokens, experts = exp_count * tokens, per_owner * exp_count
    mixed, groups = None, []
    for start, stop in zip(cuts, cuts[1:]):
        first = mixed is None
        size = stop - start
        extra = LANES if first else 0
        halves = (shape((length // 2, size), bf16), shape((length // 2, size + extra), bf16))
        cost = 2 * length * heads * dh * size
        if first:
            mixed, keep, send = call(
                functools.partial(mix_kernel, heads, order, stop),
                (shape((length, heads * dh), bf16), *halves),
                q_near, base, scale, *latest, weight_early, slots,
                scratch=[part],
                flops=cost,
            )
        else:
            keep, send = call(functools.partial(project_kernel, 0, size), halves, mixed, weight_late, flops=cost)
        for bit in range(exp_bits - 2):
            rest = keep.shape[0] // 2
            send, keep = call(
                functools.partial(halve_kernel, bit, tokens, first),
                (shape((rest, size + extra), bf16), shape((rest, size), f32)),
                keep, send, swap(send, "exp", 1 << bit),
            )
        own = call(
            functools.partial(carry_kernel, exp_bits - 2, start, first),
            shape((2 * tokens, size + extra), bf16),
            keep, send, swap(send, "exp", top // 2), residual[0],
        )
        whole = shape((2 * tokens, size), bf16)
        if first:
            other = swap(own, "exp", top)
            facts = call(
                functools.partial(facts_kernel, exp_count, experts, tokens),
                (shape((all_tokens, 2 * per_owner * CAP), bf16), shape((all_tokens, LANES), jnp.int32)),
                own, other,
            )
            block = relay(call(combine_kernel, whole, own, other))
        else:
            own = relay(own)
            other, *facts = lax.optimization_barrier((swap(own, "exp", top), *facts))
            block = call(combine_kernel, whole, own, other)
        groups.append([block])
        for index in range(1, top):
            groups[-1].append(swap(groups[-1][index & (index - 1)], "exp", index & -index))
    rows_shape = (per_owner, exp_count, CAP, width)
    count = 2 * sum(len(pieces(0, part_groups[0].shape[1])) for part_groups in groups)
    late_tokens = all_tokens - 2 * tokens
    held = (2, per_owner, CAP, width)
    rows, *near = call(
        functools.partial(near_kernel, PARTS, top),
        (
            shape(rows_shape, bf16),
            shape((experts, LANES), f32),
            shape((late_tokens, LANES), f32),
            shape((late_tokens, experts), f32),
        ),
        *[part_groups[0] for part_groups in groups],
        *[part_groups[i] for i in range(1, top) for part_groups in groups[:-1]],
        *facts, norm_gain, router_t,
        out_specs=(HBM, VMEM, VMEM, VMEM),
        scratch=[pltpu.VMEM(held, bf16), dma((count,))],
    )
    rows, gates = call(
        functools.partial(far_kernel, PARTS, top),
        (shape(rows_shape, bf16), shape(rows_shape[:-1], bf16)),
        *[part_groups[i] for i in range(1, top) for part_groups in groups],
        *facts, norm_gain, router_t, *near, rows,
        specs=[VMEM] * (PARTS * (top - 1) + 7) + [HBM],
        out_specs=(HBM, HBM),
        scratch=[
            pltpu.VMEM((top - 1, *held), bf16),
            pltpu.VMEM(rows_shape[:-1], bf16),
            dma((top - 1, count)),
            dma,
        ],
        aliases={PARTS * (top - 1) + 7: 0},
    )
    return rows[None, None], gates[None, None]


def solution(mesh):
    placed = (
        P("section", "ctx", "exp"),
        P("section", "ctx", "exp"),
        P("section", "ctx", "exp"),
        P("section", "exp", "ctx"),
        P("section", "exp", None),
        P("section", ("ctx", "exp"), None),
        P("section", None),
        P("section", None, None),
        P("section", ("ctx", "exp"), None),
    )
    return jax.shard_map(
        on_device,
        mesh=mesh,
        in_specs=placed,
        out_specs=(
            P("section", "ctx", "exp", None, None, None),
            P("section", "ctx", "exp", None, None),
        ),
        check_vma=False,
    )
```

```python
import functools

import jax
import jax.numpy as jnp
from jax import lax
from jax.experimental import pallas as pl
from jax.experimental.pallas import tpu as pltpu
from jax.sharding import PartitionSpec as P

CAP = 4
EPSILON = 1e-05
LANES = 128
ROWS = 16
MIB = 1 << 20
PARTS = 2

VMEM = pl.BlockSpec(memory_space=pltpu.VMEM)
HBM = pl.BlockSpec(memory_space=pltpu.HBM)
bf16 = jnp.bfloat16
f32 = jnp.float32


def iota(shape, dim):
    return lax.broadcasted_iota(jnp.int32, shape, dim)


def mm(a, b, dims):
    return lax.dot_general(a, b, (dims, ((), ())), preferred_element_type=f32)


NN = ((1,), (0,))
NT = ((1,), (1,))
TN = ((0,), (0,))


def to_column(row):
    n = row.shape[1]
    square = jnp.broadcast_to(row, (n, n))
    return jnp.sum(jnp.where(iota((n, n), 0) == iota((n, n), 1), square, jnp.zeros_like(square)), axis=1, keepdims=True)


def cumulative(row):
    n = row.shape[1]
    at, of = iota((n, n), 0), iota((n, n), 1)
    column = -jnp.sum(jnp.where(of <= at, jnp.broadcast_to(row, (n, n)), 0.0), axis=1, keepdims=True)
    along = jnp.sum(jnp.where(at == of, jnp.broadcast_to(column, (n, n)), 0.0), axis=0, keepdims=True)
    return column, along


def pad_rows(heads):
    return -(-3 * heads // ROWS) * ROWS


def log_rows(values):
    heads, shape = len(values), (pad_rows(len(values)), values[0].shape[1])
    row, out = iota(shape, 0), jnp.zeros(shape, f32)
    for h, value in enumerate(values):
        for part in range(3):
            piece = value.astype(bf16).astype(f32)
            out = jnp.where(row == part * heads + h, piece, out)
            value = value - piece
    return out.astype(bf16)


def get_log(block, heads, h):
    return block[h : h + 1] + block[heads + h : heads + h + 1] + block[2 * heads + h : 2 * heads + h + 1]


def fetch(sources, places, sems):
    copies = [pltpu.make_async_copy(s, p, sems.at[i]) for i, (s, p) in enumerate(zip(sources, places, strict=True))]
    for copy in copies:
        copy.start()
    return copies


def state_kernel(k_hbm, v_hbm, decay_hbm, msg_ref, k_ref, v_ref, decay_ref, sems):
    copies = fetch((decay_hbm, k_hbm, v_hbm), (decay_ref, k_ref, v_ref), sems)
    heads = decay_ref.shape[0]
    dh = k_ref.shape[1] // heads
    base = heads * dh
    copies[0].wait()
    tails, lasts = [], []
    for h in range(heads):
        column, along = cumulative(decay_ref[h : h + 1, :])
        last = along[:, -1:]
        tails.append(jnp.exp(last - column))
        lasts.append(jnp.broadcast_to(last, (1, dh)))
    msg_ref[base:, :] = log_rows(lasts)
    copies[1].wait()
    keyed = [(k_ref[:, h * dh : (h + 1) * dh].astype(f32) * tails[h]).astype(bf16) for h in range(heads)]
    copies[2].wait()
    for h in range(heads):
        msg_ref[h * dh : (h + 1) * dh, :] = mm(keyed[h], v_ref[:, h * dh : (h + 1) * dh], TN).astype(bf16)


def joined(heads, bit, own_ref, got_ref):
    dh = own_ref.shape[1]
    base = heads * dh
    upper = (lax.axis_index("ctx") >> bit) & 1
    is_upper = jnp.full((1, dh), upper, jnp.int32) == 1
    own_block = own_ref[base:, :].astype(f32)
    got_block = got_ref[base:, :].astype(f32)
    for h in range(heads):
        own_log, got_log = get_log(own_block, heads, h), get_log(got_block, heads, h)
        own = own_ref[h * dh : (h + 1) * dh, :].astype(f32)
        got = got_ref[h * dh : (h + 1) * dh, :].astype(f32)
        scale_own = jnp.where(is_upper, 1.0, jnp.exp(got_log))
        scale_got = jnp.where(is_upper, jnp.exp(own_log), 1.0)
        yield scale_own * own + scale_got * got, own_log + got_log


def join_kernel(heads, bit, own_ref, got_ref, msg_ref):
    dh = own_ref.shape[1]
    logs = []
    for h, (state, log) in enumerate(joined(heads, bit, own_ref, got_ref)):
        msg_ref[h * dh : (h + 1) * dh, :] = state.astype(bf16)
        logs.append(log)
    if msg_ref.shape[0] > heads * dh:
        msg_ref[heads * dh :, :] = log_rows(logs)


def split_mm(a, state):
    high = state.astype(bf16)
    low = (state - high.astype(f32)).astype(bf16)
    return mm(a, high, NN) + mm(a, low, NN)


def weight_kernel(weight_hbm, out_ref, sem):
    copy = pltpu.make_async_copy(weight_hbm.at[:, : out_ref.shape[1]], out_ref, sem)
    copy.start()
    copy.wait()


def inside_kernel(q_hbm, k_hbm, v_hbm, decay_hbm, ids_hbm, weight_hbm, *refs):
    got_refs, refs = refs[:-12], refs[-12:]
    base_ref, scale_ref, slots_ref, weight_ref, q_ref, inside_ref, growth_ref, k_ref, v_ref, decay_ref, ids_ref, sems = refs
    copies = fetch(
        (decay_hbm, ids_hbm, q_hbm, k_hbm, v_hbm, weight_hbm.at[:, -weight_ref.shape[1] :]),
        (decay_ref, ids_ref, q_ref, k_ref, v_ref, weight_ref),
        sems,
    )
    for copy in copies[:-1]:
        copy.wait()
    heads = decay_ref.shape[0]
    length = q_ref.shape[0]
    dh = q_ref.shape[1] // heads
    causal = iota((length, length), 0) >= iota((length, length), 1)
    lane = iota((length, LANES), 1)
    growth = jnp.zeros((length, LANES), f32)
    for h in range(heads):
        cols = slice(h * dh, (h + 1) * dh)
        column, along = cumulative(decay_ref[h : h + 1, :])
        scores = mm(q_ref[:, cols], k_ref[:, cols], NT)
        weights = jnp.where(causal, scores * jnp.exp(jnp.minimum(column - along, 0.0)), 0.0).astype(bf16)
        inside_ref[:, cols] = mm(weights, v_ref[:, cols], NN)
        growth = jnp.where(lane == h, jnp.exp(column), growth)
    growth_ref[...] = growth
    base_kernel(heads, q_ref, inside_ref, growth_ref, *got_refs, base_ref, scale_ref)
    n = ids_ref.shape[1]
    earlier = iota((n, n), 1) < iota((n, n), 0)
    rows = [ids_ref[c : c + 1, :] for c in range(2)]
    places = []
    for c in range(2):
        mine = to_column(rows[c])
        rank = jnp.zeros((n, 1), jnp.int32)
        for other in range(2):
            rank += jnp.sum(jnp.where(earlier & (mine == rows[other]), 1, 0), axis=1, keepdims=True)
        places.append(mine * CAP + rank)
    lane = iota((n, LANES), 1)
    slots_ref[...] = jnp.where(lane == 0, places[0], jnp.where(lane == 1, places[1], 0))
    copies[-1].wait()


def base_kernel(heads, q_ref, inside_ref, growth_ref, *rest):
    got_refs, (base_ref, scale_ref) = rest[:-2], rest[-2:]
    bits = len(got_refs)
    dh = q_ref.shape[1] // heads
    base = heads * dh
    place = lax.axis_index("ctx")
    blocks = [ref[base:, :].astype(f32) for ref in got_refs]
    uppers = [jnp.full((1, dh), (place >> bit) & 1, jnp.int32) == 1 for bit in range(bits + 1)]
    lane = iota(scale_ref.shape, 1)
    scale = jnp.zeros(scale_ref.shape, f32)
    for h in range(heads):
        cols = slice(h * dh, (h + 1) * dh)
        incoming = jnp.zeros((dh, dh), f32)
        before = jnp.zeros((1, dh), f32)
        for bit in range(bits):
            got = got_refs[bit][h * dh : (h + 1) * dh, :].astype(f32)
            incoming += jnp.where(uppers[bit], jnp.exp(before), 0.0) * got
            before += jnp.where(uppers[bit], get_log(blocks[bit], heads, h), 0.0)
        growth = growth_ref[:, h : h + 1]
        base_ref[:, cols] = inside_ref[:, cols] + growth * split_mm(q_ref[:, cols], incoming)
        factor = jnp.where(uppers[bits], jnp.exp(before), 0.0)
        scale = jnp.where(lane == h, growth * factor[:, :1], scale)
    scale_ref[...] = scale


def answer_kernel(heads, asked_ref, state_ref, out_ref):
    dh = state_ref.shape[1]
    for h in range(heads):
        cols = slice(h * dh, (h + 1) * dh)
        out_ref[:, cols] = mm(asked_ref[:, cols], state_ref[h * dh : (h + 1) * dh, :], NN).astype(bf16)


def mix_kernel(heads, order, stop, q_ref, base_ref, scale_ref, state_ref, *rest):
    *answers, weight_ref, slots_ref, mixed_ref, keep_ref, send_ref, attended = rest
    dh = base_ref.shape[1] // heads
    me = lax.axis_index("exp")
    last = jnp.full((base_ref.shape[0], dh), lax.axis_index("ctx"), jnp.int32) == 3
    for h in range(heads):
        cols = slice(h * dh, (h + 1) * dh)
        outside = mm(q_ref[:, cols], state_ref[h * dh : (h + 1) * dh, :], NN)
        for answer_ref in answers:
            outside = jnp.where(last, answer_ref[:, cols].astype(f32), outside)
        attended[:, cols] = (base_ref[:, cols] + scale_ref[:, h : h + 1] * outside).astype(bf16)
    share = base_ref.shape[0] // len(order)
    for i, k in enumerate(order):
        mixed_ref[i * share : (i + 1) * share, :] = attended[pl.ds(pl.multiple_of((me ^ k) * share, share), share), :]
    project_kernel(0, stop, mixed_ref, weight_ref, keep_ref, send_ref)
    put_lanes(send_ref, slots_ref[...].astype(f32))


def project_kernel(start, stop, mixed_ref, weight_ref, keep_ref, send_ref):
    half = mixed_ref.shape[0] // 2
    mixed = mixed_ref[...]
    for at, to in pieces(start, stop):
        part = mm(mixed, weight_ref[:, at:to], NN).astype(bf16)
        keep_ref[:, at - start : to - start] = part[:half]
        send_ref[:, at - start : to - start] = part[half:]


def pieces(start, stop, step=3072):
    return [(at, min(at + step, stop)) for at in range(start, stop, step)]


def put_lanes(ref, lanes):
    tokens = lanes.shape[0]
    ref[:tokens, -LANES:] = lanes.astype(bf16)
    if ref.shape[0] > tokens:
        ref[tokens:, -LANES:] = jnp.zeros((ref.shape[0] - tokens, LANES), bf16)


def widen_lanes(bit, tokens, sent_ref, got_ref):
    own, got = sent_ref[:tokens, -LANES:].astype(f32), got_ref[:tokens, -LANES:].astype(f32)
    filled = 2 << bit
    return jnp.where(iota(own.shape, 1) < filled, own, jnp.roll(got, filled, axis=1))


def halve_kernel(bit, tokens, tagged, keep_ref, sent_ref, got_ref, send_ref, own_ref):
    half, width = own_ref.shape
    own_ref[...] = keep_ref[:half, :].astype(f32) + got_ref[:half, :width].astype(f32)
    send_ref[:, :width] = (keep_ref[half:, :].astype(f32) + got_ref[half:, :width].astype(f32)).astype(bf16)
    if tagged:
        put_lanes(send_ref, widen_lanes(bit, tokens, sent_ref, got_ref))


def carry_kernel(bit, start, tagged, keep_ref, sent_ref, got_ref, residual_ref, out_ref):
    tokens = residual_ref.shape[0]
    width = keep_ref.shape[1]
    total = keep_ref[...].astype(f32) + got_ref[:, :width].astype(f32)
    own = total[:tokens] + residual_ref[:, start : start + width].astype(f32)
    out_ref[:tokens, :width] = own.astype(bf16)
    out_ref[tokens:, :width] = total[tokens:].astype(bf16)
    if tagged:
        put_lanes(out_ref, widen_lanes(bit, tokens, sent_ref, got_ref))


def combine_kernel(own_ref, got_ref, out_ref):
    rows, width = out_ref.shape
    half = rows // 2
    out_ref[:half, :] = (own_ref[:half, :width].astype(f32) + got_ref[half:, :width].astype(f32)).astype(bf16)
    out_ref[half:, :] = (own_ref[half:, :width].astype(f32) + got_ref[:half, :width].astype(f32)).astype(bf16)


def sums(refs, gain, router):
    square, logits, start = 0.0, 0.0, 0
    for ref in refs:
        for at, to in pieces(0, ref.shape[1]):
            wide = ref[:, at:to].astype(f32)
            square += jnp.sum(wide * wide, axis=1, keepdims=True)
            cols = slice(start + at, start + to)
            logits += mm((wide * gain[:, cols]).astype(bf16), router[:, cols], NT)
        start += ref.shape[1]
    return square, logits


def facts_kernel(exp_count, experts, tokens, own_ref, got_ref, chosen_ref, target_ref):
    per_owner = experts // exp_count
    top = exp_count // 2
    me = lax.axis_index("exp")
    lanes = [ref[:tokens, -LANES:].astype(f32).astype(jnp.int32) for ref in (own_ref, got_ref)]
    places, wheres, named = [[], []], [[], []], [[], []]
    for j in range(top):
        for side in range(2):
            sender = me ^ (j + side * top)
            for c in range(2):
                slot = lanes[side][:, 2 * j + c : 2 * j + c + 1]
                place = slot - me * (per_owner * CAP)
                mine = (place >= 0) & (place < per_owner * CAP)
                places[c].append(jnp.where(mine, side * (per_owner * CAP) + place, -1))
                wheres[c].append(jnp.where(mine, (place // CAP * exp_count + sender) * CAP + place % CAP, -1))
                named[c].append(slot // CAP)
    places, wheres, named = [[jnp.concatenate(column, axis=0) for column in pair] for pair in (places, wheres, named)]
    slot = iota(chosen_ref.shape, 1)
    chosen_ref[...] = ((places[0] == slot) | (places[1] == slot)).astype(f32).astype(bf16)
    lane = iota(target_ref.shape, 1)
    target = jnp.zeros(target_ref.shape, jnp.int32)
    for i, column in enumerate(wheres + named):
        target = jnp.where(lane == i, column, target)
    target_ref[...] = target


def place_rows(block, parts, factor, chosen, gain, top, held, rows_hbm, sems):
    me = lax.axis_index("exp")
    _, per_owner, cap, _ = held.shape
    copies, start = [], 0
    for ref in parts:
        for at, to in pieces(0, ref.shape[1]):
            cols = slice(start + at, start + to)
            normed = (ref[:, at:to].astype(f32) * factor * gain[:, cols]).astype(bf16)
            held[:, :, :, cols] = mm(chosen, normed, TN).astype(bf16).reshape(2, per_owner, cap, to - at)
            for side in range(2):
                place = rows_hbm.at[:, me ^ (block + side * top), :, cols]
                copies.append(pltpu.make_async_copy(held.at[side, :, :, cols], place, sems.at[len(copies)]))
                copies[-1].start()
        start += ref.shape[1]
    return copies


def gates_of(logits, target, rows, cap):
    wheres, named = [target[:, c : c + 1] for c in range(2)], [target[:, 2 + c : 3 + c] for c in range(2)]
    expert = iota(logits.shape, 1)
    toward = jnp.where(named[1] == expert, 1.0, 0.0) - jnp.where(named[0] == expert, 1.0, 0.0)
    first = 1.0 / (1.0 + jnp.exp(jnp.sum(toward * logits, axis=1, keepdims=True)))
    gates = [first, 1.0 - first]
    total = logits.shape[0]
    hit_row, hit_rank = iota((total, rows), 1), iota((total, LANES), 1)
    out = jnp.zeros((rows, LANES), f32)
    for c in range(2):
        left = jnp.where((wheres[c] >= 0) & (wheres[c] // cap == hit_row), gates[c], 0.0).astype(bf16)
        right = jnp.where(wheres[c] % cap == hit_rank, 1.0, 0.0).astype(bf16)
        out += mm(left, right, TN)
    return out


def near_kernel(parts, top, *refs):
    own, refs = refs[:parts], refs[parts:]
    early, refs = refs[: -10], refs[-10:]
    chosen_ref, target_ref, gain_ref, router_ref, rows_hbm, gates_ref, square_ref, logits_ref, held, sems = refs
    width = gain_ref.shape[1]
    tokens = own[0].shape[0]
    square, logits = sums(own, gain_ref, router_ref)
    factor = lax.rsqrt(square * (1.0 / width) + EPSILON)
    copies = place_rows(0, own, factor, chosen_ref[:tokens, :], gain_ref, top, held, rows_hbm, sems)
    gates_ref[...] = gates_of(logits * factor, target_ref[:tokens, :], gates_ref.shape[0], held.shape[2])
    for i in range(top - 1):
        square, logits = sums(early[i * (parts - 1) : (i + 1) * (parts - 1)], gain_ref, router_ref)
        square_ref[i * tokens : (i + 1) * tokens, :] = jnp.broadcast_to(square, (tokens, square_ref.shape[1]))
        logits_ref[i * tokens : (i + 1) * tokens, :] = logits
    for copy in copies:
        copy.wait()


def far_kernel(parts, top, *refs):
    late, refs = refs[: parts * (top - 1)], refs[parts * (top - 1) :]
    chosen_ref, target_ref, gain_ref, router_ref, near_gates, square_ref, logits_ref, _, rows_hbm, gates_hbm, held, gates_ref, sems, last = refs
    width = gain_ref.shape[1]
    tokens = late[0].shape[0]
    before = width - late[parts - 1].shape[1]
    gates = near_gates[...]
    copies = []
    for i in range(top - 1):
        block = late[i * parts : (i + 1) * parts]
        rows = slice(i * tokens, (i + 1) * tokens)
        token_rows = slice((i + 1) * tokens, (i + 2) * tokens)
        square, logits = sums(block[-1:], gain_ref.at[:, before:], router_ref.at[:, before:])
        factor = lax.rsqrt((square_ref[rows, :1] + square) * (1.0 / width) + EPSILON)
        copies += place_rows(
            i + 1, block, factor, chosen_ref[token_rows, :], gain_ref, top, held.at[i], rows_hbm, sems.at[i]
        )
        logits = (logits_ref[rows, :] + logits) * factor
        gates += gates_of(logits, target_ref[token_rows, :], gates.shape[0], held.shape[3])
    per_owner, exp_count, cap = gates_ref.shape
    for e in range(per_owner):
        gates_ref[e] = gates[e * exp_count : (e + 1) * exp_count, :cap].astype(bf16)
    copies.append(pltpu.make_async_copy(gates_ref, gates_hbm, last))
    copies[-1].start()
    for copy in copies:
        copy.wait()


def swap(block, axis, mask):
    return lax.ppermute(block, axis, [(i, i ^ mask) for i in range(lax.axis_size(axis))])


def hop(block, axis, route):
    places, exps = lax.axis_size(axis), lax.axis_size("exp")
    pairs = [(c * exps + e, to * exps + to_e) for c in range(places) for e in range(exps) for to, to_e in [route(c, e)]]
    return lax.ppermute(block, (axis, "exp"), pairs)


def around(ring, place, index):
    return (ring[(ring.index(place) + 1) % len(ring)], index) if place in ring else (place, index ^ 1)


def between(pair, place, index):
    return (sum(pair) - place, index) if place in pair else (place, index ^ 1)


def call(kernel, out, *args, specs=None, out_specs=None, scratch=(), flops=0, moved=0, limit=16 * MIB, aliases=None):
    single = not isinstance(out, (tuple, list))
    specs = specs or [VMEM] * len(args)
    args = [pltpu.with_memory_space_constraint(a, pltpu.HBM) if s is HBM else a for a, s in zip(args, specs, strict=True)]
    return pl.pallas_call(
        kernel,
        out_shape=out,
        in_specs=specs,
        out_specs=out_specs or (VMEM if single else (VMEM,) * len(out)),
        scratch_shapes=scratch,
        input_output_aliases=aliases or {},
        compiler_params=pltpu.CompilerParams(vmem_limit_bytes=limit),
        cost_estimate=pl.CostEstimate(flops=flops, bytes_accessed=moved, transcendentals=0),
    )(*args)


def on_device(queries, keys_in, values, decay_rate, out_weight, residual, norm_gain, router, expert_ids):
    q, k, v, decay, weight = queries[0], keys_in[0], values[0], decay_rate[0], out_weight[0]
    ids = jnp.swapaxes(expert_ids[0], 0, 1)
    router_t = jnp.swapaxes(router[0], 0, 1)
    length, heads = q.shape[0], decay.shape[0]
    dh = q.shape[1] // heads
    width = weight.shape[1]
    tokens = residual.shape[1]
    exp_count, ctx_count = lax.axis_size("exp"), lax.axis_size("ctx")
    exp_bits, ctx_bits = exp_count.bit_length() - 1, ctx_count.bit_length() - 1
    per_owner = router.shape[2] // exp_count
    shape = jax.ShapeDtypeStruct

    msg_shape = shape((heads * dh + pad_rows(heads), dh), bf16)
    part = pltpu.VMEM((length, heads * dh), bf16)
    small = pltpu.VMEM(decay.shape, f32)
    dma = pltpu.SemaphoreType.DMA
    msg = call(state_kernel, msg_shape, k, v, decay, specs=[HBM] * 3, scratch=[part, part, small, dma((3,))])
    cuts = [width * i // PARTS // LANES * LANES for i in range(PARTS + 1)]
    weight_after, msg = lax.optimization_barrier((weight, msg))
    weight_early = call(
        weight_kernel, shape((heads * dh, cuts[1]), bf16), weight_after, specs=[HBM], scratch=[dma], moved=weight.size
    )
    got = []
    for bit in range(ctx_bits - 1):
        if ctx_bits == 2:
            got.append(lax.ppermute(msg, "ctx", [(c, (c + 1) % ctx_count) for c in range(ctx_count)]))
        else:
            got.append(swap(msg, "ctx", (2 << bit) - 1))
        if bit == 0:
            msg, weight_early = lax.optimization_barrier((msg, weight_early))
        outs = msg_shape if bit < ctx_bits - 2 else shape((heads * dh, dh), bf16)
        msg = call(functools.partial(join_kernel, heads, bit), outs, msg, got[-1])
    if ctx_bits == 2:
        asked = hop(q, "ctx", functools.partial(around, (3, 1, 2)))
        near = hop(msg, "ctx", functools.partial(between, (1, 2)))
        answer = call(functools.partial(answer_kernel, heads), shape(q.shape, bf16), asked, msg)
        latest = [near, hop(answer, "ctx", functools.partial(around, (1, 3, 2)))]
    else:
        latest = [swap(msg, "ctx", ctx_count - 1)]
    base, scale, slots, weight_late, q_near = call(
        inside_kernel,
        (
            shape((length, heads * dh), f32),
            shape((length, LANES), f32),
            shape((tokens, LANES), jnp.int32),
            shape((heads * dh, width - cuts[1]), bf16),
            shape(q.shape, bf16),
        ),
        q, k, v, decay, ids, weight, *got,
        specs=[HBM] * 6 + [VMEM] * len(got),
        scratch=[
            pltpu.VMEM((length, heads * dh), f32),
            pltpu.VMEM((length, LANES), f32),
            part, part, small, pltpu.VMEM(ids.shape, jnp.int32), dma((6,)),
        ],
        moved=weight.size * 2,
    )
    order = [sum(((i >> b) & 1) << (exp_bits - 1 - b) for b in range(exp_bits)) for i in range(exp_count)]
    sections = lax.axis_size("section")
    top = exp_count // 2

    def relay(block):
        return lax.ppermute(block, "section", [(i, (i + 1) % sections) for i in range(sections)])

    all_tokens, experts = exp_count * tokens, per_owner * exp_count
    mixed, groups = None, []
    for start, stop in zip(cuts, cuts[1:]):
        first = mixed is None
        size = stop - start
        extra = LANES if first else 0
        halves = (shape((length // 2, size), bf16), shape((length // 2, size + extra), bf16))
        cost = 2 * length * heads * dh * size
        if first:
            mixed, keep, send = call(
                functools.partial(mix_kernel, heads, order, stop),
                (shape((length, heads * dh), bf16), *halves),
                q_near, base, scale, *latest, weight_early, slots,
                scratch=[part],
                flops=cost,
            )
        else:
            keep, send = call(functools.partial(project_kernel, 0, size), halves, mixed, weight_late, flops=cost)
        for bit in range(exp_bits - 2):
            rest = keep.shape[0] // 2
            send, keep = call(
                functools.partial(halve_kernel, bit, tokens, first),
                (shape((rest, size + extra), bf16), shape((rest, size), f32)),
                keep, send, swap(send, "exp", 1 << bit),
            )
        own = call(
            functools.partial(carry_kernel, exp_bits - 2, start, first),
            shape((2 * tokens, size + extra), bf16),
            keep, send, swap(send, "exp", top // 2), residual[0],
        )
        whole = shape((2 * tokens, size), bf16)
        if first:
            other = swap(own, "exp", top)
            facts = call(
                functools.partial(facts_kernel, exp_count, experts, tokens),
                (shape((all_tokens, 2 * per_owner * CAP), bf16), shape((all_tokens, LANES), jnp.int32)),
                own, other,
            )
            block = relay(call(combine_kernel, whole, own, other))
        else:
            own = relay(own)
            other, *facts = lax.optimization_barrier((swap(own, "exp", top), *facts))
            block = call(combine_kernel, whole, own, other)
        groups.append([block])
        for index in range(1, top):
            groups[-1].append(swap(groups[-1][index & (index - 1)], "exp", index & -index))
    rows_shape = (per_owner, exp_count, CAP, width)
    count = 2 * sum(len(pieces(0, part_groups[0].shape[1])) for part_groups in groups)
    late_tokens = all_tokens - 2 * tokens
    held = (2, per_owner, CAP, width)
    rows, *near = call(
        functools.partial(near_kernel, PARTS, top),
        (
            shape(rows_shape, bf16),
            shape((experts, LANES), f32),
            shape((late_tokens, LANES), f32),
            shape((late_tokens, experts), f32),
        ),
        *[part_groups[0] for part_groups in groups],
        *[part_groups[i] for i in range(1, top) for part_groups in groups[:-1]],
        *facts, norm_gain, router_t,
        out_specs=(HBM, VMEM, VMEM, VMEM),
        scratch=[pltpu.VMEM(held, bf16), dma((count,))],
    )
    rows, gates = call(
        functools.partial(far_kernel, PARTS, top),
        (shape(rows_shape, bf16), shape(rows_shape[:-1], bf16)),
        *[part_groups[i] for i in range(1, top) for part_groups in groups],
        *facts, norm_gain, router_t, *near, rows,
        specs=[VMEM] * (PARTS * (top - 1) + 7) + [HBM],
        out_specs=(HBM, HBM),
        scratch=[
            pltpu.VMEM((top - 1, *held), bf16),
            pltpu.VMEM(rows_shape[:-1], bf16),
            dma((top - 1, count)),
            dma,
        ],
        aliases={PARTS * (top - 1) + 7: 0},
    )
    return rows[None, None], gates[None, None]


def solution(mesh):
    placed = (
        P("section", "ctx", "exp"),
        P("section", "ctx", "exp"),
        P("section", "ctx", "exp"),
        P("section", "exp", "ctx"),
        P("section", "exp", None),
        P("section", ("ctx", "exp"), None),
        P("section", None),
        P("section", None, None),
        P("section", ("ctx", "exp"), None),
    )
    return jax.shard_map(
        on_device,
        mesh=mesh,
        in_specs=placed,
        out_specs=(
            P("section", "ctx", "exp", None, None, None),
            P("section", "ctx", "exp", None, None),
        ),
        check_vma=False,
    )
```
